256 devices in a mesh: row: 32 (over z, x), col: 8 (over y, core).
Axes of the slice: x: 4, y: 4, z: 8, core: 2. Of those that a mesh axis runs over, the one named last changes fastest.
Arguments:
- acts: bfloat16 [4096, 28672], P('col', 'row'), may hold values from -450 to 450
- out_grads: bfloat16 [4096, 8192], P('row', 'col'), may hold values from -150 to 150
- moment: float32 [28672, 8192], P('row', 'col'), may hold values from -6 to 6
- row_state: float32 [28672], P('row'), may hold values from 0.2 to 3
- col_state: float32 [8192], P('col'), may hold values from 0.2 to 3
- row_conf: float32 [28672], P('row'), may hold values from 0.2 to 2
- col_conf: float32 [8192], P('col'), may hold values from 0.2 to 2
Outputs:
- moment_new: float32 [28672, 8192], P('row', 'col')
- update: float32 [28672, 8192], P('row', 'col')
- row_new: float32 [28672], P('row')
- col_new: float32 [8192], P('col')
- row_conf_new: float32 [28672], P('row')
- col_conf_new: float32 [8192], P('col')
The draws below stay inside these ranges and needn't reach their ends.
All inputs are finite; a program needn't handle non-finite values.
Results may differ from the reference program's by a relative error of at most 0.0003.
Values may be sent and summed in bfloat16 or wider, within the bound.
A program may use at most 128 MiB of HBM per device.

```python
import math
import jax
import jax.numpy as jnp
from jax import lax

D = 8192
FF = 28672
STEP = 10
TOKENS = 4096


def column_scales(key, width, ramp_base):
    spread = jnp.exp(jax.random.uniform(key, (width,), jnp.float32, 0.0, math.log(10.0)))
    ramp = ramp_base ** (jnp.arange(width, dtype=jnp.float32) / width)
    return spread * ramp


def draw_acts(key, part):
    key = jax.random.fold_in(key, 11)
    value_key, scale_key = jax.random.split(key, 2)
    values = jnp.clip(jax.random.normal(value_key, (TOKENS, FF), jnp.float32), -5.0, 5.0)
    scales = column_scales(scale_key, FF, 3.0)
    return (values * scales[None, :]).astype(jnp.bfloat16)


def draw_out_grads(key, part):
    key = jax.random.fold_in(key, 23)
    value_key, scale_key = jax.random.split(key, 2)
    values = jnp.clip(jax.random.normal(value_key, (TOKENS, D), jnp.float32), -5.0, 5.0)
    scales = column_scales(scale_key, D, 3.0)
    return (values * scales[None, :]).astype(jnp.bfloat16)


def block_scale(stream_key, shape, cuts, smallest, high):
    loudness = 1.0
    for position, shards_of in cuts:
        steps = jax.random.uniform(jax.random.fold_in(jax.random.fold_in(stream_key, 6), position), (shards_of,), jnp.float32, smallest / len(cuts), high / len(cuts))
        loudness = loudness * jnp.repeat(jnp.exp(steps), shape[position] // shards_of).reshape((-1,) + (1,) * (len(shape) - 1 - position))
    return loudness


def noise(own_key, shape, scale, limit, cuts=(), held_as=jnp.bfloat16):
    values = scale * jax.random.normal(own_key, shape, jnp.float32)
    if cuts:
        values = values * block_scale(own_key, shape, cuts, -0.22, 0.18)
    return jnp.clip(values, -limit, limit).astype(held_as)


def setup_inputs(seed: int = 0) -> dict:
    streams_of = jax.random.split(jax.random.key(seed), 8)
    return {
        "acts": draw_acts(jax.random.fold_in(streams_of[7], 71), 0),
        "out_grads": draw_out_grads(jax.random.fold_in(streams_of[7], 71), 0),
        "moment": noise(streams_of[2], (FF, D), 1.0, 6.0, ((0, 32), (1, 8)), jnp.float32),
        "row_state": jnp.clip(jnp.exp(math.log(3.0) - 2.7080502 * jax.random.uniform(streams_of[3], (FF,), jnp.float32) ** block_scale(streams_of[3], (FF,), ((0, 32),), -0.2, 0.2)), 0.2, 3.0),
        "col_state": jnp.clip(jnp.exp(math.log(3.0) - 2.7080502 * jax.random.uniform(streams_of[4], (D,), jnp.float32) ** block_scale(streams_of[4], (D,), ((0, 8),), -0.2, 0.2)), 0.2, 3.0),
        "row_conf": jnp.clip(jnp.exp(math.log(2.0) - 2.3025851 * jax.random.uniform(streams_of[5], (FF,), jnp.float32) ** block_scale(streams_of[5], (FF,), ((0, 32),), -0.2, 0.2)), 0.2, 2.0),
        "col_conf": jnp.clip(jnp.exp(math.log(2.0) - 2.3025851 * jax.random.uniform(streams_of[6], (D,), jnp.float32) ** block_scale(streams_of[6], (D,), ((0, 8),), -0.2, 0.2)), 0.2, 2.0),
    }


first_decay = 0.9
tiny_moment = 1e-30
tiny_confidence = 1e-16

def reference(acts, out_grads, moment, row_state, col_state, row_conf, col_conf):
    gradient = jnp.dot(acts.T, out_grads, preferred_element_type=jnp.float32)
    squares = gradient * gradient
    overall = jnp.sum(squares)
    scaling = jnp.minimum(1.0, math.sqrt(FF * D) / jnp.sqrt(overall + 1e-06))
    squared = scaling * scaling * squares + tiny_moment
    second_decay = 1.0 - STEP ** (-0.8)
    row_new = second_decay * row_state + (1.0 - second_decay) * lax.optimization_barrier(jnp.mean(squared, axis=1))
    col_new = second_decay * col_state + (1.0 - second_decay) * lax.optimization_barrier(jnp.mean(squared, axis=0))
    factored = row_new[:, None] * col_new[None, :] / jnp.mean(row_new)
    direction = scaling * gradient / jnp.sqrt(factored)
    moment_new = first_decay * moment + (1.0 - first_decay) * direction
    unsteady = (direction - moment_new) ** 2 + tiny_confidence
    row_conf_new = second_decay * row_conf + (1.0 - second_decay) * lax.optimization_barrier(jnp.mean(unsteady, axis=1))
    col_conf_new = second_decay * col_conf + (1.0 - second_decay) * lax.optimization_barrier(jnp.mean(unsteady, axis=0))
    confident = row_conf_new[:, None] * col_conf_new[None, :] / jnp.mean(row_conf_new)
    update = moment_new / jnp.sqrt(confident)
    return (moment_new, update, row_new, col_new, row_conf_new, col_conf_new)
```

```python
import functools

import jax
import jax.numpy as jnp
from jax import lax
from jax.experimental import pallas as pl
from jax.experimental.pallas import tpu as pltpu
from jax.sharding import PartitionSpec as P

MESH = pl.DeviceIdType.MESH
F32 = jnp.float32
STEP = 10
X = 4
LANES = 128

first_decay = 0.9
tiny_moment = 1e-30
tiny_confidence = 1e-16
second_decay = 1.0 - STEP ** (-0.8)


def kernel(R, C, acts, grads, moment, row_state, col_state, row_conf, col_conf,
           moment_out, update_out, row_out, col_out, row_conf_out, col_conf_out,
           A, B, G, M, states, row_part, row_got, col_part, col_got, tot_part, tot_got,
           ring_send, ring_recv, act_send, act_recv, load_sem, store_sem,
           row_send, row_recv, col_send, col_recv, tot_send, tot_recv):
    Z, Y = R // X, C // 2
    row, col = lax.axis_index("row"), lax.axis_index("col")
    div, rem = lax.div, lax.rem
    z, x, y, core = div(row, X), rem(row, X), div(col, 2), rem(col, 2)
    tb, shard = grads.shape[0], acts.shape[0]
    half, chunk, hs = tb // 2, tb // 4, shard // 2
    rows, cols = G.shape
    nr, nc = rows // LANES, cols // LANES
    full_rows, full_cols = rows * R, cols * C
    S = R // 2
    near_step, far_step = 7 * S // 16, 10 * S // 16

    def cycle0(t):
        t = rem(t, R)
        u, v = div(t, X), rem(t, X)
        return u * X + rem(v + 3 * u, X)

    def cycle1(t):
        t = rem(t, R)
        u, v = div(t, X), rem(t, X)
        return rem(3 * u + v, Z) * X + rem(u, X)

    p0 = z * X + rem(x + z, X)
    w = rem(z + (3 * Z - 3) * x, Z)
    p1 = X * (x + X * div(w, X)) + rem(w, X)

    def origin(lane, k):
        cycle, p = ((cycle0, p0), (cycle1, p1))[lane // 2]
        return cycle(p - k + R) if lane % 2 == 0 else cycle(p + k + R)

    def part(first, unit, size):
        return pl.ds(pl.multiple_of(first, unit), size)

    ring_to = [origin(lane, -1) for lane in range(4)]
    up, down = rem(y + 1, Y) * 2 + core, rem(y + Y - 1, Y) * 2 + core
    far, twin = rem(y + 2, Y) * 2 + core, y * 2 + 1 - core

    barrier = pltpu.get_barrier_semaphore()
    for r in ring_to:
        pl.semaphore_signal(barrier, inc=1, device_id=(r, col), device_id_type=MESH)
    for c in (up, down, twin):
        pl.semaphore_signal(barrier, inc=1, device_id=(row, c), device_id_type=MESH)

    loads = [
        pltpu.make_async_copy(grads, B.at[part(row * tb, tb, tb)], load_sem.at[0]),
        pltpu.make_async_copy(acts, A.at[part(col * shard, shard, shard)], load_sem.at[1]),
        pltpu.make_async_copy(moment, M, load_sem.at[2]),
        pltpu.make_async_copy(row_state, states.at[0, pl.ds(0, nr)], load_sem.at[3]),
        pltpu.make_async_copy(col_state, states.at[1, pl.ds(0, nc)], load_sem.at[4]),
        pltpu.make_async_copy(row_conf, states.at[2, pl.ds(0, nr)], load_sem.at[5]),
        pltpu.make_async_copy(col_conf, states.at[3, pl.ds(0, nc)], load_sem.at[6]),
    ]
    states[...] = jnp.zeros_like(states)
    for load in loads:
        load.start()
    pl.semaphore_wait(barrier, 7)

    def ring(lane, s, q, k):
        rows_k = part(origin(lane, k) * tb + (lane // 2) * half + q * chunk, chunk, chunk)
        return pltpu.make_async_remote_copy(
            src_ref=B.at[rows_k], dst_ref=B.at[rows_k],
            send_sem=ring_send.at[lane, 2 * s + q], recv_sem=ring_recv.at[lane, 2 * s + q],
            device_id=(ring_to[lane], col), device_id_type=MESH)

    def ring_first(lane, q):
        first = (lane // 2) * half + q * chunk
        return pltpu.make_async_remote_copy(
            src_ref=grads.at[pl.ds(first, chunk)],
            dst_ref=B.at[part(row * tb + first, chunk, chunk)],
            send_sem=ring_send.at[lane, q], recv_sem=ring_recv.at[lane, q],
            device_id=(ring_to[lane], col), device_id_type=MESH)

    def ring_out(lane, s, q):
        return ring(lane, s, q, s)

    def ring_in(lane, s, q):
        return ring(lane, s, q, s + 1)

    def act(i, owner, first, size, to, src=None):
        there = A.at[part(owner * shard + first, hs, size)]
        return pltpu.make_async_remote_copy(
            src_ref=there if src is None else src, dst_ref=there,
            send_sem=act_send.at[i], recv_sem=act_recv.at[i],
            device_id=(row, to), device_id_type=MESH)

    low, high = acts.at[pl.ds(0, hs)], acts.at[pl.ds(hs, hs)]
    act_out = {
        0: act(0, col, 0, hs, up, low), 3: act(3, col, hs, hs, down, high),
        1: act(1, col, hs, hs, up, high), 4: act(4, col, 0, hs, down, low),
        6: act(6, col, 0, shard, twin, acts),
        2: act(2, down, 0, hs, up), 5: act(5, up, hs, hs, down),
        7: act(7, down, 0, shard, twin), 8: act(8, up, 0, shard, twin),
        9: act(9, far, 0, hs, twin), 10: act(10, far, hs, hs, twin),
    }
    swap = 1 - 2 * core
    act_in = {
        0: act(0, down, 0, hs, up), 1: act(1, down, hs, hs, up), 2: act(2, far, 0, hs, up),
        3: act(3, up, hs, hs, down), 4: act(4, up, 0, hs, down), 5: act(5, far, hs, hs, down),
        6: act(6, twin, 0, shard, twin), 7: act(7, down + swap, 0, shard, twin),
        8: act(8, up + swap, 0, shard, twin), 9: act(9, far + swap, 0, hs, twin),
        10: act(10, far + swap, hs, hs, twin),
    }

    for q in range(2):
        for lane in range(4):
            ring_first(lane, q).start()
    for i in (0, 3, 1, 4, 6):
        act_out[i].start()

    def product(firsts):
        a = jnp.concatenate([A[part(f, half, half), :] for f in firsts], 0)
        b = jnp.concatenate([B[part(f, half, half), :] for f in firsts], 0)
        return lax.dot_general(a, b, (((0,), (0,)), ((), ())), preferred_element_type=F32)

    def hop(s, q):
        for lane in range(4):
            ring_in(lane, s, q).wait_recv()
            ring_out(lane, s + 1, q).start()

    def hops(first, last):
        def both(s, carry):
            hop(s, 0)
            hop(s, 1)
            return carry
        lax.fori_loop(first, last, both, 0)

    def add_units(first, last):
        def add(k, carry):
            G[...] += product([origin(lane, k) * tb + (lane // 2) * half for lane in range(4)])
            return carry
        lax.fori_loop(first, last, add, 0)

    loads[0].wait()
    loads[1].wait()
    G[...] = jnp.zeros_like(G)
    hops(0, near_step)
    for i in (0, 3, 1, 4):
        act_in[i].wait_recv()
    for i in (2, 5, 7, 8):
        act_out[i].start()
    hops(near_step, far_step)
    for i in (2, 5):
        act_in[i].wait_recv()
    for i in (9, 10):
        act_out[i].start()
    hops(far_step, far_step + 1)
    for i in (6, 7, 8, 9, 10):
        act_in[i].wait_recv()

    slots = 2 * (S - 2 - far_step)
    done = 1
    for slot in range(slots):
        s, q = far_step + 1 + slot // 2, slot % 2
        if s < S - 2:
            hop(s, q)
        else:
            for lane in range(4):
                ring_in(lane, s, q).wait_recv()
                if q == lane % 2:
                    ring_out(lane, S - 1, q).start()
        upto = min(1 + (S - 1) * (slot + 1) // slots, s + 1 + q)
        add_units(done, upto)
        done = upto
    add_units(done, S)
    for lane in range(4):
        ring_in(lane, S - 1, lane % 2).wait_recv()
    G[...] += product([row * tb, row * tb + half,
                       cycle0(p0 + S) * tb, cycle1(p1 + S) * tb + half])
    for load in loads[2:]:
        load.wait()

    def exchange(phase, src, got, size, me, along, send_sem, recv_sem):
        def copy(i, slot):
            to = rem(me + i, size)
            return pltpu.make_async_remote_copy(
                src_ref=src, dst_ref=got.at[phase, slot],
                send_sem=send_sem.at[phase, i], recv_sem=recv_sem.at[phase, i],
                device_id=(to, col) if along == "row" else (row, to), device_id_type=MESH)

        def start():
            got[phase, me] = src[...]
            for i in range(1, size):
                copy(i, me).start()

        def result():
            for i in range(1, size):
                copy(i, rem(me + size - i, size)).wait_recv()
            return jnp.sum(got[phase], axis=0)

        def drain():
            for i in range(1, size):
                copy(i, me).wait_send()

        return start, result, drain

    def whole(tile):
        return jnp.sum(tile, axis=(0, 1), keepdims=True)

    def sums(phase, block):
        def rows_of(i, col_sum):
            at = part(i * LANES, LANES, LANES)
            row_sum = jnp.zeros((LANES, LANES), F32)
            col_sums = []
            for j in range(nc):
                square = block(i, at, j)
                row_sum += square
                col_sums.append(jnp.sum(square.reshape(LANES // 8, 8, LANES), axis=0))
            row_part[phase, pl.ds(i, 1), :] = jnp.sum(row_sum.T, axis=0, keepdims=True)
            return col_sum + jnp.concatenate(col_sums, 1)

        col_sum = lax.fori_loop(0, nr, rows_of, jnp.zeros((8, cols), F32))
        col_sum = jnp.sum(col_sum, axis=0, keepdims=True)
        for j in range(nc):
            col_part[phase, j:j + 1, :] = col_sum[:, j * LANES:(j + 1) * LANES]

    def reduced(phase, meanwhile):
        by_col = exchange(phase, col_part.at[phase], col_got, R, row, "row", col_send, col_recv)
        by_row = exchange(phase, row_part.at[phase], row_got, C, col, "col", row_send, row_recv)
        by_col[0]()
        by_row[0]()
        meanwhile()
        col_all = by_col[1]()
        tot_part[phase] = col_all[0:8, :]
        by_tot = exchange(phase, tot_part.at[phase], tot_got, C, col, "col", tot_send, tot_recv)
        by_tot[0]()
        row_all = by_row[1]()
        total = whole(by_tot[1]())

        def drain():
            for one in (by_col, by_row, by_tot):
                one[2]()
        return row_all, col_all, total, drain

    def down_rows(factor_ref, i):
        return jnp.broadcast_to(factor_ref[pl.ds(i, 1), :], (LANES, LANES)).T

    col_part[...] = jnp.zeros_like(col_part)
    row_part[...] = jnp.zeros_like(row_part)
    col_part[0, 8:9, :] = jnp.sum(states[0], axis=0, keepdims=True)
    col_part[0, 9:10, :] = jnp.sum(states[2], axis=0, keepdims=True)

    def squared(i, at, j):
        g = G[at, j * LANES:(j + 1) * LANES]
        return g * g

    def ring_drain():
        def wait(s, carry):
            for q in range(2):
                for lane in range(4):
                    ring_out(lane, s, q).wait_send()
            return carry
        lax.fori_loop(0, S - 1, wait, 0)
        for lane in range(4):
            ring_out(lane, S - 1, lane % 2).wait_send()
        for copy in act_out.values():
            copy.wait_send()

    sums(0, squared)
    row_all, col_all, total, drain0 = reduced(0, ring_drain)
    scaling = jnp.minimum(1.0, (full_rows * full_cols) ** 0.5 / jnp.sqrt(total + 1e-06))
    keep, fresh = second_decay, 1.0 - second_decay
    spread = scaling * scaling
    row_new = keep * states[0] + fresh * (spread * row_all * (1.0 / full_cols) + tiny_moment)
    col_new = keep * states[1] + fresh * (spread * col_all[0:8, :] * (1.0 / full_rows) + tiny_moment)
    row_mean = keep * (whole(col_all[8:9, :]) * (1.0 / full_rows)) + fresh * (
        spread * total * (1.0 / (full_rows * full_cols)) + tiny_moment)
    row_conf_sum = whole(col_all[9:10, :])
    states[0] = row_new
    states[1] = col_new
    row_part[2] = lax.rsqrt(row_new)
    col_scale = lax.rsqrt(col_new) * (scaling * jnp.sqrt(row_mean))

    def strays(i, at, j):
        here = (at, slice(j * LANES, (j + 1) * LANES))
        direction = G[here] * down_rows(row_part.at[2], i) * col_scale[j:j + 1, :]
        stray = direction - M[here]
        M[here] = M[here] + (1.0 - first_decay) * stray
        return stray * stray

    sums(1, strays)
    stores = [
        pltpu.make_async_copy(M, moment_out, store_sem.at[0]),
        pltpu.make_async_copy(states.at[0, pl.ds(0, nr)], row_out, store_sem.at[1]),
        pltpu.make_async_copy(states.at[1, pl.ds(0, nc)], col_out, store_sem.at[2]),
    ]

    def store_first():
        for store in stores:
            store.start()
        drain0()

    row_all, col_all, total, drain1 = reduced(1, store_first)
    share = first_decay * first_decay
    row_conf_new = keep * states[2] + fresh * (row_all * (share / full_cols) + tiny_confidence)
    col_conf_new = keep * states[3] + fresh * (col_all[0:8, :] * (share / full_rows) + tiny_confidence)
    conf_mean = keep * (row_conf_sum * (1.0 / full_rows)) + fresh * (
        total * (share / (full_rows * full_cols)) + tiny_confidence)
    states[2] = row_conf_new
    states[3] = col_conf_new
    stores += [
        pltpu.make_async_copy(states.at[2, pl.ds(0, nr)], row_conf_out, store_sem.at[3]),
        pltpu.make_async_copy(states.at[3, pl.ds(0, nc)], col_conf_out, store_sem.at[4]),
    ]
    for store in stores[3:]:
        store.start()
    row_part[3] = lax.rsqrt(row_conf_new)
    conf_scale = lax.rsqrt(col_conf_new) * jnp.sqrt(conf_mean)

    def update_store(i):
        at = part(i * LANES, LANES, LANES)
        return pltpu.make_async_copy(G.at[at], update_out.at[at], store_sem.at[5 + i])

    def finish(i, carry):
        at = part(i * LANES, LANES, LANES)
        scale = down_rows(row_part.at[3], i)
        for j in range(nc):
            here = (at, slice(j * LANES, (j + 1) * LANES))
            G[here] = M[here] * scale * conf_scale[j:j + 1, :]
        update_store(i).start()
        return carry

    lax.fori_loop(0, nr, finish, 0)
    drain1()
    for store in stores:
        store.wait()

    def stored(i, carry):
        update_store(i).wait()
        return carry

    lax.fori_loop(0, nr, stored, 0)


def on_device(acts, out_grads, moment, row_state, col_state, row_conf, col_conf):
    R, C = lax.axis_size("row"), lax.axis_size("col")
    rows, cols = moment.shape
    nr, nc = rows // LANES, cols // LANES
    dma = pltpu.SemaphoreType.DMA
    big = jax.ShapeDtypeStruct((rows, cols), F32)
    by_row, by_col = (jax.ShapeDtypeStruct((n, LANES), F32) for n in (nr, nc))
    anywhere = pl.BlockSpec(memory_space=pl.ANY)
    tokens = R * out_grads.shape[0]
    outs = pl.pallas_call(
        functools.partial(kernel, R, C),
        out_shape=(big, big, by_row, by_col, by_row, by_col),
        in_specs=[anywhere] * 7,
        out_specs=(anywhere,) * 6,
        scratch_shapes=[
            pltpu.VMEM((tokens, rows), acts.dtype),
            pltpu.VMEM((tokens, cols), out_grads.dtype),
            pltpu.VMEM((rows, cols), F32),
            pltpu.VMEM((rows, cols), F32),
            pltpu.VMEM((4, 8, LANES), F32),
            pltpu.VMEM((4, 8, LANES), F32),
            pltpu.VMEM((2, C, 8, LANES), F32),
            pltpu.VMEM((2, 16, LANES), F32),
            pltpu.VMEM((2, R, 16, LANES), F32),
            pltpu.VMEM((2, 8, LANES), F32),
            pltpu.VMEM((2, C, 8, LANES), F32),
            dma((4, R)), dma((4, R)), dma((11,)), dma((11,)), dma((7,)), dma((5 + nr,)),
            dma((2, C)), dma((2, C)), dma((2, R)), dma((2, R)), dma((2, C)), dma((2, C)),
        ],
        compiler_params=pltpu.CompilerParams(
            collective_id=0, has_side_effects=True, vmem_limit_bytes=48 * 2**20),
        cost_estimate=pl.CostEstimate(
            flops=2 * tokens * rows * cols, transcendentals=0, bytes_accessed=30 * 2**20),
        name="came_step",
    )(acts, out_grads, moment, row_state.reshape(nr, LANES), col_state.reshape(nc, LANES),
      row_conf.reshape(nr, LANES), col_conf.reshape(nc, LANES))
    return outs[0], outs[1], *(out.reshape(-1) for out in outs[2:])


def solution(mesh):
    placed = (
        P("col", "row"),
        P("row", "col"),
        P("row", "col"),
        P("row"),
        P("col"),
        P("row"),
        P("col"),
    )
    return jax.shard_map(
        on_device,
        mesh=mesh,
        in_specs=placed,
        out_specs=(P("row", "col"), P("row", "col"), P("row"), P("col"), P("row"), P("col")),
        check_vma=False,
    )
```

```python
import functools

import jax
import jax.numpy as jnp
from jax import lax
from jax.experimental import pallas as pl
from jax.experimental.pallas import tpu as pltpu
from jax.sharding import PartitionSpec as P

MESH = pl.DeviceIdType.MESH
F32 = jnp.float32
STEP = 10
X = 4
LANES = 128

first_decay = 0.9
tiny_moment = 1e-30
tiny_confidence = 1e-16
second_decay = 1.0 - STEP ** (-0.8)


ORDER = (
    ("z", "Q", 0, 0), ("x", "P", 0, 0), ("x", "Q", 0, 0), ("z", "P", 0, 0), "own low",
    ("z", "P", 1, 0), ("x", "P", 0, 1), ("x", "Q", 1, 0), ("z", "Q", 0, 1), "own high",
    ("x", "Q", -1, 0), ("z", "P", -1, 0), ("z", "P", 2, 0), ("x", "Q", 0, 1),
    ("z", "Q", 0, 2), ("x", "Q", 2, 0), ("z", "P", 0, 1), ("x", "Q", 1, 1), "near",
    ("z", "P", 1, 1), ("x", "Q", -2, 0), ("x", "Q", -1, 1), ("z", "Q", 0, 3), ("z", "P", -1, 1),
    ("x", "Q", 3, 0), ("z", "P", 2, 1), "cross",
    ("x", "Q", 2, 1), ("z", "P", 0, 2), ("x", "Q", -3, 0), ("z", "P", 1, 2), ("z", "P", -1, 2),
    ("x", "Q", -2, 1), ("z", "P", 2, 2), ("x", "Q", 4, 0), "far",
    ("z", "P", 0, 3), ("z", "P", 1, 3), "all", (0, 1, -1),
    ("x", "Q", 3, 1), ("z", "P", -1, 3), ("x", "Q", -3, 1), ("z", "P", 2, 3), (2, -2),
    ("x", "Q", 4, 1), (3, -3), (4,),
)
HOPS = {"z": 4, "x": 2}


def kernel(R, C, acts, grads, moment, row_state, col_state, row_conf, col_conf, M, packed,
           A, B, G, states, row_part, row_got, col_part, col_got, tot_part, tot_got,
           ring_send, ring_recv, act_send, act_recv, load_sem,
           row_send, row_recv, col_send, col_recv, tot_send, tot_recv):
    Z, Y = R // X, C // 2
    row, col = lax.axis_index("row"), lax.axis_index("col")
    div, rem = lax.div, lax.rem
    z, x, y, core = div(row, X), rem(row, X), div(col, 2), rem(col, 2)
    tb, shard = grads.shape[0], acts.shape[0]
    hs = shard // 2
    rows, cols = G.shape
    nr, nc = rows // LANES, cols // LANES
    full_rows, full_cols = rows * R, cols * C
    p_rows = 3 * tb // 8

    def at_offset(dz, dx):
        return rem(z + dz + Z, Z) * X + rem(x + dx + X, X)

    def part(first, unit, size):
        return pl.ds(pl.multiple_of(first, unit), size)

    ring_to = {("z", s): at_offset(s, 0) for s in (1, -1)} | {("x", s): at_offset(0, s) for s in (1, -1)}
    up, down = rem(y + 1, Y) * 2 + core, rem(y + Y - 1, Y) * 2 + core
    far, twin = rem(y + 2, Y) * 2 + core, y * 2 + 1 - core

    barrier = pltpu.get_barrier_semaphore()
    for r in ring_to.values():
        pl.semaphore_signal(barrier, inc=1, device_id=(r, col), device_id_type=MESH)
    for c in (up, down, twin):
        pl.semaphore_signal(barrier, inc=1, device_id=(row, c), device_id_type=MESH)

    loads = [
        pltpu.make_async_copy(grads, B.at[part(row * tb, tb, tb)], load_sem.at[0]),
        pltpu.make_async_copy(acts, A.at[part(col * shard, shard, shard)], load_sem.at[1]),
        pltpu.make_async_copy(moment, M, load_sem.at[2]),
        pltpu.make_async_copy(row_state, states.at[0, pl.ds(0, nr)], load_sem.at[3]),
        pltpu.make_async_copy(col_state, states.at[1, pl.ds(0, nc)], load_sem.at[4]),
        pltpu.make_async_copy(row_conf, states.at[2, pl.ds(0, nr)], load_sem.at[5]),
        pltpu.make_async_copy(col_conf, states.at[3, pl.ds(0, nc)], load_sem.at[6]),
    ]
    states[...] = jnp.zeros_like(states)
    for load in loads:
        load.start()
    pl.semaphore_wait(barrier, 7)

    def extent(message):
        axis, sign, kind, off, hops = message
        first, size = (0, p_rows) if kind == "P" else (p_rows, tb - p_rows)
        if hops == HOPS[axis] - 1:
            low = (size // 2 + 15) // 16 * 16
            low = size - low if off % 2 else low
            return (first, low) if sign > 0 else (first + low, size - low)
        return first, size

    def placed(message, hops):
        axis, sign, _, off, _ = message
        dz, dx = (-sign * hops, off) if axis == "z" else (off, -sign * hops)
        first, size = extent(message)
        return B.at[part(at_offset(dz, dx) * tb + first, 16, size)]

    numbers = {}

    def ring(message, hops):
        axis, sign, _, off, made = message
        lane = 2 * (axis == "x") + (sign < 0)
        number = numbers.setdefault(message, sum(m[:2] == message[:2] for m in numbers))
        first, size = extent(message)
        there = placed(message, hops)
        return pltpu.make_async_remote_copy(
            src_ref=grads.at[pl.ds(first, size)] if made == 0 and off == 0 else there, dst_ref=there,
            send_sem=ring_send.at[lane, number], recv_sem=ring_recv.at[lane, number],
            device_id=(ring_to[axis, sign], col), device_id_type=MESH)

    sent, landed = [], set()

    def await_messages(messages):
        for message in messages:
            if message not in landed:
                landed.add(message)
                ring(message, message[4] + 1).wait_recv()

    def brought(message):
        axis, sign, kind, off, hops = message
        if hops > 0:
            return [(axis, sign, kind, off, hops - 1)]
        if off == 0:
            return []
        other = "x" if axis == "z" else "z"
        last = HOPS[other] - 1
        if abs(off) == HOPS[other]:
            return [(other, 1, kind, 0, last), (other, -1, kind, 0, last)]
        return [(other, -1 if off > 0 else 1, kind, 0, abs(off) - 1)]

    def send(axis, kind, off, hops):
        mirrored = off if abs(off) == HOPS["x" if axis == "z" else "z"] else -off
        pair = [(axis, 1, kind, off, hops), (axis, -1, kind, mirrored, hops)]
        for message in pair:
            await_messages(brought(message))
            ring(message, hops).start()
            sent.append(message)

    def brings(message, dz):
        axis, sign, _, off, hops = message
        if axis == "x":
            return off == dz
        return dz == HOPS["z"] if hops == HOPS["z"] - 1 else dz == -sign * (hops + 1)

    def act(i, owner, first, size, to, src=None):
        there = A.at[part(owner * shard + first, hs, size)]
        return pltpu.make_async_remote_copy(
            src_ref=there if src is None else src, dst_ref=there,
            send_sem=act_send.at[i], recv_sem=act_recv.at[i],
            device_id=(row, to), device_id_type=MESH)

    low, high = acts.at[pl.ds(0, hs)], acts.at[pl.ds(hs, hs)]
    act_out = {
        0: act(0, col, 0, hs, up, low), 3: act(3, col, hs, hs, down, high),
        1: act(1, col, hs, hs, up, high), 4: act(4, col, 0, hs, down, low),
        6: act(6, col, 0, shard, twin, acts),
        2: act(2, down, 0, hs, up), 5: act(5, up, hs, hs, down),
        7: act(7, down, 0, shard, twin), 8: act(8, up, 0, shard, twin),
        9: act(9, far, 0, hs, twin), 10: act(10, far, hs, hs, twin),
    }
    swap = 1 - 2 * core
    act_in = {
        0: act(0, down, 0, hs, up), 1: act(1, down, hs, hs, up), 2: act(2, far, 0, hs, up),
        3: act(3, up, hs, hs, down), 4: act(4, up, 0, hs, down), 5: act(5, far, hs, hs, down),
        6: act(6, twin, 0, shard, twin), 7: act(7, down + swap, 0, shard, twin),
        8: act(8, up + swap, 0, shard, twin), 9: act(9, far + swap, 0, hs, twin),
        10: act(10, far + swap, hs, hs, twin),
    }
    act_steps = {
        "own low": ((), (0, 3, 6)), "own high": ((), (1, 4)), "near": ((0, 3), (2, 5)),
        "cross": ((1, 4), (7, 8)), "far": ((2, 5), (9, 10)), "all": ((6, 7, 8, 9, 10), ()),
    }

    def add_products(dzs):
        for dz in dzs:
            await_messages([m for m in sent if brings(m, dz)])

        def add(i, carry):
            dz = dzs[0] if len(dzs) == 1 else dzs[0] + i
            if len(dzs) == 2:
                dz = dzs[0] + i * (Z + dzs[1] - dzs[0])
            if len(dzs) == 3:
                dz = i + (Z - 3) * div(i, 2)
            tokens = part(rem(z + dz, Z) * (X * tb), X * tb, X * tb)
            G[...] += lax.dot_general(
                A[tokens, :], B[tokens, :], (((0,), (0,)), ((), ())), preferred_element_type=F32)
            return carry

        if len(dzs) == 1:
            add(0, 0)
        else:
            lax.fori_loop(0, len(dzs), add, 0)

    for entry in ORDER:
        if isinstance(entry, str):
            arrive, leave = act_steps[entry]
            for i in arrive:
                act_in[i].wait_recv()
            for i in leave:
                act_out[i].start()
            if entry == "own high":
                loads[0].wait()
                loads[1].wait()
                G[...] = jnp.zeros_like(G)
        elif entry[0] in ("x", "z"):
            send(*entry)
        else:
            add_products(entry)
    for load in loads[2:]:
        load.wait()

    def exchange(phase, src, got, axis, send_sem, recv_sem):
        me, size = (row, R) if axis == "row" else (col, C)
        steps = sorted(range(1, size), key=lambda i: -hops_to(axis, i))

        def copy(i, slot):
            to = rem(me + i, size)
            return pltpu.make_async_remote_copy(
                src_ref=src, dst_ref=got.at[phase, slot],
                send_sem=send_sem.at[phase, i], recv_sem=recv_sem.at[phase, i],
                device_id=(to, col) if axis == "row" else (row, to), device_id_type=MESH)

        def start():
            for i in steps:
                copy(i, me).start()
            got[phase, me] = src[...]

        def result():
            for i in reversed(steps):
                copy(i, rem(me + size - i, size)).wait_recv()
            return jnp.sum(got[phase, pl.ds(0, size)], axis=0)

        def drain():
            for i in steps:
                copy(i, me).wait_send()

        return start, result, drain

    def hops_to(axis, i):
        if axis == "row":
            dz, dx = i // X, i % X
            return min(dz, Z - dz) + min(dx, X - dx)
        return min(i // 2, Y - i // 2) + i % 2

    def whole(tile):
        return jnp.sum(tile, axis=(0, 1), keepdims=True)

    lane_ids = lax.broadcasted_iota(jnp.int32, (1, LANES), 1)

    def sums(phase, block):
        def rows_of(i, col_sum):
            at = part(i * LANES, LANES, LANES)
            row_sum = jnp.zeros((LANES, LANES), F32)
            col_sums = []
            for j in range(nc):
                square = block(i, at, j)
                row_sum += square
                col_sums.append(jnp.sum(square.reshape(LANES // 8, 8, LANES), axis=0))
            row_part[phase, pl.ds(i, 1), :] = jnp.sum(row_sum.T, axis=0, keepdims=True)
            return col_sum + jnp.concatenate(col_sums, 1)

        return lax.fori_loop(0, nr, rows_of, jnp.zeros((8, cols), F32))

    def reduced(phase, col_sum, beside, meanwhile):
        values = [whole(col_sum)] + beside
        packed_values = jnp.zeros((1, LANES), F32)
        for lane, value in enumerate(values):
            packed_values = jnp.where(lane_ids == lane, value, packed_values)
        tot_part[phase] = packed_values
        by_tot = exchange(phase, tot_part.at[phase], tot_got, "row", tot_send, tot_recv)
        by_tot[0]()
        col_sum = jnp.sum(col_sum, axis=0, keepdims=True)
        for j in range(nc):
            col_part[phase, j:j + 1, :] = col_sum[:, j * LANES:(j + 1) * LANES]
        by_col = exchange(phase, col_part.at[phase], col_got, "row", col_send, col_recv)
        by_row = exchange(phase, row_part.at[phase], row_got, "col", row_send, row_recv)
        by_col[0]()
        by_row[0]()
        meanwhile()
        tot_rows = by_tot[1]()
        tot_part[2 + phase] = tot_rows
        by_all = exchange(2 + phase, tot_part.at[2 + phase], tot_got, "col", tot_send, tot_recv)
        by_all[0]()
        col_all = by_col[1]()
        row_all = by_row[1]()
        for one in (by_tot, by_col, by_row):
            one[2]()
        tot_all = by_all[1]()

        def drain():
            by_all[2]()
        return row_all, col_all, tot_all, tot_rows, drain

    def down_rows(factor_ref, i):
        return jnp.broadcast_to(factor_ref[pl.ds(i, 1), :], (LANES, LANES)).T

    col_part[...] = jnp.zeros_like(col_part)
    row_part[...] = jnp.zeros_like(row_part)

    def squared(i, at, j):
        g = G[at, j * LANES:(j + 1) * LANES]
        return g * g

    def gather_drain():
        for message in sent:
            ring(message, message[4]).wait_send()
        for copy in act_out.values():
            copy.wait_send()

    col_sum = sums(0, squared)
    row_all, col_all, tot_all, tot_rows, drain0 = reduced(
        0, col_sum, [whole(states[0]), whole(states[2])], gather_drain)
    total, row_state_sum, row_conf_sum = tot_all[:, 0:1], tot_rows[:, 1:2], tot_rows[:, 2:3]
    scaling = jnp.minimum(1.0, (full_rows * full_cols) ** 0.5 / jnp.sqrt(total + 1e-06))
    keep, fresh = second_decay, 1.0 - second_decay
    spread = scaling * scaling
    row_new = keep * states[0] + fresh * (spread * row_all * (1.0 / full_cols) + tiny_moment)
    col_new = keep * states[1] + fresh * (spread * col_all * (1.0 / full_rows) + tiny_moment)
    row_mean = keep * (row_state_sum * (1.0 / full_rows)) + fresh * (
        spread * total * (1.0 / (full_rows * full_cols)) + tiny_moment)
    packed[0] = row_new
    packed[1] = col_new
    row_part[2] = lax.rsqrt(row_new)
    col_scale = lax.rsqrt(col_new) * (scaling * jnp.sqrt(row_mean))

    def strays(i, at, j):
        here = (at, slice(j * LANES, (j + 1) * LANES))
        direction = G[here] * down_rows(row_part.at[2], i) * col_scale[j:j + 1, :]
        stray = direction - M[here]
        M[here] = M[here] + (1.0 - first_decay) * stray
        return stray * stray

    col_sum = sums(1, strays)
    row_all, col_all, tot_all, _, drain1 = reduced(1, col_sum, [], drain0)
    total = tot_all[:, 0:1]
    share = first_decay * first_decay
    row_conf_new = keep * states[2] + fresh * (row_all * (share / full_cols) + tiny_confidence)
    col_conf_new = keep * states[3] + fresh * (col_all * (share / full_rows) + tiny_confidence)
    conf_mean = keep * (row_conf_sum * (1.0 / full_rows)) + fresh * (
        total * (share / (full_rows * full_cols)) + tiny_confidence)
    packed[2] = row_conf_new
    packed[3] = col_conf_new
    packed[4] = lax.rsqrt(row_conf_new)
    packed[5] = lax.rsqrt(col_conf_new) * jnp.sqrt(conf_mean)
    drain1()


def finish(M, packed, moment_out, update_out, row_out, col_out, row_conf_out, col_conf_out, U, sem, block_sem):
    rows, cols = U.shape
    nr, nc = rows // LANES, cols // LANES
    stores = [pltpu.make_async_copy(M, moment_out, sem.at[0])]
    for k, (out, n) in enumerate(((row_out, nr), (col_out, nc), (row_conf_out, nr), (col_conf_out, nc))):
        stores.append(pltpu.make_async_copy(packed.at[k, pl.ds(0, n)], out, sem.at[1 + k]))
    for store in stores:
        store.start()

    def block_store(i):
        at = pl.ds(pl.multiple_of(i * LANES, LANES), LANES)
        return pltpu.make_async_copy(U.at[at], update_out.at[at], block_sem.at[i])

    def scale_block(i, carry):
        at = pl.ds(pl.multiple_of(i * LANES, LANES), LANES)
        scale = jnp.broadcast_to(packed[4, pl.ds(i, 1), :], (LANES, LANES)).T
        for j in range(nc):
            here = (at, slice(j * LANES, (j + 1) * LANES))
            U[here] = M[here] * scale * packed[5, j:j + 1, :]
        block_store(i).start()
        return carry

    def wait_block(i, carry):
        block_store(i).wait()
        return carry

    lax.fori_loop(0, nr, scale_block, 0)
    lax.fori_loop(0, nr, wait_block, 0)
    for store in stores:
        store.wait()


def on_device(acts, out_grads, moment, row_state, col_state, row_conf, col_conf):
    R, C = lax.axis_size("row"), lax.axis_size("col")
    rows, cols = moment.shape
    nr, nc = rows // LANES, cols // LANES
    dma = pltpu.SemaphoreType.DMA
    big = jax.ShapeDtypeStruct((rows, cols), F32)
    by_row, by_col = (jax.ShapeDtypeStruct((n, LANES), F32) for n in (nr, nc))
    in_hbm = pl.BlockSpec(memory_space=pltpu.HBM)
    in_vmem = pl.BlockSpec(memory_space=pltpu.VMEM)
    tokens = R * out_grads.shape[0]
    moment_new, packed = pl.pallas_call(
        functools.partial(kernel, R, C),
        out_shape=(pltpu.VMEM((rows, cols), F32), pltpu.VMEM((6, 8, LANES), F32)),
        in_specs=[in_hbm] * 7,
        out_specs=(in_vmem,) * 2,
        scratch_shapes=[
            pltpu.VMEM((tokens, rows), acts.dtype),
            pltpu.VMEM((tokens, cols), out_grads.dtype),
            pltpu.VMEM((rows, cols), F32),
            pltpu.VMEM((4, 8, LANES), F32),
            pltpu.VMEM((3, 8, LANES), F32),
            pltpu.VMEM((2, C, 8, LANES), F32),
            pltpu.VMEM((2, 8, LANES), F32),
            pltpu.VMEM((2, R, 8, LANES), F32),
            pltpu.VMEM((4, 1, LANES), F32),
            pltpu.VMEM((4, R, 1, LANES), F32),
            dma((4, 20)), dma((4, 20)), dma((11,)), dma((11,)), dma((7,)),
            dma((2, C)), dma((2, C)), dma((2, R)), dma((2, R)), dma((4, R)), dma((4, R)),
        ],
        compiler_params=pltpu.CompilerParams(
            collective_id=0, has_side_effects=True, vmem_limit_bytes=40 * 2**20),
        cost_estimate=pl.CostEstimate(
            flops=2 * tokens * rows * cols, transcendentals=0, bytes_accessed=30 * 2**20),
        name="came_step",
    )(*(pltpu.with_memory_space_constraint(v, pltpu.HBM) for v in (
        acts, out_grads, moment, row_state.reshape(nr, LANES), col_state.reshape(nc, LANES),
        row_conf.reshape(nr, LANES), col_conf.reshape(nc, LANES))))
    outs = pl.pallas_call(
        finish,
        out_shape=(big, big, by_row, by_col, by_row, by_col),
        in_specs=[in_vmem] * 2,
        out_specs=(in_hbm,) * 6,
        scratch_shapes=[pltpu.VMEM((rows, cols), F32), dma((5,)), dma((nr,))],
        compiler_params=pltpu.CompilerParams(vmem_limit_bytes=16 * 2**20),
        cost_estimate=pl.CostEstimate(
            flops=2 * rows * cols, transcendentals=0, bytes_accessed=12 * rows * cols),
        name="finish",
    )(moment_new, packed)
    return outs[0], outs[1], *(out.reshape(-1) for out in outs[2:])


def solution(mesh):
    placed = (
        P("col", "row"),
        P("row", "col"),
        P("row", "col"),
        P("row"),
        P("col"),
        P("row"),
        P("col"),
    )
    return jax.shard_map(
        on_device,
        mesh=mesh,
        in_specs=placed,
        out_specs=(P("row", "col"), P("row", "col"), P("row"), P("col"), P("row"), P("col")),
        check_vma=False,
    )
```

```python
import functools

import jax
import jax.numpy as jnp
from jax import lax
from jax.experimental import pallas as pl
from jax.experimental.pallas import tpu as pltpu
from jax.sharding import PartitionSpec as P

MESH = pl.DeviceIdType.MESH
F32 = jnp.float32
STEP = 10
X = 4
LANES = 128

first_decay = 0.9
tiny_moment = 1e-30
tiny_confidence = 1e-16
second_decay = 1.0 - STEP ** (-0.8)


ORDER = (
    ("z", "Q", 0, 0), ("x", "P", 0, 0), ("x", "Q", 0, 0), ("z", "P", 0, 0), "own low",
    ("z", "P", 1, 0), ("x", "P", 0, 1), ("x", "Q", 1, 0), ("z", "Q", 0, 1), "own high",
    ("x", "Q", -1, 0), ("z", "P", -1, 0), "strip", ("z", "P", 2, 0), ("x", "Q", 0, 1),
    ("z", "Q", 0, 2), ("x", "Q", 2, 0), ("z", "P", 0, 1), ("x", "Q", 1, 1), "near",
    ("z", "P", 1, 1), ("x", "Q", -2, 0), ("x", "Q", -1, 1), ("z", "Q", 0, 3), ("z", "P", -1, 1),
    ("x", "Q", 3, 0), ("z", "P", 2, 1), "cross",
    ("x", "Q", 2, 1), ("z", "P", 0, 2), ("x", "Q", -3, 0), ("z", "P", 1, 2), ("z", "P", -1, 2),
    ("x", "Q", -2, 1), ("z", "P", 2, 2), ("x", "Q", 4, 0), "far",
    ("z", "P", 0, 3), ("z", "P", 1, 3), "all", (0, 1, -1),
    ("x", "Q", 3, 1), ("z", "P", -1, 3), ("x", "Q", -3, 1), ("z", "P", 2, 3), (2, -2),
    ("x", "Q", 4, 1), ((3, 0), (3, 1), (3, -1), (-3, 0), (-3, 1), (-3, -1)),
    ((4, 0), (4, 1), (4, -1), (3, 2)), ((-3, 2), (4, 2)),
)
HOPS = {"z": 4, "x": 2}


def kernel(R, C, acts, grads, moment, row_state, col_state, row_conf, col_conf, M, packed,
           A, B, G, states, row_part, row_got, col_part, col_got, tot_part, tot_got, all_part, all_got,
           ring_send, ring_recv, act_send, act_recv, load_sem,
           row_send, row_recv, col_send, col_recv, tot_send, tot_recv, all_send, all_recv):
    Z, Y = R // X, C // 2
    row, col = lax.axis_index("row"), lax.axis_index("col")
    div, rem = lax.div, lax.rem
    z, x, y, core = div(row, X), rem(row, X), div(col, 2), rem(col, 2)
    tb, shard = grads.shape[0], acts.shape[0]
    hs = shard // 2
    rows, cols = G.shape
    nr, nc = rows // LANES, cols // LANES
    full_rows, full_cols = rows * R, cols * C
    p_rows = 3 * tb // 8

    def at_offset(dz, dx):
        return rem(z + dz + Z, Z) * X + rem(x + dx + X, X)

    across = at_offset(0, 2)


    def part(first, unit, size):
        return pl.ds(pl.multiple_of(first, unit), size)

    ring_to = {("z", s): at_offset(s, 0) for s in (1, -1)} | {("x", s): at_offset(0, s) for s in (1, -1)}
    up, down = rem(y + 1, Y) * 2 + core, rem(y + Y - 1, Y) * 2 + core
    far, twin = rem(y + 2, Y) * 2 + core, y * 2 + 1 - core

    barrier = pltpu.get_barrier_semaphore()
    for r in (*ring_to.values(), across):
        pl.semaphore_signal(barrier, inc=1, device_id=(r, col), device_id_type=MESH)
    for c in (up, down, twin):
        pl.semaphore_signal(barrier, inc=1, device_id=(row, c), device_id_type=MESH)

    loads = [
        pltpu.make_async_copy(grads, B.at[part(row * tb, tb, tb)], load_sem.at[0]),
        pltpu.make_async_copy(acts, A.at[part(col * shard, shard, shard)], load_sem.at[1]),
        pltpu.make_async_copy(moment, M, load_sem.at[2]),
        pltpu.make_async_copy(row_state, states.at[0, pl.ds(0, nr)], load_sem.at[3]),
        pltpu.make_async_copy(col_state, states.at[1, pl.ds(0, nc)], load_sem.at[4]),
        pltpu.make_async_copy(row_conf, states.at[2, pl.ds(0, nr)], load_sem.at[5]),
        pltpu.make_async_copy(col_conf, states.at[3, pl.ds(0, nc)], load_sem.at[6]),
    ]
    states[...] = jnp.zeros_like(states)
    for load in loads:
        load.start()
    pl.semaphore_wait(barrier, 8)

    def extent(message):
        axis, sign, kind, off, hops = message
        first, size = (0, p_rows) if kind == "P" else (p_rows, tb - p_rows)
        if axis == "z" and kind == "P" and off == HOPS["x"]:
            size += 16
        if axis == "x" and kind == "Q" and hops == HOPS["x"] - 1:
            first, size = first + 16, size - 16
        if hops == HOPS[axis] - 1:
            low = (size // 2 + 15) // 16 * 16
            low = size - low if off % 2 else low
            return (first, low) if sign > 0 else (first + low, size - low)
        return first, size

    def placed(message, hops):
        axis, sign, _, off, _ = message
        dz, dx = (-sign * hops, off) if axis == "z" else (off, -sign * hops)
        first, size = extent(message)
        return B.at[part(at_offset(dz, dx) * tb + first, 16, size)]

    numbers = {}

    def ring(message, hops):
        axis, sign, _, off, made = message
        lane = 2 * (axis == "x") + (sign < 0)
        number = numbers.setdefault(message, sum(m[:2] == message[:2] for m in numbers))
        first, size = extent(message)
        there = placed(message, hops)
        return pltpu.make_async_remote_copy(
            src_ref=grads.at[pl.ds(first, size)] if made == 0 and off == 0 else there, dst_ref=there,
            send_sem=ring_send.at[lane, number], recv_sem=ring_recv.at[lane, number],
            device_id=(ring_to[axis, sign], col), device_id_type=MESH)

    def strip(owner):
        return pltpu.make_async_remote_copy(
            src_ref=grads.at[pl.ds(p_rows, 16)], dst_ref=B.at[part(owner * tb + p_rows, 16, 16)],
            send_sem=act_send.at[11], recv_sem=act_recv.at[11],
            device_id=(across, col), device_id_type=MESH)

    sent, landed = [], set()

    def await_messages(messages):
        for message in messages:
            if message not in landed:
                landed.add(message)
                ring(message, message[4] + 1).wait_recv()

    def brought(message):
        axis, sign, kind, off, hops = message
        if hops > 0:
            return [(axis, sign, kind, off, hops - 1)]
        if off == 0:
            return []
        other = "x" if axis == "z" else "z"
        last = HOPS[other] - 1
        if abs(off) == HOPS[other]:
            return [(other, 1, kind, 0, last), (other, -1, kind, 0, last)]
        return [(other, -1 if off > 0 else 1, kind, 0, abs(off) - 1)]

    def send(axis, kind, off, hops):
        mirrored = off if abs(off) == HOPS["x" if axis == "z" else "z"] else -off
        pair = [(axis, 1, kind, off, hops), (axis, -1, kind, mirrored, hops)]
        for message in pair:
            await_messages(brought(message))
            ring(message, hops).start()
            sent.append(message)

    def brings(message, dz):
        axis, sign, _, off, hops = message
        if axis == "x":
            return off == dz
        return dz == HOPS["z"] if hops == HOPS["z"] - 1 else dz == -sign * (hops + 1)

    def act(i, owner, first, size, to, src=None):
        there = A.at[part(owner * shard + first, hs, size)]
        return pltpu.make_async_remote_copy(
            src_ref=there if src is None else src, dst_ref=there,
            send_sem=act_send.at[i], recv_sem=act_recv.at[i],
            device_id=(row, to), device_id_type=MESH)

    low, high = acts.at[pl.ds(0, hs)], acts.at[pl.ds(hs, hs)]
    act_out = {
        0: act(0, col, 0, hs, up, low), 3: act(3, col, hs, hs, down, high),
        1: act(1, col, hs, hs, up, high), 4: act(4, col, 0, hs, down, low),
        6: act(6, col, 0, shard, twin, acts),
        2: act(2, down, 0, hs, up), 5: act(5, up, hs, hs, down),
        7: act(7, down, 0, shard, twin), 8: act(8, up, 0, shard, twin),
        9: act(9, far, 0, hs, twin), 10: act(10, far, hs, hs, twin),
    }
    swap = 1 - 2 * core
    act_in = {
        0: act(0, down, 0, hs, up), 1: act(1, down, hs, hs, up), 2: act(2, far, 0, hs, up),
        3: act(3, up, hs, hs, down), 4: act(4, up, 0, hs, down), 5: act(5, far, hs, hs, down),
        6: act(6, twin, 0, shard, twin), 7: act(7, down + swap, 0, shard, twin),
        8: act(8, up + swap, 0, shard, twin), 9: act(9, far + swap, 0, hs, twin),
        10: act(10, far + swap, hs, hs, twin),
    }
    act_steps = {
        "own low": ((), (0, 3, 6)), "own high": ((), (1, 4)), "near": ((0, 3), (2, 5)),
        "cross": ((1, 4), (7, 8)), "far": ((2, 5), (9, 10)), "all": ((6, 7, 8, 9, 10), ()),
        "strip": ((), ()),
    }

    def accumulate(a, b):
        G[...] += lax.dot_general(a, b, (((0,), (0,)), ((), ())), preferred_element_type=F32)

    def add_planes(dzs):
        for dz in dzs:
            await_messages([m for m in sent if brings(m, dz)])

        def add(i, carry):
            dz = i + (Z - 3) * div(i, 2) if len(dzs) == 3 else dzs[0] + i * (Z + dzs[1] - dzs[0])
            tokens = part(rem(z + dz, Z) * (X * tb), X * tb, X * tb)
            accumulate(A[tokens, :], B[tokens, :])
            return carry

        lax.fori_loop(0, len(dzs), add, 0)

    def add_blocks(offsets):
        for dz, dx in offsets:
            await_messages([m for m in sent if brings(m, dz) and (
                m[3] == dx if m[0] == "z" else dx == -m[1] * (m[4] + 1) or (dx == 2 and m[4] == 1))])
        tokens = [part(at_offset(dz, dx) * tb, tb, tb) for dz, dx in offsets]
        accumulate(jnp.concatenate([A[t, :] for t in tokens], 0),
                   jnp.concatenate([B[t, :] for t in tokens], 0))

    for entry in ORDER:
        if isinstance(entry, str):
            arrive, leave = act_steps[entry]
            for i in arrive:
                act_in[i].wait_recv()
            for i in leave:
                act_out[i].start()
            if entry == "own low":
                strip(row).start()
            if entry == "strip":
                strip(across).wait_recv()
            if entry == "own high":
                loads[0].wait()
                loads[1].wait()
                G[...] = jnp.zeros_like(G)
        elif entry[0] in ("x", "z"):
            send(*entry)
        elif isinstance(entry[0], int):
            add_planes(entry)
        else:
            add_blocks(entry)
    for load in loads[2:]:
        load.wait()

    def exchange(phase, src, got, axis, send_sem, recv_sem):
        me, size = (row, R) if axis == "row" else (col, C)
        steps = sorted(range(1, size), key=lambda i: -hops_to(axis, i))

        def copy(i, source, target):
            to = rem(me + i, size)
            return pltpu.make_async_remote_copy(
                src_ref=source, dst_ref=target,
                send_sem=send_sem.at[phase], recv_sem=recv_sem.at[phase],
                device_id=(to, col) if axis == "row" else (row, to), device_id_type=MESH)

        others = got.at[phase, pl.ds(0, size - 1)]

        def start():
            for i in steps:
                copy(i, src, got.at[phase, me]).start()
            got[phase, me] = src[...]

        def result():
            copy(1, others, others).wait_recv()
            return jnp.sum(got[phase, pl.ds(0, size)], axis=0)

        def drain():
            copy(1, others, others).wait_send()

        return start, result, drain

    def hops_to(axis, i):
        if axis == "row":
            dz, dx = i // X, i % X
            return min(dz, Z - dz) + min(dx, X - dx)
        return min(i // 2, Y - i // 2) + i % 2

    def whole(tile):
        return jnp.sum(tile, axis=(0, 1), keepdims=True)

    def sums(phase, block):
        def rows_of(i, col_sum):
            at = part(i * LANES, LANES, LANES)
            row_sum = jnp.zeros((LANES, LANES), F32)
            col_sums = []
            scale = down_rows(row_part.at[2], i) if phase else None
            for j in range(nc):
                square = block(at, j, scale)
                row_sum += square
                col_sums.append(jnp.sum(square.reshape(LANES // 8, 8, LANES), axis=0))
            row_part[phase, pl.ds(i, 1), :] = jnp.sum(row_sum.T, axis=0, keepdims=True)
            return col_sum + jnp.concatenate(col_sums, 1)

        return lax.fori_loop(0, nr, rows_of, jnp.zeros((8, cols), F32))

    def reduced(phase, col_sum, beside, meanwhile):
        col_sum = jnp.sum(col_sum, axis=0, keepdims=True)
        col_sums = [col_sum[:, j * LANES:(j + 1) * LANES] for j in range(nc)]
        tot_part[phase] = jnp.concatenate([functools.reduce(jnp.add, col_sums)] + beside, 1)
        by_tot = exchange(phase, tot_part.at[phase], tot_got, "row", tot_send, tot_recv)
        by_tot[0]()
        for j in range(nc):
            col_part[phase, j:j + 1, :] = col_sums[j]
        by_col = exchange(phase, col_part.at[phase], col_got, "row", col_send, col_recv)
        by_row = exchange(phase, row_part.at[phase], row_got, "col", row_send, row_recv)
        by_col[0]()
        by_row[0]()
        meanwhile()
        tot_rows = by_tot[1]()
        all_part[phase] = tot_rows[:, :LANES]
        by_all = exchange(phase, all_part.at[phase], all_got, "col", all_send, all_recv)
        by_all[0]()
        col_all = by_col[1]()
        row_all = by_row[1]()
        for one in (by_tot, by_col, by_row):
            one[2]()
        total = whole(by_all[1]())

        def drain():
            by_all[2]()
        return row_all, col_all, total, tot_rows, drain

    def down_rows(factor_ref, i):
        return jnp.broadcast_to(factor_ref[pl.ds(i, 1), :], (LANES, LANES)).T

    col_part[...] = jnp.zeros_like(col_part)
    row_part[...] = jnp.zeros_like(row_part)

    def squared(at, j, scale):
        g = G[at, j * LANES:(j + 1) * LANES]
        return g * g

    def gather_drain():
        for message in sent:
            ring(message, message[4]).wait_send()
        for copy in act_out.values():
            copy.wait_send()
        strip(row).wait_send()

    col_sum = sums(0, squared)
    states_sums = [jnp.sum(states[k], axis=0, keepdims=True) for k in (0, 2)]
    row_all, col_all, total, tot_rows, drain0 = reduced(0, col_sum, states_sums, gather_drain)
    row_state_sum, row_conf_sum = whole(tot_rows[:, LANES:2 * LANES]), whole(tot_rows[:, 2 * LANES:])
    spread = jnp.minimum(1.0, (full_rows * full_cols) / (total + 1e-06))
    keep, fresh = second_decay, 1.0 - second_decay
    row_new = keep * states[0] + fresh * (spread * row_all * (1.0 / full_cols) + tiny_moment)
    col_new = keep * states[1] + fresh * (spread * col_all * (1.0 / full_rows) + tiny_moment)
    row_mean = keep * (row_state_sum * (1.0 / full_rows)) + fresh * (
        spread * total * (1.0 / (full_rows * full_cols)) + tiny_moment)
    packed[0] = row_new
    packed[1] = col_new
    row_part[2] = lax.rsqrt(row_new)
    col_scale = lax.rsqrt(col_new) * jnp.sqrt(spread * row_mean)

    def strays(at, j, scale):
        here = (at, slice(j * LANES, (j + 1) * LANES))
        direction = G[here] * scale * col_scale[j:j + 1, :]
        stray = direction - M[here]
        M[here] = M[here] + (1.0 - first_decay) * stray
        return stray * stray

    col_sum = sums(1, strays)
    row_all, col_all, total, _, drain1 = reduced(1, col_sum, [jnp.zeros((1, 2 * LANES), F32)], drain0)
    share = first_decay * first_decay
    row_conf_new = keep * states[2] + fresh * (row_all * (share / full_cols) + tiny_confidence)
    col_conf_new = keep * states[3] + fresh * (col_all * (share / full_rows) + tiny_confidence)
    conf_mean = keep * (row_conf_sum * (1.0 / full_rows)) + fresh * (
        total * (share / (full_rows * full_cols)) + tiny_confidence)
    packed[2] = row_conf_new
    packed[3] = col_conf_new
    packed[4] = lax.rsqrt(row_conf_new)
    packed[5] = lax.rsqrt(col_conf_new) * jnp.sqrt(conf_mean)
    drain1()


def finish(M, packed, moment_out, update_out, row_out, col_out, row_conf_out, col_conf_out, U, sem, block_sem):
    rows, cols = U.shape
    nr, nc = rows // LANES, cols // LANES
    stores = [pltpu.make_async_copy(M, moment_out, sem.at[0])]
    for k, (out, n) in enumerate(((row_out, nr), (col_out, nc), (row_conf_out, nr), (col_conf_out, nc))):
        stores.append(pltpu.make_async_copy(packed.at[k, pl.ds(0, n)], out, sem.at[1 + k]))
    for store in stores:
        store.start()

    def block_store(i):
        at = pl.ds(pl.multiple_of(i * LANES, LANES), LANES)
        return pltpu.make_async_copy(U.at[at], update_out.at[at], block_sem.at[i])

    def scale_block(i, carry):
        at = pl.ds(pl.multiple_of(i * LANES, LANES), LANES)
        scale = jnp.broadcast_to(packed[4, pl.ds(i, 1), :], (LANES, LANES)).T
        for j in range(nc):
            here = (at, slice(j * LANES, (j + 1) * LANES))
            U[here] = M[here] * scale * packed[5, j:j + 1, :]
        block_store(i).start()
        return carry

    def wait_block(i, carry):
        block_store(i).wait()
        return carry

    lax.fori_loop(0, nr, scale_block, 0)
    lax.fori_loop(0, nr, wait_block, 0)
    for store in stores:
        store.wait()


def on_device(acts, out_grads, moment, row_state, col_state, row_conf, col_conf):
    R, C = lax.axis_size("row"), lax.axis_size("col")
    rows, cols = moment.shape
    nr, nc = rows // LANES, cols // LANES
    dma = pltpu.SemaphoreType.DMA
    big = jax.ShapeDtypeStruct((rows, cols), F32)
    by_row, by_col = (jax.ShapeDtypeStruct((n, LANES), F32) for n in (nr, nc))
    in_hbm = pl.BlockSpec(memory_space=pltpu.HBM)
    in_vmem = pl.BlockSpec(memory_space=pltpu.VMEM)
    tokens = R * out_grads.shape[0]
    moment_new, packed = pl.pallas_call(
        functools.partial(kernel, R, C),
        out_shape=(pltpu.VMEM((rows, cols), F32), pltpu.VMEM((6, 8, LANES), F32)),
        in_specs=[in_hbm] * 7,
        out_specs=(in_vmem,) * 2,
        scratch_shapes=[
            pltpu.VMEM((tokens, rows), acts.dtype),
            pltpu.VMEM((tokens, cols), out_grads.dtype),
            pltpu.VMEM((rows, cols), F32),
            pltpu.VMEM((4, 8, LANES), F32),
            pltpu.VMEM((3, 8, LANES), F32),
            pltpu.VMEM((2, C, 8, LANES), F32),
            pltpu.VMEM((2, 8, LANES), F32),
            pltpu.VMEM((2, R, 8, LANES), F32),
            pltpu.VMEM((2, 1, 3 * LANES), F32),
            pltpu.VMEM((2, R, 1, 3 * LANES), F32),
            pltpu.VMEM((2, 1, LANES), F32),
            pltpu.VMEM((2, C, 1, LANES), F32),
            dma((4, 20)), dma((4, 20)), dma((12,)), dma((12,)), dma((7,)),
            dma((2,)), dma((2,)), dma((2,)), dma((2,)), dma((2,)), dma((2,)), dma((2,)), dma((2,)),
        ],
        compiler_params=pltpu.CompilerParams(
            collective_id=0, has_side_effects=True, vmem_limit_bytes=40 * 2**20),
        cost_estimate=pl.CostEstimate(
            flops=2 * tokens * rows * cols, transcendentals=0, bytes_accessed=30 * 2**20),
        name="came_step",
    )(*(pltpu.with_memory_space_constraint(v, pltpu.HBM) for v in (
        acts, out_grads, moment, row_state.reshape(nr, LANES), col_state.reshape(nc, LANES),
        row_conf.reshape(nr, LANES), col_conf.reshape(nc, LANES))))
    outs = pl.pallas_call(
        finish,
        out_shape=(big, big, by_row, by_col, by_row, by_col),
        in_specs=[in_vmem] * 2,
        out_specs=(in_hbm,) * 6,
        scratch_shapes=[pltpu.VMEM((rows, cols), F32), dma((5,)), dma((nr,))],
        compiler_params=pltpu.CompilerParams(vmem_limit_bytes=16 * 2**20),
        cost_estimate=pl.CostEstimate(
            flops=2 * rows * cols, transcendentals=0, bytes_accessed=12 * rows * cols),
        name="finish",
    )(moment_new, packed)
    return outs[0], outs[1], *(out.reshape(-1) for out in outs[2:])


def solution(mesh):
    placed = (
        P("col", "row"),
        P("row", "col"),
        P("row", "col"),
        P("row"),
        P("col"),
        P("row"),
        P("col"),
    )
    return jax.shard_map(
        on_device,
        mesh=mesh,
        in_specs=placed,
        out_specs=(P("row", "col"), P("row", "col"), P("row"), P("col"), P("row"), P("col")),
        check_vma=False,
    )
```

```python
import functools

import jax
import jax.numpy as jnp
from jax import lax
from jax.experimental import pallas as pl
from jax.experimental.pallas import tpu as pltpu
from jax.sharding import PartitionSpec as P

MESH = pl.DeviceIdType.MESH
F32 = jnp.float32
STEP = 10
X = 4
LANES = 128

first_decay = 0.9
tiny_moment = 1e-30
tiny_confidence = 1e-16
second_decay = 1.0 - STEP ** (-0.8)


ORDER = (
    ("z", "Q", 0, 0), ("x", "P", 0, 0), ("x", "Q", 0, 0), ("z", "P", 0, 0), "own low",
    ("z", "P", 1, 0), ("x", "P", 0, 1), ("x", "Q", 1, 0), ("z", "Q", 0, 1), "own high",
    ("x", "Q", -1, 0), ("z", "P", -1, 0), "strip", ("z", "P", 2, 0), ("x", "Q", 0, 1),
    ("z", "Q", 0, 2), ("x", "Q", 2, 0), ("z", "P", 0, 1), ("x", "Q", 1, 1), "near",
    ("z", "P", 1, 1), ("x", "Q", -2, 0), ("x", "Q", -1, 1), ("z", "Q", 0, 3), ("z", "P", -1, 1),
    ("x", "Q", 3, 0), ("z", "P", 2, 1), "cross",
    ("x", "Q", 2, 1), ("x", "Q", -3, 0), ("z", "P", 0, 2), ("z", "P", 1, 2), ("x", "Q", -2, 1),
    ("z", "P", -1, 2), ("x", "Q", 4, 0), ("z", "P", 2, 2), "far", ("x", "Q", 3, 1), ("z", "P", 0, 3), "all",
)
FOURS_ORDER = ((), (("x", "Q", -3, 1),), (("z", "P", 1, 3),), (("z", "P", -1, 3),), (), (("x", "Q", 4, 1),))
TWOS_ORDER = ((("z", "P", 2, 3),), (), (), ())
HOPS = {"z": 4, "x": 2}


def kernel(R, C, acts, grads, moment, row_state, col_state, row_conf, col_conf, M, packed,
           A, B, G, states, row_sums, row_scale, row_part, row_got, col_part, col_got, tot_part, tot_got, all_part, all_got,
           ring_send, ring_recv, act_send, act_recv, load_sem,
           row_send, row_recv, col_send, col_recv, tot_send, tot_recv, all_send, all_recv):
    Z, Y = R // X, C // 2
    row, col = lax.axis_index("row"), lax.axis_index("col")
    div, rem = lax.div, lax.rem
    z, x, y, core = div(row, X), rem(row, X), div(col, 2), rem(col, 2)
    tb, shard = grads.shape[0], acts.shape[0]
    hs = shard // 2
    rows, cols = G.shape
    nr, nc = rows // LANES, cols // LANES
    full_rows, full_cols = rows * R, cols * C
    p_rows = 3 * tb // 8

    def at_offset(dz, dx):
        return rem(z + dz + Z, Z) * X + rem(x + dx + X, X)

    across = at_offset(0, 2)


    def part(first, unit, size):
        return pl.ds(pl.multiple_of(first, unit), size)

    ring_to = {("z", s): at_offset(s, 0) for s in (1, -1)} | {("x", s): at_offset(0, s) for s in (1, -1)}
    up, down = rem(y + 1, Y) * 2 + core, rem(y + Y - 1, Y) * 2 + core
    far, twin = rem(y + 2, Y) * 2 + core, y * 2 + 1 - core

    barrier = pltpu.get_barrier_semaphore()
    for r in (*ring_to.values(), across):
        pl.semaphore_signal(barrier, inc=1, device_id=(r, col), device_id_type=MESH)
    for c in (up, down, twin):
        pl.semaphore_signal(barrier, inc=1, device_id=(row, c), device_id_type=MESH)

    loads = [
        pltpu.make_async_copy(grads, B.at[part(row * tb, tb, tb)], load_sem.at[0]),
        pltpu.make_async_copy(acts, A.at[part(col * shard, shard, shard)], load_sem.at[1]),
        pltpu.make_async_copy(moment, M, load_sem.at[2]),
        pltpu.make_async_copy(row_state, states.at[0, pl.ds(0, nr)], load_sem.at[3]),
        pltpu.make_async_copy(col_state, states.at[1, pl.ds(0, nc)], load_sem.at[4]),
        pltpu.make_async_copy(row_conf, states.at[2, pl.ds(0, nr)], load_sem.at[5]),
        pltpu.make_async_copy(col_conf, states.at[3, pl.ds(0, nc)], load_sem.at[6]),
    ]
    states[...] = jnp.zeros_like(states)
    for load in loads:
        load.start()
    pl.semaphore_wait(barrier, 8)

    def extent(message):
        axis, sign, kind, off, hops = message
        first, size = (0, p_rows) if kind == "P" else (p_rows, tb - p_rows)
        if axis == "z" and kind == "P" and off == HOPS["x"]:
            size += 16
        if axis == "x" and kind == "Q" and hops == HOPS["x"] - 1:
            first, size = first + 16, size - 16
        if hops == HOPS[axis] - 1:
            low = (size // 2 + 15) // 16 * 16
            low = size - low if off % 2 else low
            return (first, low) if sign > 0 else (first + low, size - low)
        return first, size

    def placed(message, hops):
        axis, sign, _, off, _ = message
        dz, dx = (-sign * hops, off) if axis == "z" else (off, -sign * hops)
        first, size = extent(message)
        return B.at[part(at_offset(dz, dx) * tb + first, 16, size)]

    numbers = {}

    def ring(message, hops):
        axis, sign, _, off, made = message
        lane = 2 * (axis == "x") + (sign < 0)
        number = numbers.setdefault(message, sum(m[:2] == message[:2] for m in numbers))
        first, size = extent(message)
        there = placed(message, hops)
        return pltpu.make_async_remote_copy(
            src_ref=grads.at[pl.ds(first, size)] if made == 0 and off == 0 else there, dst_ref=there,
            send_sem=ring_send.at[lane, number], recv_sem=ring_recv.at[lane, number],
            device_id=(ring_to[axis, sign], col), device_id_type=MESH)

    def strip(owner):
        return pltpu.make_async_remote_copy(
            src_ref=grads.at[pl.ds(p_rows, 16)], dst_ref=B.at[part(owner * tb + p_rows, 16, 16)],
            send_sem=act_send.at[11], recv_sem=act_recv.at[11],
            device_id=(across, col), device_id_type=MESH)

    sent, landed = [], set()

    def await_messages(messages):
        for message in messages:
            if message not in landed:
                landed.add(message)
                ring(message, message[4] + 1).wait_recv()

    def brought(message):
        axis, sign, kind, off, hops = message
        if hops > 0:
            return [(axis, sign, kind, off, hops - 1)]
        if off == 0:
            return []
        other = "x" if axis == "z" else "z"
        last = HOPS[other] - 1
        if abs(off) == HOPS[other]:
            return [(other, 1, kind, 0, last), (other, -1, kind, 0, last)]
        return [(other, -1 if off > 0 else 1, kind, 0, abs(off) - 1)]

    def send(axis, kind, off, hops):
        mirrored = off if abs(off) == HOPS["x" if axis == "z" else "z"] else -off
        pair = [(axis, 1, kind, off, hops), (axis, -1, kind, mirrored, hops)]
        for message in pair:
            await_messages(brought(message))
            ring(message, hops).start()
            sent.append(message)

    def brings(message, dz):
        axis, sign, _, off, hops = message
        if axis == "x":
            return off == dz
        return dz == HOPS["z"] if hops == HOPS["z"] - 1 else dz == -sign * (hops + 1)

    def act(i, owner, first, size, to, src=None):
        there = A.at[part(owner * shard + first, hs, size)]
        return pltpu.make_async_remote_copy(
            src_ref=there if src is None else src, dst_ref=there,
            send_sem=act_send.at[i], recv_sem=act_recv.at[i],
            device_id=(row, to), device_id_type=MESH)

    low, high = acts.at[pl.ds(0, hs)], acts.at[pl.ds(hs, hs)]
    act_out = {
        0: act(0, col, 0, hs, up, low), 3: act(3, col, hs, hs, down, high),
        1: act(1, col, hs, hs, up, high), 4: act(4, col, 0, hs, down, low),
        6: act(6, col, 0, shard, twin, acts),
        2: act(2, down, 0, hs, up), 5: act(5, up, hs, hs, down),
        7: act(7, down, 0, shard, twin), 8: act(8, up, 0, shard, twin),
        9: act(9, far, 0, hs, twin), 10: act(10, far, hs, hs, twin),
    }
    swap = 1 - 2 * core
    act_in = {
        0: act(0, down, 0, hs, up), 1: act(1, down, hs, hs, up), 2: act(2, far, 0, hs, up),
        3: act(3, up, hs, hs, down), 4: act(4, up, 0, hs, down), 5: act(5, far, hs, hs, down),
        6: act(6, twin, 0, shard, twin), 7: act(7, down + swap, 0, shard, twin),
        8: act(8, up + swap, 0, shard, twin), 9: act(9, far + swap, 0, hs, twin),
        10: act(10, far + swap, hs, hs, twin),
    }
    act_steps = {
        "own low": ((), (0, 3, 6)), "own high": ((), (1, 4)), "near": ((0, 3), (2, 5)),
        "cross": ((1, 4), (7, 8)), "far": ((2, 5), (9, 10)), "all": ((6, 7, 8, 9, 10), ()),
        "strip": ((), ()),
    }

    def fours(i):
        dz, odd = div(i + 1, 2) * (2 * rem(i, 2) - 1), div(i, 5)
        return (dz, 0), (dz, 1), (dz, 3), (dz - 6 * odd, 2 - 2 * odd)

    def twos(i):
        return (5 - 2 * rem(i, 2) + div(i, 3), 1 + div(i + 1, 2)), (5 - div(i + 2, 3), i - 1)

    def await_blocks(offsets):
        for dz, dx in offsets:
            dz, dx = (dz + Z // 2 - 1) % Z - Z // 2 + 1, (dx + 1) % X - 1
            await_messages([m for m in sent if brings(m, dz) and (
                m[3] == dx if m[0] == "z" else dx == -m[1] * (m[4] + 1) or (dx == 2 and m[4] == 1))])

    def add_products(blocks, order):
        def ahead(n):
            for message in order[n]:
                send(*message)
            await_blocks(static_blocks(blocks, n))

        def add(i, carry):
            for n in range(len(order)):
                pl.when(i == n)(functools.partial(ahead, n))
            tokens = [part(at_offset(dz, dx) * tb, tb, tb) for dz, dx in blocks(i)]
            G[...] += lax.dot_general(
                jnp.concatenate([A[t, :] for t in tokens], 0), jnp.concatenate([B[t, :] for t in tokens], 0),
                (((0,), (0,)), ((), ())), preferred_element_type=F32)
            return carry

        lax.fori_loop(0, len(order), add, 0)

    def static_blocks(blocks, n):
        if blocks is fours:
            dz, odd = (n + 1) // 2 * (2 * (n % 2) - 1), n // 5
            return (dz, 0), (dz, 1), (dz, 3), (dz - 6 * odd, 2 - 2 * odd)
        return (5 - 2 * (n % 2) + n // 3, 1 + (n + 1) // 2), (5 - (n + 2) // 3, n - 1)

    for entry in ORDER:
        if isinstance(entry, str):
            arrive, leave = act_steps[entry]
            for i in arrive:
                act_in[i].wait_recv()
            for i in leave:
                act_out[i].start()
            if entry == "own low":
                strip(row).start()
            if entry == "strip":
                strip(across).wait_recv()
            if entry == "own high":
                loads[0].wait()
                loads[1].wait()
                G[...] = jnp.zeros_like(G)
        else:
            send(*entry)
    add_products(fours, FOURS_ORDER)
    add_products(twos, TWOS_ORDER)
    for load in loads[2:]:
        load.wait()

    def exchange(phase, src, got, axis, send_sem, recv_sem):
        me, size = (row, R) if axis == "row" else (col, C)
        steps = sorted(range(1, size), key=lambda i: -hops_to(axis, i))

        def copy(i, source, target):
            to = rem(me + i, size)
            return pltpu.make_async_remote_copy(
                src_ref=source, dst_ref=target,
                send_sem=send_sem.at[phase], recv_sem=recv_sem.at[phase],
                device_id=(to, col) if axis == "row" else (row, to), device_id_type=MESH)

        others = got.at[phase, pl.ds(0, size - 1)]

        def start():
            for i in steps:
                copy(i, src, got.at[phase, me]).start()
            got[phase, me] = src[...]

        def result():
            copy(1, others, others).wait_recv()
            return jnp.sum(got[phase, pl.ds(0, size)], axis=0)

        def drain():
            copy(1, others, others).wait_send()

        return start, result, drain

    def hops_to(axis, i):
        if axis == "row":
            dz, dx = i // X, i % X
            return min(dz, Z - dz) + min(dx, X - dx)
        return min(i // 2, Y - i // 2) + i % 2

    def whole(tile):
        return jnp.sum(tile, axis=(0, 1), keepdims=True)

    def sums(block):
        def rows_of(i, col_sum):
            at = part(i * LANES, LANES, LANES)
            row_sum = jnp.zeros((LANES, LANES), F32)
            col_sums = []
            for j in range(nc):
                square = block(at, j)
                row_sum += square
                col_sums.append(jnp.sum(square.reshape(LANES // 8, 8, LANES), axis=0))
            row_sums[at, :] = row_sum
            return col_sum + jnp.concatenate(col_sums, 1)

        return lax.fori_loop(0, nr, rows_of, jnp.zeros((8, cols), F32))

    def reduced(phase, col_sum, beside, meanwhile):
        col_sum = jnp.sum(col_sum, axis=0, keepdims=True)
        col_sums = [col_sum[:, j * LANES:(j + 1) * LANES] for j in range(nc)]
        tot_part[phase] = jnp.concatenate([functools.reduce(jnp.add, col_sums)] + beside, 1)
        by_tot = exchange(phase, tot_part.at[phase], tot_got, "row", tot_send, tot_recv)
        by_tot[0]()
        for j in range(nc):
            col_part[phase, j:j + 1, :] = col_sums[j]
        by_col = exchange(phase, col_part.at[phase], col_got, "row", col_send, col_recv)
        by_row = exchange(phase, row_part.at[phase], row_got, "col", row_send, row_recv)
        by_col[0]()
        for i in range(nr):
            turned = row_sums[i * LANES:(i + 1) * LANES, :].T
            row_part[phase, i:i + 1, :] = jnp.sum(turned, axis=0, keepdims=True)
        by_row[0]()
        meanwhile()
        tot_rows = by_tot[1]()
        all_part[phase] = tot_rows[:, :LANES]
        by_all = exchange(phase, all_part.at[phase], all_got, "col", all_send, all_recv)
        by_all[0]()
        col_all = by_col[1]()
        row_all = by_row[1]()
        for one in (by_tot, by_col, by_row):
            one[2]()
        total = whole(by_all[1]())

        def drain():
            by_all[2]()
        return row_all, col_all, total, tot_rows, drain

    def down_rows(factors):
        for i in range(nr):
            row_scale[i * LANES:(i + 1) * LANES, :] = jnp.broadcast_to(factors[i:i + 1, :], (LANES, LANES)).T

    col_part[...] = jnp.zeros_like(col_part)
    row_part[...] = jnp.zeros_like(row_part)

    def squared(at, j):
        g = G[at, j * LANES:(j + 1) * LANES]
        return g * g

    def gather_drain():
        for message in sent:
            ring(message, message[4]).wait_send()
        for copy in act_out.values():
            copy.wait_send()
        strip(row).wait_send()

    col_sum = sums(squared)
    states_sums = [jnp.sum(states[k], axis=0, keepdims=True) for k in (0, 2)]
    row_all, col_all, total, tot_rows, drain0 = reduced(0, col_sum, states_sums, gather_drain)
    row_state_sum, row_conf_sum = whole(tot_rows[:, LANES:2 * LANES]), whole(tot_rows[:, 2 * LANES:])
    spread = jnp.minimum(1.0, (full_rows * full_cols) / (total + 1e-06))
    keep, fresh = second_decay, 1.0 - second_decay
    row_new = keep * states[0] + fresh * (spread * row_all * (1.0 / full_cols) + tiny_moment)
    col_new = keep * states[1] + fresh * (spread * col_all * (1.0 / full_rows) + tiny_moment)
    row_mean = keep * (row_state_sum * (1.0 / full_rows)) + fresh * (
        spread * total * (1.0 / (full_rows * full_cols)) + tiny_moment)
    down_rows(lax.rsqrt(row_new))
    packed[0] = row_new
    packed[1] = col_new
    col_scale = lax.rsqrt(col_new) * jnp.sqrt(spread * row_mean)

    def strays(at, j):
        here = (at, slice(j * LANES, (j + 1) * LANES))
        direction = G[here] * row_scale[at, :] * col_scale[j:j + 1, :]
        stray = direction - M[here]
        M[here] = M[here] + (1.0 - first_decay) * stray
        return stray * stray

    col_sum = sums(strays)
    row_all, col_all, total, _, drain1 = reduced(1, col_sum, [jnp.zeros((1, 2 * LANES), F32)], drain0)
    share = first_decay * first_decay
    row_conf_new = keep * states[2] + fresh * (row_all * (share / full_cols) + tiny_confidence)
    col_conf_new = keep * states[3] + fresh * (col_all * (share / full_rows) + tiny_confidence)
    conf_mean = keep * (row_conf_sum * (1.0 / full_rows)) + fresh * (
        total * (share / (full_rows * full_cols)) + tiny_confidence)
    packed[2] = row_conf_new
    packed[3] = col_conf_new
    packed[4] = lax.rsqrt(row_conf_new)
    packed[5] = lax.rsqrt(col_conf_new) * jnp.sqrt(conf_mean)
    drain1()


def finish(M, packed, moment_out, update_out, row_out, col_out, row_conf_out, col_conf_out, U, sem, block_sem):
    rows, cols = U.shape
    nr, nc = rows // LANES, cols // LANES
    stores = [pltpu.make_async_copy(M, moment_out, sem.at[0])]
    for k, (out, n) in enumerate(((row_out, nr), (col_out, nc), (row_conf_out, nr), (col_conf_out, nc))):
        stores.append(pltpu.make_async_copy(packed.at[k, pl.ds(0, n)], out, sem.at[1 + k]))
    for store in stores:
        store.start()

    def block_store(i):
        at = pl.ds(pl.multiple_of(i * LANES, LANES), LANES)
        return pltpu.make_async_copy(U.at[at], update_out.at[at], block_sem.at[i])

    def scale_block(i, carry):
        at = pl.ds(pl.multiple_of(i * LANES, LANES), LANES)
        scale = jnp.broadcast_to(packed[4, pl.ds(i, 1), :], (LANES, LANES)).T
        for j in range(nc):
            here = (at, slice(j * LANES, (j + 1) * LANES))
            U[here] = M[here] * scale * packed[5, j:j + 1, :]
        block_store(i).start()
        return carry

    def wait_block(i, carry):
        block_store(i).wait()
        return carry

    lax.fori_loop(0, nr, scale_block, 0)
    lax.fori_loop(0, nr, wait_block, 0)
    for store in stores:
        store.wait()


def on_device(acts, out_grads, moment, row_state, col_state, row_conf, col_conf):
    R, C = lax.axis_size("row"), lax.axis_size("col")
    rows, cols = moment.shape
    nr, nc = rows // LANES, cols // LANES
    dma = pltpu.SemaphoreType.DMA
    big = jax.ShapeDtypeStruct((rows, cols), F32)
    by_row, by_col = (jax.ShapeDtypeStruct((n, LANES), F32) for n in (nr, nc))
    in_hbm = pl.BlockSpec(memory_space=pltpu.HBM)
    in_vmem = pl.BlockSpec(memory_space=pltpu.VMEM)
    tokens = R * out_grads.shape[0]
    moment_new, packed = pl.pallas_call(
        functools.partial(kernel, R, C),
        out_shape=(pltpu.VMEM((rows, cols), F32), pltpu.VMEM((6, 8, LANES), F32)),
        in_specs=[in_hbm] * 7,
        out_specs=(in_vmem,) * 2,
        scratch_shapes=[
            pltpu.VMEM((tokens, rows), acts.dtype),
            pltpu.VMEM((tokens, cols), out_grads.dtype),
            pltpu.VMEM((rows, cols), F32),
            pltpu.VMEM((4, 8, LANES), F32),
            pltpu.VMEM((rows, LANES), F32),
            pltpu.VMEM((rows, LANES), F32),
            pltpu.VMEM((2, 8, LANES), F32),
            pltpu.VMEM((2, C, 8, LANES), F32),
            pltpu.VMEM((2, 8, LANES), F32),
            pltpu.VMEM((2, R, 8, LANES), F32),
            pltpu.VMEM((2, 1, 3 * LANES), F32),
            pltpu.VMEM((2, R, 1, 3 * LANES), F32),
            pltpu.VMEM((2, 1, LANES), F32),
            pltpu.VMEM((2, C, 1, LANES), F32),
            dma((4, 20)), dma((4, 20)), dma((12,)), dma((12,)), dma((7,)),
            dma((2,)), dma((2,)), dma((2,)), dma((2,)), dma((2,)), dma((2,)), dma((2,)), dma((2,)),
        ],
        compiler_params=pltpu.CompilerParams(
            collective_id=0, has_side_effects=True, vmem_limit_bytes=40 * 2**20),
        cost_estimate=pl.CostEstimate(
            flops=2 * tokens * rows * cols, transcendentals=0, bytes_accessed=30 * 2**20),
        name="came_step",
    )(*(pltpu.with_memory_space_constraint(v, pltpu.HBM) for v in (
        acts, out_grads, moment, row_state.reshape(nr, LANES), col_state.reshape(nc, LANES),
        row_conf.reshape(nr, LANES), col_conf.reshape(nc, LANES))))
    outs = pl.pallas_call(
        finish,
        out_shape=(big, big, by_row, by_col, by_row, by_col),
        in_specs=[in_vmem] * 2,
        out_specs=(in_hbm,) * 6,
        scratch_shapes=[pltpu.VMEM((rows, cols), F32), dma((5,)), dma((nr,))],
        compiler_params=pltpu.CompilerParams(vmem_limit_bytes=16 * 2**20),
        cost_estimate=pl.CostEstimate(
            flops=2 * rows * cols, transcendentals=0, bytes_accessed=12 * rows * cols),
        name="finish",
    )(moment_new, packed)
    return outs[0], outs[1], *(out.reshape(-1) for out in outs[2:])


def solution(mesh):
    placed = (
        P("col", "row"),
        P("row", "col"),
        P("row", "col"),
        P("row"),
        P("col"),
        P("row"),
        P("col"),
    )
    return jax.shard_map(
        on_device,
        mesh=mesh,
        in_specs=placed,
        out_specs=(P("row", "col"), P("row", "col"), P("row"), P("col"), P("row"), P("col")),
        check_vma=False,
    )
```

```python
import functools

import jax
import jax.numpy as jnp
from jax import lax
from jax.experimental import pallas as pl
from jax.experimental.pallas import tpu as pltpu
from jax.sharding import PartitionSpec as P

MESH = pl.DeviceIdType.MESH
F32 = jnp.float32
STEP = 10
X = 4
LANES = 128

first_decay = 0.9
tiny_moment = 1e-30
tiny_confidence = 1e-16
second_decay = 1.0 - STEP ** (-0.8)


ORDER = (
    ("z", "Q", 0, 0), ("x", "P", 0, 0), ("x", "Q", 0, 0), ("z", "P", 0, 0), "own low",
    ("z", "P", 1, 0), ("x", "P", 0, 1), ("x", "Q", 1, 0), ("z", "Q", 0, 1), "own high",
    ("x", "Q", -1, 0), ("z", "P", -1, 0), ("x", "Q", 0, 1), "strip out", ("z", "P", 0, 1),
    ("z", "Q", 0, 2), ("x", "Q", 2, 0), ("x", "Q", 1, 1), "strip", ("z", "P", 2, 0), "near",
    ("z", "P", 1, 1), ("x", "Q", -2, 0), ("x", "Q", -1, 1), ("z", "Q", 0, 3), ("z", "P", -1, 1),
    ("x", "Q", 3, 0), ("z", "P", 2, 1), "cross",
    ("x", "Q", 2, 1), ("x", "Q", -3, 0), ("z", "P", 0, 2), ("z", "P", 1, 2), ("x", "Q", -2, 1),
    ("z", "P", -1, 2), ("x", "Q", 4, 0), ("z", "P", 2, 2), "far", ("x", "Q", 3, 1), ("z", "P", 0, 3), "all",
)
FOURS_ORDER = ((), (("x", "Q", -3, 1),), (("z", "P", 1, 3),), (("z", "P", -1, 3),), (), (("x", "Q", 4, 1),))
TWOS_ORDER = ((("z", "P", 2, 3),), (), (), ())
HOPS = {"z": 4, "x": 2}


def kernel(R, C, acts, grads, moment, row_state, col_state, row_conf, col_conf, M, packed,
           A, B, G, states, row_sums, row_scale, row_part, row_got, col_part, col_got, tot_part, tot_got, all_part, all_got,
           ring_send, ring_recv, act_send, act_recv, load_sem,
           row_send, row_recv, col_send, col_recv, tot_send, tot_recv, all_send, all_recv):
    Z, Y = R // X, C // 2
    row, col = lax.axis_index("row"), lax.axis_index("col")
    div, rem = lax.div, lax.rem
    z, x, y, core = div(row, X), rem(row, X), div(col, 2), rem(col, 2)
    tb, shard = grads.shape[0], acts.shape[0]
    hs = shard // 2
    rows, cols = G.shape
    nr, nc = rows // LANES, cols // LANES
    full_rows, full_cols = rows * R, cols * C
    p_rows = 3 * tb // 8

    def at_offset(dz, dx):
        return rem(z + dz + Z, Z) * X + rem(x + dx + X, X)

    across = at_offset(0, 2)


    def part(first, unit, size):
        return pl.ds(pl.multiple_of(first, unit), size)

    ring_to = {("z", s): at_offset(s, 0) for s in (1, -1)} | {("x", s): at_offset(0, s) for s in (1, -1)}
    up, down = rem(y + 1, Y) * 2 + core, rem(y + Y - 1, Y) * 2 + core
    far, twin = rem(y + 2, Y) * 2 + core, y * 2 + 1 - core

    barrier = pltpu.get_barrier_semaphore()
    for r in ring_to.values():
        pl.semaphore_signal(barrier, inc=1, device_id=(r, col), device_id_type=MESH)
    for c in (up, down, twin):
        pl.semaphore_signal(barrier, inc=1, device_id=(row, c), device_id_type=MESH)

    loads = [
        pltpu.make_async_copy(grads, B.at[part(row * tb, tb, tb)], load_sem.at[0]),
        pltpu.make_async_copy(acts, A.at[part(col * shard, shard, shard)], load_sem.at[1]),
        pltpu.make_async_copy(moment, M, load_sem.at[2]),
        pltpu.make_async_copy(row_state, states.at[0, pl.ds(0, nr)], load_sem.at[3]),
        pltpu.make_async_copy(col_state, states.at[1, pl.ds(0, nc)], load_sem.at[4]),
        pltpu.make_async_copy(row_conf, states.at[2, pl.ds(0, nr)], load_sem.at[5]),
        pltpu.make_async_copy(col_conf, states.at[3, pl.ds(0, nc)], load_sem.at[6]),
    ]
    states[...] = jnp.zeros_like(states)
    for load in loads:
        load.start()
    pl.semaphore_wait(barrier, 7)

    def extent(message):
        axis, sign, kind, off, hops = message
        first, size = (0, p_rows) if kind == "P" else (p_rows, tb - p_rows)
        if axis == "z" and kind == "P" and off == HOPS["x"]:
            size += 16
        if axis == "x" and kind == "Q" and hops == HOPS["x"] - 1:
            first, size = first + 16, size - 16
        if hops == HOPS[axis] - 1:
            low = (size // 2 + 15) // 16 * 16
            low = size - low if off % 2 else low
            return (first, low) if sign > 0 else (first + low, size - low)
        return first, size

    def placed(message, hops):
        axis, sign, _, off, _ = message
        dz, dx = (-sign * hops, off) if axis == "z" else (off, -sign * hops)
        first, size = extent(message)
        return B.at[part(at_offset(dz, dx) * tb + first, 16, size)]

    numbers = {}

    def ring(message, hops):
        axis, sign, _, off, made = message
        lane = 2 * (axis == "x") + (sign < 0)
        number = numbers.setdefault(message, sum(m[:2] == message[:2] for m in numbers))
        first, size = extent(message)
        there = placed(message, hops)
        return pltpu.make_async_remote_copy(
            src_ref=grads.at[pl.ds(first, size)] if made == 0 and off == 0 else there, dst_ref=there,
            send_sem=ring_send.at[lane], recv_sem=ring_recv.at[lane, number],
            device_id=(ring_to[axis, sign], col), device_id_type=MESH)

    def strip(owner):
        return pltpu.make_async_remote_copy(
            src_ref=grads.at[pl.ds(p_rows, 16)], dst_ref=B.at[part(owner * tb + p_rows, 16, 16)],
            send_sem=act_send.at[1], recv_sem=act_recv.at[11],
            device_id=(across, col), device_id_type=MESH)

    sent, landed = [], set()

    def await_messages(messages):
        for message in messages:
            if message not in landed:
                landed.add(message)
                ring(message, message[4] + 1).wait_recv()

    def brought(message):
        axis, sign, kind, off, hops = message
        if hops > 0:
            return [(axis, sign, kind, off, hops - 1)]
        if off == 0:
            return []
        other = "x" if axis == "z" else "z"
        last = HOPS[other] - 1
        if abs(off) == HOPS[other]:
            return [(other, 1, kind, 0, last), (other, -1, kind, 0, last)]
        return [(other, -1 if off > 0 else 1, kind, 0, abs(off) - 1)]

    def send(axis, kind, off, hops):
        mirrored = off if abs(off) == HOPS["x" if axis == "z" else "z"] else -off
        pair = [(axis, 1, kind, off, hops), (axis, -1, kind, mirrored, hops)]
        for message in pair:
            await_messages(brought(message))
            ring(message, hops).start()
            sent.append(message)

    def brings(message, dz):
        axis, sign, _, off, hops = message
        if axis == "x":
            return off == dz
        return dz == HOPS["z"] if hops == HOPS["z"] - 1 else dz == -sign * (hops + 1)

    def act(i, owner, first, size, to, src=None):
        there = A.at[part(owner * shard + first, hs, size)]
        return pltpu.make_async_remote_copy(
            src_ref=there if src is None else src, dst_ref=there,
            send_sem=act_send.at[0], recv_sem=act_recv.at[i],
            device_id=(row, to), device_id_type=MESH)

    low, high = acts.at[pl.ds(0, hs)], acts.at[pl.ds(hs, hs)]
    act_out = {
        0: act(0, col, 0, hs, up, low), 3: act(3, col, hs, hs, down, high),
        1: act(1, col, hs, hs, up, high), 4: act(4, col, 0, hs, down, low),
        6: act(6, col, 0, shard, twin, acts),
        2: act(2, down, 0, hs, up), 5: act(5, up, hs, hs, down),
        7: act(7, down, 0, shard, twin), 8: act(8, up, 0, shard, twin),
        9: act(9, far, 0, hs, twin), 10: act(10, far, hs, hs, twin),
    }
    swap = 1 - 2 * core
    act_in = {
        0: act(0, down, 0, hs, up), 1: act(1, down, hs, hs, up), 2: act(2, far, 0, hs, up),
        3: act(3, up, hs, hs, down), 4: act(4, up, 0, hs, down), 5: act(5, far, hs, hs, down),
        6: act(6, twin, 0, shard, twin), 7: act(7, down + swap, 0, shard, twin),
        8: act(8, up + swap, 0, shard, twin), 9: act(9, far + swap, 0, hs, twin),
        10: act(10, far + swap, hs, hs, twin),
    }
    act_steps = {
        "own low": ((), (0, 3, 6)), "own high": ((), (1, 4)), "near": ((0, 3), (2, 5)),
        "cross": ((1, 4), (7, 8)), "far": ((2, 5), (9, 10)), "all": ((6, 7, 8, 9, 10), ()),
        "strip": ((), ()), "strip out": ((), ()),
    }

    def fours(i):
        dz, odd = div(i + 1, 2) * (2 * rem(i, 2) - 1), div(i, 5)
        return (dz, 0), (dz, 1), (dz, 3), (dz - 6 * odd, 2 - 2 * odd)

    def twos(i):
        return (5 - 2 * rem(i, 2) + div(i, 3), 1 + div(i + 1, 2)), (5 - div(i + 2, 3), i - 1)

    def await_blocks(offsets):
        for dz, dx in offsets:
            dz, dx = (dz + Z // 2 - 1) % Z - Z // 2 + 1, (dx + 1) % X - 1
            await_messages([m for m in sent if brings(m, dz) and (
                m[3] == dx if m[0] == "z" else dx == -m[1] * (m[4] + 1) or (dx == 2 and m[4] == 1))])

    def add_products(blocks, order):
        def ahead(n):
            for message in order[n]:
                send(*message)
            await_blocks(static_blocks(blocks, n))

        def add(i, carry):
            for n in range(len(order)):
                pl.when(i == n)(functools.partial(ahead, n))
            tokens = [part(at_offset(dz, dx) * tb, tb, tb) for dz, dx in blocks(i)]
            G[...] += lax.dot_general(
                jnp.concatenate([A[t, :] for t in tokens], 0), jnp.concatenate([B[t, :] for t in tokens], 0),
                (((0,), (0,)), ((), ())), preferred_element_type=F32)
            return carry

        lax.fori_loop(0, len(order), add, 0)

    def static_blocks(blocks, n):
        if blocks is fours:
            dz, odd = (n + 1) // 2 * (2 * (n % 2) - 1), n // 5
            return (dz, 0), (dz, 1), (dz, 3), (dz - 6 * odd, 2 - 2 * odd)
        return (5 - 2 * (n % 2) + n // 3, 1 + (n + 1) // 2), (5 - (n + 2) // 3, n - 1)

    for entry in ORDER:
        if isinstance(entry, str):
            arrive, leave = act_steps[entry]
            for i in arrive:
                act_in[i].wait_recv()
            for i in leave:
                act_out[i].start()
            if entry == "strip out":
                await_messages([("x", s, "P", 0, 1) for s in (1, -1)])
                strip(row).start()
            if entry == "strip":
                strip(across).wait_recv()
            if entry == "own high":
                loads[0].wait()
                loads[1].wait()
                G[...] = jnp.zeros_like(G)
        else:
            send(*entry)
    add_products(fours, FOURS_ORDER)
    add_products(twos, TWOS_ORDER)
    for load in loads[2:]:
        load.wait()

    def exchange(phase, src, got, axis, send_sem, recv_sem):
        me, size = (row, R) if axis == "row" else (col, C)

        def from_far(k, length):
            return length // 2 + div(k + 1, 2) * (2 * rem(k, 2) - 1)

        def copy(k, source, target):
            if axis == "row":
                to = at_offset(from_far(div(k, X), Z), from_far(rem(k, X), X)), col
            else:
                to = row, rem(y + from_far(div(k, 2), Y), Y) * 2 + rem(core + 1 + k, 2)
            return pltpu.make_async_remote_copy(
                src_ref=source, dst_ref=target,
                send_sem=send_sem.at[phase], recv_sem=recv_sem.at[phase],
                device_id=to, device_id_type=MESH)

        others = got.at[phase, pl.ds(0, size - 1)]

        def start():
            def go(k, carry):
                copy(k, src, got.at[phase, me]).start()
                return carry
            lax.fori_loop(0, size - 1, go, 0)
            got[phase, me] = src[...]

        def result():
            copy(0, others, others).wait_recv()
            return jnp.sum(got[phase, pl.ds(0, size)], axis=0)

        def drain():
            copy(0, others, others).wait_send()

        return start, result, drain

    def whole(tile):
        return jnp.sum(tile, axis=(0, 1), keepdims=True)

    def sums(block):
        def rows_of(i, col_sum):
            at = part(i * LANES, LANES, LANES)
            row_sum = jnp.zeros((LANES, LANES), F32)
            col_sums = []
            for j in range(nc):
                square = block(at, j)
                row_sum += square
                col_sums.append(jnp.sum(square.reshape(LANES // 8, 8, LANES), axis=0))
            row_sums[at, :] = row_sum
            return col_sum + jnp.concatenate(col_sums, 1)

        return lax.fori_loop(0, nr, rows_of, jnp.zeros((8, cols), F32))

    def reduced(phase, col_sum, beside, meanwhile):
        col_sum = jnp.sum(col_sum, axis=0, keepdims=True)
        col_sums = [col_sum[:, j * LANES:(j + 1) * LANES] for j in range(nc)]
        tot_part[phase] = jnp.concatenate([functools.reduce(jnp.add, col_sums)] + beside, 1)
        by_tot = exchange(phase, tot_part.at[phase], tot_got, "row", tot_send, tot_recv)
        by_tot[0]()
        for j in range(nc):
            col_part[phase, j:j + 1, :] = col_sums[j]
        by_col = exchange(phase, col_part.at[phase], col_got, "row", col_send, col_recv)
        by_row = exchange(phase, row_part.at[phase], row_got, "col", row_send, row_recv)
        by_col[0]()
        for i in range(nr):
            turned = row_sums[i * LANES:(i + 1) * LANES, :].T
            row_part[phase, i:i + 1, :] = jnp.sum(turned, axis=0, keepdims=True)
        by_row[0]()
        meanwhile()
        tot_rows = by_tot[1]()
        all_part[phase] = tot_rows[:, :LANES]
        by_all = exchange(phase, all_part.at[phase], all_got, "col", all_send, all_recv)
        by_all[0]()
        col_all = by_col[1]()
        row_all = by_row[1]()
        for one in (by_tot, by_col, by_row):
            one[2]()
        total = whole(by_all[1]())

        def drain():
            by_all[2]()
        return row_all, col_all, total, tot_rows, drain

    def down_rows(factors):
        for i in range(nr):
            row_scale[i * LANES:(i + 1) * LANES, :] = jnp.broadcast_to(factors[i:i + 1, :], (LANES, LANES)).T

    col_part[...] = jnp.zeros_like(col_part)
    row_part[...] = jnp.zeros_like(row_part)

    def squared(at, j):
        g = G[at, j * LANES:(j + 1) * LANES]
        return g * g

    def gather_drain():
        for lane, (axis, sign) in enumerate(ring_to):
            gone = sum(extent(m)[1] for m in sent if m[:2] == (axis, sign))
            gone = B.at[pl.ds(0, gone)]
            pltpu.make_async_remote_copy(
                src_ref=gone, dst_ref=gone, send_sem=ring_send.at[lane], recv_sem=ring_recv.at[lane, 0],
                device_id=(ring_to[axis, sign], col), device_id_type=MESH).wait_send()
        gone = A.at[pl.ds(0, 7 * shard)]
        pltpu.make_async_remote_copy(
            src_ref=gone, dst_ref=gone, send_sem=act_send.at[0], recv_sem=act_recv.at[0],
            device_id=(row, twin), device_id_type=MESH).wait_send()
        strip(row).wait_send()

    col_sum = sums(squared)
    states_sums = [jnp.sum(states[k], axis=0, keepdims=True) for k in (0, 2)]
    row_all, col_all, total, tot_rows, drain0 = reduced(0, col_sum, states_sums, gather_drain)
    row_state_sum, row_conf_sum = whole(tot_rows[:, LANES:2 * LANES]), whole(tot_rows[:, 2 * LANES:])
    spread = jnp.minimum(1.0, (full_rows * full_cols) / (total + 1e-06))
    keep, fresh = second_decay, 1.0 - second_decay
    row_new = keep * states[0] + fresh * (spread * row_all * (1.0 / full_cols) + tiny_moment)
    col_new = keep * states[1] + fresh * (spread * col_all * (1.0 / full_rows) + tiny_moment)
    row_mean = keep * (row_state_sum * (1.0 / full_rows)) + fresh * (
        spread * total * (1.0 / (full_rows * full_cols)) + tiny_moment)
    down_rows(lax.rsqrt(row_new))
    packed[0] = row_new
    packed[1] = col_new
    col_scale = lax.rsqrt(col_new) * jnp.sqrt(spread * row_mean)

    def strays(at, j):
        here = (at, slice(j * LANES, (j + 1) * LANES))
        direction = G[here] * row_scale[at, :] * col_scale[j:j + 1, :]
        stray = direction - M[here]
        M[here] = M[here] + (1.0 - first_decay) * stray
        return stray * stray

    col_sum = sums(strays)
    row_all, col_all, total, _, drain1 = reduced(1, col_sum, [jnp.zeros((1, 2 * LANES), F32)], drain0)
    share = first_decay * first_decay
    row_conf_new = keep * states[2] + fresh * (row_all * (share / full_cols) + tiny_confidence)
    col_conf_new = keep * states[3] + fresh * (col_all * (share / full_rows) + tiny_confidence)
    conf_mean = keep * (row_conf_sum * (1.0 / full_rows)) + fresh * (
        total * (share / (full_rows * full_cols)) + tiny_confidence)
    packed[2] = row_conf_new
    packed[3] = col_conf_new
    packed[4] = lax.rsqrt(row_conf_new)
    packed[5] = lax.rsqrt(col_conf_new) * jnp.sqrt(conf_mean)
    drain1()


def finish(M, packed, moment_out, update_out, row_out, col_out, row_conf_out, col_conf_out, U, sem, block_sem):
    rows, cols = U.shape
    nr, nc = rows // LANES, cols // LANES
    stores = [pltpu.make_async_copy(M, moment_out, sem.at[0])]
    for k, (out, n) in enumerate(((row_out, nr), (col_out, nc), (row_conf_out, nr), (col_conf_out, nc))):
        stores.append(pltpu.make_async_copy(packed.at[k, pl.ds(0, n)], out, sem.at[1 + k]))
    for store in stores:
        store.start()

    def block_store(i):
        at = pl.ds(pl.multiple_of(i * LANES, LANES), LANES)
        return pltpu.make_async_copy(U.at[at], update_out.at[at], block_sem.at[i])

    def scale_block(i, carry):
        at = pl.ds(pl.multiple_of(i * LANES, LANES), LANES)
        scale = jnp.broadcast_to(packed[4, pl.ds(i, 1), :], (LANES, LANES)).T
        for j in range(nc):
            here = (at, slice(j * LANES, (j + 1) * LANES))
            U[here] = M[here] * scale * packed[5, j:j + 1, :]
        block_store(i).start()
        return carry

    def wait_block(i, carry):
        block_store(i).wait()
        return carry

    lax.fori_loop(0, nr, scale_block, 0)
    lax.fori_loop(0, nr, wait_block, 0)
    for store in stores:
        store.wait()


def on_device(acts, out_grads, moment, row_state, col_state, row_conf, col_conf):
    R, C = lax.axis_size("row"), lax.axis_size("col")
    rows, cols = moment.shape
    nr, nc = rows // LANES, cols // LANES
    dma = pltpu.SemaphoreType.DMA
    big = jax.ShapeDtypeStruct((rows, cols), F32)
    by_row, by_col = (jax.ShapeDtypeStruct((n, LANES), F32) for n in (nr, nc))
    in_hbm = pl.BlockSpec(memory_space=pltpu.HBM)
    in_vmem = pl.BlockSpec(memory_space=pltpu.VMEM)
    tokens = R * out_grads.shape[0]
    moment_new, packed = pl.pallas_call(
        functools.partial(kernel, R, C),
        out_shape=(pltpu.VMEM((rows, cols), F32), pltpu.VMEM((6, 8, LANES), F32)),
        in_specs=[in_hbm] * 7,
        out_specs=(in_vmem,) * 2,
        scratch_shapes=[
            pltpu.VMEM((tokens, rows), acts.dtype),
            pltpu.VMEM((tokens, cols), out_grads.dtype),
            pltpu.VMEM((rows, cols), F32),
            pltpu.VMEM((4, 8, LANES), F32),
            pltpu.VMEM((rows, LANES), F32),
            pltpu.VMEM((rows, LANES), F32),
            pltpu.VMEM((2, 8, LANES), F32),
            pltpu.VMEM((2, C, 8, LANES), F32),
            pltpu.VMEM((2, 8, LANES), F32),
            pltpu.VMEM((2, R, 8, LANES), F32),
            pltpu.VMEM((2, 1, 3 * LANES), F32),
            pltpu.VMEM((2, R, 1, 3 * LANES), F32),
            pltpu.VMEM((2, 1, LANES), F32),
            pltpu.VMEM((2, C, 1, LANES), F32),
            dma((4,)), dma((4, 20)), dma((2,)), dma((12,)), dma((7,)),
            dma((2,)), dma((2,)), dma((2,)), dma((2,)), dma((2,)), dma((2,)), dma((2,)), dma((2,)),
        ],
        compiler_params=pltpu.CompilerParams(
            collective_id=0, has_side_effects=True, vmem_limit_bytes=40 * 2**20),
        cost_estimate=pl.CostEstimate(
            flops=2 * tokens * rows * cols, transcendentals=0, bytes_accessed=30 * 2**20),
        name="came_step",
    )(*(pltpu.with_memory_space_constraint(v, pltpu.HBM) for v in (
        acts, out_grads, moment, row_state.reshape(nr, LANES), col_state.reshape(nc, LANES),
        row_conf.reshape(nr, LANES), col_conf.reshape(nc, LANES))))
    outs = pl.pallas_call(
        finish,
        out_shape=(big, big, by_row, by_col, by_row, by_col),
        in_specs=[in_vmem] * 2,
        out_specs=(in_hbm,) * 6,
        scratch_shapes=[pltpu.VMEM((rows, cols), F32), dma((5,)), dma((nr,))],
        compiler_params=pltpu.CompilerParams(vmem_limit_bytes=16 * 2**20),
        cost_estimate=pl.CostEstimate(
            flops=2 * rows * cols, transcendentals=0, bytes_accessed=12 * rows * cols),
        name="finish",
    )(moment_new, packed)
    return outs[0], outs[1], *(out.reshape(-1) for out in outs[2:])


def solution(mesh):
    placed = (
        P("col", "row"),
        P("row", "col"),
        P("row", "col"),
        P("row"),
        P("col"),
        P("row"),
        P("col"),
    )
    return jax.shard_map(
        on_device,
        mesh=mesh,
        in_specs=placed,
        out_specs=(P("row", "col"), P("row", "col"), P("row"), P("col"), P("row"), P("col")),
        check_vma=False,
    )
```

```python
import functools

import jax
import jax.numpy as jnp
from jax import lax
from jax.experimental import pallas as pl
from jax.experimental.pallas import tpu as pltpu
from jax.sharding import PartitionSpec as P

MESH = pl.DeviceIdType.MESH
F32 = jnp.float32
STEP = 10
X = 4
LANES = 128

first_decay = 0.9
tiny_moment = 1e-30
tiny_confidence = 1e-16
second_decay = 1.0 - STEP ** (-0.8)


ORDER = (
    ("z", "Q", 0, 0), ("x", "P", 0, 0), ("x", "Q", 0, 0), ("z", "P", 0, 0), "own low",
    ("z", "P", 1, 0), ("x", "P", 0, 1), ("x", "Q", 1, 0), ("z", "Q", 0, 1), "own high",
    ("x", "Q", -1, 0), ("z", "P", -1, 0), ("x", "Q", 0, 1), "strip out", ("z", "P", 0, 1),
    ("z", "Q", 0, 2), ("x", "Q", 2, 0), ("x", "Q", 1, 1), "strip", ("z", "P", 2, 0), "near",
    ("z", "P", 1, 1), ("x", "Q", -2, 0), ("x", "Q", -1, 1), ("z", "Q", 0, 3), ("z", "P", -1, 1),
    ("x", "Q", 3, 0), ("z", "P", 2, 1), "cross",
    ("x", "Q", 2, 1), ("x", "Q", -3, 0), ("z", "P", 0, 2), ("z", "P", 1, 2), ("x", "Q", -2, 1),
    ("z", "P", -1, 2), ("x", "Q", 4, 0), "far", ("z", "P", 2, 2), ("x", "Q", 3, 1), "all",
)
FOURS_ORDER = (
    (), (("z", "P", 0, 3),), (), (("x", "Q", -3, 1), ("z", "P", 1, 3)), (), (("z", "P", -1, 3),))
TWOS_ORDER = ((), (("x", "Q", 4, 1), ("z", "P", 2, 3)), (), ())
HOPS = {"z": 4, "x": 2}


def kernel(R, C, acts, grads, moment, row_state, col_state, row_conf, col_conf, M, packed,
           A, B, G, states, row_sums, row_scale, row_part, row_got, col_part, col_got, tot_part, tot_got, all_part, all_got,
           ring_send, ring_recv, act_send, act_recv, load_sem,
           row_send, row_recv, col_send, col_recv, tot_send, tot_recv, all_send, all_recv):
    Z, Y = R // X, C // 2
    row, col = lax.axis_index("row"), lax.axis_index("col")
    div, rem = lax.div, lax.rem
    z, x, y, core = div(row, X), rem(row, X), div(col, 2), rem(col, 2)
    tb, shard = grads.shape[0], acts.shape[0]
    hs = shard // 2
    rows, cols = G.shape
    nr, nc = rows // LANES, cols // LANES
    full_rows, full_cols = rows * R, cols * C
    p_rows = 3 * tb // 8

    def at_offset(dz, dx):
        return rem(z + dz + Z, Z) * X + rem(x + dx + X, X)

    across = at_offset(0, 2)


    def part(first, unit, size):
        return pl.ds(pl.multiple_of(first, unit), size)

    ring_to = {("z", s): at_offset(s, 0) for s in (1, -1)} | {("x", s): at_offset(0, s) for s in (1, -1)}
    up, down = rem(y + 1, Y) * 2 + core, rem(y + Y - 1, Y) * 2 + core
    far, twin = rem(y + 2, Y) * 2 + core, y * 2 + 1 - core

    barrier = pltpu.get_barrier_semaphore()
    for r in ring_to.values():
        pl.semaphore_signal(barrier, inc=1, device_id=(r, col), device_id_type=MESH)
    for c in (up, down, twin):
        pl.semaphore_signal(barrier, inc=1, device_id=(row, c), device_id_type=MESH)

    loads = [
        pltpu.make_async_copy(grads, B.at[part(row * tb, tb, tb)], load_sem.at[0]),
        pltpu.make_async_copy(acts, A.at[part(col * shard, shard, shard)], load_sem.at[1]),
        pltpu.make_async_copy(moment, M, load_sem.at[2]),
        pltpu.make_async_copy(row_state, states.at[0, pl.ds(0, nr)], load_sem.at[3]),
        pltpu.make_async_copy(col_state, states.at[1, pl.ds(0, nc)], load_sem.at[4]),
        pltpu.make_async_copy(row_conf, states.at[2, pl.ds(0, nr)], load_sem.at[5]),
        pltpu.make_async_copy(col_conf, states.at[3, pl.ds(0, nc)], load_sem.at[6]),
    ]
    states[...] = jnp.zeros_like(states)
    for load in loads:
        load.start()
    pl.semaphore_wait(barrier, 7)

    def extent(message):
        axis, sign, kind, off, hops = message
        first, size = (0, p_rows) if kind == "P" else (p_rows, tb - p_rows)
        if axis == "z" and kind == "P" and off == HOPS["x"]:
            size += 16
        if axis == "x" and kind == "Q" and hops == HOPS["x"] - 1:
            first, size = first + 16, size - 16
        if hops == HOPS[axis] - 1:
            low = (size // 2 + 15) // 16 * 16
            low = size - low if off % 2 else low
            return (first, low) if sign > 0 else (first + low, size - low)
        return first, size

    def placed(message, hops):
        axis, sign, _, off, _ = message
        dz, dx = (-sign * hops, off) if axis == "z" else (off, -sign * hops)
        first, size = extent(message)
        return B.at[part(at_offset(dz, dx) * tb + first, 16, size)]

    numbers = {}

    def ring(message, hops):
        axis, sign, _, off, made = message
        lane = 2 * (axis == "x") + (sign < 0)
        number = numbers.setdefault(message, sum(m[:2] == message[:2] for m in numbers))
        first, size = extent(message)
        there = placed(message, hops)
        return pltpu.make_async_remote_copy(
            src_ref=grads.at[pl.ds(first, size)] if made == 0 and off == 0 else there, dst_ref=there,
            send_sem=ring_send.at[lane], recv_sem=ring_recv.at[lane, number],
            device_id=(ring_to[axis, sign], col), device_id_type=MESH)

    def strip(owner):
        return pltpu.make_async_remote_copy(
            src_ref=grads.at[pl.ds(p_rows, 16)], dst_ref=B.at[part(owner * tb + p_rows, 16, 16)],
            send_sem=act_send.at[1], recv_sem=act_recv.at[11],
            device_id=(across, col), device_id_type=MESH)

    sent, landed = [], set()

    def await_messages(messages):
        for message in messages:
            if message not in landed:
                landed.add(message)
                ring(message, message[4] + 1).wait_recv()

    def brought(message):
        axis, sign, kind, off, hops = message
        if hops > 0:
            return [(axis, sign, kind, off, hops - 1)]
        if off == 0:
            return []
        other = "x" if axis == "z" else "z"
        last = HOPS[other] - 1
        if abs(off) == HOPS[other]:
            return [(other, 1, kind, 0, last), (other, -1, kind, 0, last)]
        return [(other, -1 if off > 0 else 1, kind, 0, abs(off) - 1)]

    def send(axis, kind, off, hops):
        mirrored = off if abs(off) == HOPS["x" if axis == "z" else "z"] else -off
        pair = [(axis, 1, kind, off, hops), (axis, -1, kind, mirrored, hops)]
        for message in pair:
            await_messages(brought(message))
            ring(message, hops).start()
            sent.append(message)

    def brings(message, dz):
        axis, sign, _, off, hops = message
        if axis == "x":
            return off == dz
        return dz == HOPS["z"] if hops == HOPS["z"] - 1 else dz == -sign * (hops + 1)

    def act(i, owner, first, size, to, src=None):
        there = A.at[part(owner * shard + first, hs, size)]
        return pltpu.make_async_remote_copy(
            src_ref=there if src is None else src, dst_ref=there,
            send_sem=act_send.at[0], recv_sem=act_recv.at[i],
            device_id=(row, to), device_id_type=MESH)

    low, high = acts.at[pl.ds(0, hs)], acts.at[pl.ds(hs, hs)]
    act_out = {
        0: act(0, col, 0, hs, up, low), 3: act(3, col, hs, hs, down, high),
        1: act(1, col, hs, hs, up, high), 4: act(4, col, 0, hs, down, low),
        6: act(6, col, 0, shard, twin, acts),
        2: act(2, down, 0, hs, up), 5: act(5, up, hs, hs, down),
        7: act(7, down, 0, shard, twin), 8: act(8, up, 0, shard, twin),
        9: act(9, far, 0, hs, twin), 10: act(10, far, hs, hs, twin),
    }
    swap = 1 - 2 * core
    act_in = {
        0: act(0, down, 0, hs, up), 1: act(1, down, hs, hs, up), 2: act(2, far, 0, hs, up),
        3: act(3, up, hs, hs, down), 4: act(4, up, 0, hs, down), 5: act(5, far, hs, hs, down),
        6: act(6, twin, 0, shard, twin), 7: act(7, down + swap, 0, shard, twin),
        8: act(8, up + swap, 0, shard, twin), 9: act(9, far + swap, 0, hs, twin),
        10: act(10, far + swap, hs, hs, twin),
    }
    act_steps = {
        "own low": ((), (0, 3, 6)), "own high": ((), (1, 4)), "near": ((0, 3), (2, 5)),
        "cross": ((1, 4), (7, 8)), "far": ((2, 5), (9, 10)), "all": ((6, 7, 8, 9, 10), ()),
        "strip": ((), ()), "strip out": ((), ()),
    }

    def fours(i):
        dz, odd = div(i + 1, 2) * (2 * rem(i, 2) - 1), div(i, 5)
        return (dz, 0), (dz, 1), (dz, 3), (dz - 6 * odd, 2 - 2 * odd)

    def twos(i):
        return (5 - 2 * rem(i, 2) + div(i, 3), 1 + div(i + 1, 2)), (5 - div(i + 2, 3), i - 1)

    def await_blocks(offsets):
        for dz, dx in offsets:
            dz, dx = (dz + Z // 2 - 1) % Z - Z // 2 + 1, (dx + 1) % X - 1
            await_messages([m for m in sent if brings(m, dz) and (
                m[3] == dx if m[0] == "z" else dx == -m[1] * (m[4] + 1) or (dx == 2 and m[4] == 1))])

    def add_products(blocks, order):
        def ahead(n):
            for message in order[n]:
                send(*message)
            await_blocks(static_blocks(blocks, n))

        def add(i, carry):
            for n in range(len(order)):
                pl.when(i == n)(functools.partial(ahead, n))
            tokens = [part(at_offset(dz, dx) * tb, tb, tb) for dz, dx in blocks(i)]
            G[...] += lax.dot_general(
                jnp.concatenate([A[t, :] for t in tokens], 0), jnp.concatenate([B[t, :] for t in tokens], 0),
                (((0,), (0,)), ((), ())), preferred_element_type=F32)
            return carry

        lax.fori_loop(0, len(order), add, 0)

    def static_blocks(blocks, n):
        if blocks is fours:
            dz, odd = (n + 1) // 2 * (2 * (n % 2) - 1), n // 5
            return (dz, 0), (dz, 1), (dz, 3), (dz - 6 * odd, 2 - 2 * odd)
        return (5 - 2 * (n % 2) + n // 3, 1 + (n + 1) // 2), (5 - (n + 2) // 3, n - 1)

    for entry in ORDER:
        if isinstance(entry, str):
            arrive, leave = act_steps[entry]
            for i in arrive:
                act_in[i].wait_recv()
            for i in leave:
                act_out[i].start()
            if entry == "strip out":
                await_messages([("x", s, "P", 0, 1) for s in (1, -1)])
                strip(row).start()
            if entry == "strip":
                strip(across).wait_recv()
            if entry == "own high":
                loads[0].wait()
                loads[1].wait()
                G[...] = jnp.zeros_like(G)
        else:
            send(*entry)
    add_products(fours, FOURS_ORDER)
    add_products(twos, TWOS_ORDER)
    for load in loads[2:]:
        load.wait()

    def exchange(phase, src, got, axis, send_sem, recv_sem):
        me, size = (row, R) if axis == "row" else (col, C)

        def from_far(k, length):
            return length // 2 + div(k + 1, 2) * (2 * rem(k, 2) - 1)

        def copy(k, source, target):
            if axis == "row":
                to = at_offset(from_far(div(k, X), Z), from_far(rem(k, X), X)), col
            else:
                to = row, rem(y + from_far(div(k, 2), Y), Y) * 2 + rem(core + 1 + k, 2)
            return pltpu.make_async_remote_copy(
                src_ref=source, dst_ref=target,
                send_sem=send_sem.at[phase], recv_sem=recv_sem.at[phase],
                device_id=to, device_id_type=MESH)

        others = got.at[phase, pl.ds(0, size - 1)]

        def start():
            def go(k, carry):
                copy(k, src, got.at[phase, me]).start()
                return carry
            lax.fori_loop(0, size - 1, go, 0)
            got[phase, me] = src[...]

        def result():
            copy(0, others, others).wait_recv()
            return jnp.sum(got[phase, pl.ds(0, size)], axis=0)

        def drain():
            copy(0, others, others).wait_send()

        return start, result, drain

    def whole(tile):
        return jnp.sum(tile, axis=(0, 1), keepdims=True)

    def sums(block):
        def rows_of(i, col_sum):
            at = part(i * LANES, LANES, LANES)
            row_sum = jnp.zeros((LANES, LANES), F32)
            col_sums = []
            for j in range(nc):
                square = block(at, j)
                row_sum += square
                col_sums.append(jnp.sum(square.reshape(LANES // 8, 8, LANES), axis=0))
            row_sums[at, :] = row_sum
            return col_sum + jnp.concatenate(col_sums, 1)

        return lax.fori_loop(0, nr, rows_of, jnp.zeros((8, cols), F32))

    def reduced(phase, col_sum, beside, meanwhile):
        col_sum = jnp.sum(col_sum, axis=0, keepdims=True)
        col_sums = [col_sum[:, j * LANES:(j + 1) * LANES] for j in range(nc)]
        tot_part[phase] = jnp.concatenate([functools.reduce(jnp.add, col_sums)] + beside, 1)
        by_tot = exchange(phase, tot_part.at[phase], tot_got, "row", tot_send, tot_recv)
        by_tot[0]()
        for j in range(nc):
            col_part[phase, j:j + 1, :] = col_sums[j]
        by_col = exchange(phase, col_part.at[phase], col_got, "row", col_send, col_recv)
        by_row = exchange(phase, row_part.at[phase], row_got, "col", row_send, row_recv)
        by_col[0]()
        for i in range(nr):
            turned = row_sums[i * LANES:(i + 1) * LANES, :].T
            row_part[phase, i:i + 1, :] = jnp.sum(turned, axis=0, keepdims=True)
        by_row[0]()
        meanwhile()
        tot_rows = by_tot[1]()
        all_part[phase] = tot_rows[:, :LANES]
        by_all = exchange(phase, all_part.at[phase], all_got, "col", all_send, all_recv)
        by_all[0]()
        col_all = by_col[1]()
        row_all = by_row[1]()
        for one in (by_tot, by_col, by_row):
            one[2]()
        total = whole(by_all[1]())

        def drain():
            by_all[2]()
        return row_all, col_all, total, tot_rows, drain

    def down_rows(factors):
        for i in range(nr):
            row_scale[i * LANES:(i + 1) * LANES, :] = jnp.broadcast_to(factors[i:i + 1, :], (LANES, LANES)).T

    col_part[...] = jnp.zeros_like(col_part)
    row_part[...] = jnp.zeros_like(row_part)

    def squared(at, j):
        g = G[at, j * LANES:(j + 1) * LANES]
        return g * g

    def gather_drain():
        for lane, (axis, sign) in enumerate(ring_to):
            gone = sum(extent(m)[1] for m in sent if m[:2] == (axis, sign))
            gone = B.at[pl.ds(0, gone)]
            pltpu.make_async_remote_copy(
                src_ref=gone, dst_ref=gone, send_sem=ring_send.at[lane], recv_sem=ring_recv.at[lane, 0],
                device_id=(ring_to[axis, sign], col), device_id_type=MESH).wait_send()
        gone = A.at[pl.ds(0, 7 * shard)]
        pltpu.make_async_remote_copy(
            src_ref=gone, dst_ref=gone, send_sem=act_send.at[0], recv_sem=act_recv.at[0],
            device_id=(row, twin), device_id_type=MESH).wait_send()
        strip(row).wait_send()

    col_sum = sums(squared)
    states_sums = [jnp.sum(states[k], axis=0, keepdims=True) for k in (0, 2)]
    row_all, col_all, total, tot_rows, drain0 = reduced(0, col_sum, states_sums, gather_drain)
    row_state_sum, row_conf_sum = whole(tot_rows[:, LANES:2 * LANES]), whole(tot_rows[:, 2 * LANES:])
    spread = jnp.minimum(1.0, (full_rows * full_cols) / (total + 1e-06))
    keep, fresh = second_decay, 1.0 - second_decay
    row_new = keep * states[0] + fresh * (spread * row_all * (1.0 / full_cols) + tiny_moment)
    col_new = keep * states[1] + fresh * (spread * col_all * (1.0 / full_rows) + tiny_moment)
    row_mean = keep * (row_state_sum * (1.0 / full_rows)) + fresh * (
        spread * total * (1.0 / (full_rows * full_cols)) + tiny_moment)
    down_rows(lax.rsqrt(row_new))
    packed[0] = row_new
    packed[1] = col_new
    col_scale = lax.rsqrt(col_new) * jnp.sqrt(spread * row_mean)

    def strays(at, j):
        here = (at, slice(j * LANES, (j + 1) * LANES))
        direction = G[here] * row_scale[at, :] * col_scale[j:j + 1, :]
        stray = direction - M[here]
        M[here] = M[here] + (1.0 - first_decay) * stray
        return stray * stray

    col_sum = sums(strays)
    row_all, col_all, total, _, drain1 = reduced(1, col_sum, [jnp.zeros((1, 2 * LANES), F32)], drain0)
    share = first_decay * first_decay
    row_conf_new = keep * states[2] + fresh * (row_all * (share / full_cols) + tiny_confidence)
    col_conf_new = keep * states[3] + fresh * (col_all * (share / full_rows) + tiny_confidence)
    conf_mean = keep * (row_conf_sum * (1.0 / full_rows)) + fresh * (
        total * (share / (full_rows * full_cols)) + tiny_confidence)
    packed[2] = row_conf_new
    packed[3] = col_conf_new
    packed[4] = lax.rsqrt(row_conf_new)
    packed[5] = lax.rsqrt(col_conf_new) * jnp.sqrt(conf_mean)
    drain1()


def finish(M, packed, moment_out, update_out, row_out, col_out, row_conf_out, col_conf_out, U, sem, block_sem):
    rows, cols = U.shape
    nr, nc = rows // LANES, cols // LANES
    stores = [pltpu.make_async_copy(M, moment_out, sem.at[0])]
    for k, (out, n) in enumerate(((row_out, nr), (col_out, nc), (row_conf_out, nr), (col_conf_out, nc))):
        stores.append(pltpu.make_async_copy(packed.at[k, pl.ds(0, n)], out, sem.at[1 + k]))
    for store in stores:
        store.start()

    def block_store(i):
        at = pl.ds(pl.multiple_of(i * LANES, LANES), LANES)
        return pltpu.make_async_copy(U.at[at], update_out.at[at], block_sem.at[i])

    def scale_block(i, carry):
        at = pl.ds(pl.multiple_of(i * LANES, LANES), LANES)
        scale = jnp.broadcast_to(packed[4, pl.ds(i, 1), :], (LANES, LANES)).T
        for j in range(nc):
            here = (at, slice(j * LANES, (j + 1) * LANES))
            U[here] = M[here] * scale * packed[5, j:j + 1, :]
        block_store(i).start()
        return carry

    def wait_block(i, carry):
        block_store(i).wait()
        return carry

    lax.fori_loop(0, nr, scale_block, 0)
    lax.fori_loop(0, nr, wait_block, 0)
    for store in stores:
        store.wait()


def on_device(acts, out_grads, moment, row_state, col_state, row_conf, col_conf):
    R, C = lax.axis_size("row"), lax.axis_size("col")
    rows, cols = moment.shape
    nr, nc = rows // LANES, cols // LANES
    dma = pltpu.SemaphoreType.DMA
    big = jax.ShapeDtypeStruct((rows, cols), F32)
    by_row, by_col = (jax.ShapeDtypeStruct((n, LANES), F32) for n in (nr, nc))
    in_hbm = pl.BlockSpec(memory_space=pltpu.HBM)
    in_vmem = pl.BlockSpec(memory_space=pltpu.VMEM)
    tokens = R * out_grads.shape[0]
    moment_new, packed = pl.pallas_call(
        functools.partial(kernel, R, C),
        out_shape=(pltpu.VMEM((rows, cols), F32), pltpu.VMEM((6, 8, LANES), F32)),
        in_specs=[in_hbm] * 7,
        out_specs=(in_vmem,) * 2,
        scratch_shapes=[
            pltpu.VMEM((tokens, rows), acts.dtype),
            pltpu.VMEM((tokens, cols), out_grads.dtype),
            pltpu.VMEM((rows, cols), F32),
            pltpu.VMEM((4, 8, LANES), F32),
            pltpu.VMEM((rows, LANES), F32),
            pltpu.VMEM((rows, LANES), F32),
            pltpu.VMEM((2, 8, LANES), F32),
            pltpu.VMEM((2, C, 8, LANES), F32),
            pltpu.VMEM((2, 8, LANES), F32),
            pltpu.VMEM((2, R, 8, LANES), F32),
            pltpu.VMEM((2, 1, 3 * LANES), F32),
            pltpu.VMEM((2, R, 1, 3 * LANES), F32),
            pltpu.VMEM((2, 1, LANES), F32),
            pltpu.VMEM((2, C, 1, LANES), F32),
            dma((4,)), dma((4, 20)), dma((2,)), dma((12,)), dma((7,)),
            dma((2,)), dma((2,)), dma((2,)), dma((2,)), dma((2,)), dma((2,)), dma((2,)), dma((2,)),
        ],
        compiler_params=pltpu.CompilerParams(
            collective_id=0, has_side_effects=True, vmem_limit_bytes=40 * 2**20),
        cost_estimate=pl.CostEstimate(
            flops=2 * tokens * rows * cols, transcendentals=0, bytes_accessed=30 * 2**20),
        name="came_step",
    )(*(pltpu.with_memory_space_constraint(v, pltpu.HBM) for v in (
        acts, out_grads, moment, row_state.reshape(nr, LANES), col_state.reshape(nc, LANES),
        row_conf.reshape(nr, LANES), col_conf.reshape(nc, LANES))))
    outs = pl.pallas_call(
        finish,
        out_shape=(big, big, by_row, by_col, by_row, by_col),
        in_specs=[in_vmem] * 2,
        out_specs=(in_hbm,) * 6,
        scratch_shapes=[pltpu.VMEM((rows, cols), F32), dma((5,)), dma((nr,))],
        compiler_params=pltpu.CompilerParams(vmem_limit_bytes=16 * 2**20),
        cost_estimate=pl.CostEstimate(
            flops=2 * rows * cols, transcendentals=0, bytes_accessed=12 * rows * cols),
        name="finish",
    )(moment_new, packed)
    return outs[0], outs[1], *(out.reshape(-1) for out in outs[2:])


def solution(mesh):
    placed = (
        P("col", "row"),
        P("row", "col"),
        P("row", "col"),
        P("row"),
        P("col"),
        P("row"),
        P("col"),
    )
    return jax.shard_map(
        on_device,
        mesh=mesh,
        in_specs=placed,
        out_specs=(P("row", "col"), P("row", "col"), P("row"), P("col"), P("row"), P("col")),
        check_vma=False,
    )
```

```python
import functools

import jax
import jax.numpy as jnp
from jax import lax
from jax.experimental import pallas as pl
from jax.experimental.pallas import tpu as pltpu
from jax.sharding import PartitionSpec as P

MESH = pl.DeviceIdType.MESH
F32 = jnp.float32
STEP = 10
X = 4
LANES = 128

first_decay = 0.9
tiny_moment = 1e-30
tiny_confidence = 1e-16
second_decay = 1.0 - STEP ** (-0.8)


ORDER = (
    ("z", "Q", 0, 0), ("x", "P", 0, 0), ("x", "Q", 0, 0), ("z", "P", 0, 0), "own low",
    ("z", "P", 1, 0), ("x", "P", 0, 1), ("x", "Q", 1, 0), ("z", "Q", 0, 1), "own high",
    ("x", "Q", -1, 0), ("z", "P", -1, 0), ("x", "Q", 0, 1), "strip out", ("z", "P", 0, 1),
    ("z", "Q", 0, 2), ("x", "Q", 2, 0), ("x", "Q", 1, 1), "strip", ("z", "P", 2, 0), "near",
    ("z", "P", 1, 1), ("x", "Q", -2, 0), ("x", "Q", -1, 1), ("z", "Q", 0, 3), ("z", "P", -1, 1),
    ("x", "Q", 3, 0), ("z", "P", 2, 1), "cross",
    ("x", "Q", 2, 1), ("x", "Q", -3, 0), ("z", "P", 0, 2), ("z", "P", 1, 2), ("x", "Q", -2, 1),
    ("z", "P", -1, 2), ("x", "Q", 4, 0), "far", ("z", "P", 2, 2), ("x", "Q", 3, 1), "all",
)
FOURS_ORDER = (
    (), (("z", "P", 0, 3),), (), (("x", "Q", -3, 1), ("z", "P", 1, 3)), (), (("z", "P", -1, 3),))
TWOS_ORDER = ((), (("x", "Q", 4, 1), ("z", "P", 2, 3)), (), ())
HOPS = {"z": 4, "x": 2}


def kernel(R, C, acts, grads, moment, row_state, col_state, row_conf, col_conf, M, packed,
           A, B, G, states, row_sums, row_scale, row_part, row_got, col_part, x_got, z_part, col_got,
           tot_part, tot_got, all_part, all_got,
           ring_send, ring_recv, act_send, act_recv, load_sem,
           row_send, row_recv, x_send, x_recv, col_send, col_recv, tot_send, tot_recv, all_send, all_recv, known):
    Z, Y = R // X, C // 2
    row, col = lax.axis_index("row"), lax.axis_index("col")
    div, rem = lax.div, lax.rem
    z, x, y, core = div(row, X), rem(row, X), div(col, 2), rem(col, 2)
    tb, shard = grads.shape[0], acts.shape[0]
    hs = shard // 2
    rows, cols = G.shape
    nr, nc = rows // LANES, cols // LANES
    full_rows, full_cols = rows * R, cols * C
    p_rows = 3 * tb // 8

    def at_offset(dz, dx):
        return rem(z + dz + Z, Z) * X + rem(x + dx + X, X)

    across = at_offset(0, 2)


    def part(first, unit, size):
        return pl.ds(pl.multiple_of(first, unit), size)

    ring_to = {("z", s): at_offset(s, 0) for s in (1, -1)} | {("x", s): at_offset(0, s) for s in (1, -1)}
    up, down = rem(y + 1, Y) * 2 + core, rem(y + Y - 1, Y) * 2 + core
    far, twin = rem(y + 2, Y) * 2 + core, y * 2 + 1 - core

    def whole(tile):
        return jnp.sum(tile, axis=(0, 1), keepdims=True)

    def from_far(length):
        return sorted(range(length), key=lambda d: -min(d, length - d))

    def to_twin(go):
        go((row, twin))

    def to_x(go):
        for dx in from_far(X)[:-1]:
            go((at_offset(0, dx), col))

    def to_z(go):
        for dz in from_far(Z)[:-1]:
            go((at_offset(dz, 0), col))

    def to_col(go):
        for dy in from_far(Y):
            for dc in (1, 0):
                if dy or dc:
                    go((row, rem(y + dy, Y) * 2 + rem(core + dc, 2)))

    def to_chips(go):
        def plane(a, carry):
            dz = Z // 2 + div(a + 1, 2) * (2 * rem(a, 2) - 1)
            for dx in from_far(X):
                for dy in from_far(Y):
                    to = at_offset(dz, dx), rem(y + dy, Y) * 2 + core
                    if dx or dy:
                        go(to)
                    else:
                        pl.when(a < Z - 1)(functools.partial(go, to))
            return carry
        lax.fori_loop(0, Z, plane, 0)

    barrier = pltpu.get_barrier_semaphore()
    for r in ring_to.values():
        pl.semaphore_signal(barrier, inc=1, device_id=(r, col), device_id_type=MESH)
    for c in (up, down, twin):
        pl.semaphore_signal(barrier, inc=1, device_id=(row, c), device_id_type=MESH)

    loads = [
        pltpu.make_async_copy(grads, B.at[part(row * tb, tb, tb)], load_sem.at[0]),
        pltpu.make_async_copy(acts, A.at[part(col * shard, shard, shard)], load_sem.at[1]),
        pltpu.make_async_copy(moment, M, load_sem.at[2]),
        pltpu.make_async_copy(row_state, states.at[0, pl.ds(0, nr)], load_sem.at[3]),
        pltpu.make_async_copy(col_state, states.at[1, pl.ds(0, nc)], load_sem.at[4]),
        pltpu.make_async_copy(row_conf, states.at[2, pl.ds(0, nr)], load_sem.at[5]),
        pltpu.make_async_copy(col_conf, states.at[3, pl.ds(0, nc)], load_sem.at[6]),
    ]
    states[...] = jnp.zeros_like(states)
    for load in loads:
        load.start()
    pl.semaphore_wait(barrier, 7)

    def extent(message):
        axis, sign, kind, off, hops = message
        first, size = (0, p_rows) if kind == "P" else (p_rows, tb - p_rows)
        if axis == "z" and kind == "P" and off == HOPS["x"]:
            size += 16
        if axis == "x" and kind == "Q" and hops == HOPS["x"] - 1:
            first, size = first + 16, size - 16
        if hops == HOPS[axis] - 1:
            low = (size // 2 + 15) // 16 * 16
            low = size - low if off % 2 else low
            return (first, low) if sign > 0 else (first + low, size - low)
        return first, size

    def placed(message, hops):
        axis, sign, _, off, _ = message
        dz, dx = (-sign * hops, off) if axis == "z" else (off, -sign * hops)
        first, size = extent(message)
        return B.at[part(at_offset(dz, dx) * tb + first, 16, size)]

    numbers = {}

    def ring(message, hops):
        axis, sign, _, off, made = message
        lane = 2 * (axis == "x") + (sign < 0)
        number = numbers.setdefault(message, sum(m[:2] == message[:2] for m in numbers))
        first, size = extent(message)
        there = placed(message, hops)
        return pltpu.make_async_remote_copy(
            src_ref=grads.at[pl.ds(first, size)] if made == 0 and off == 0 else there, dst_ref=there,
            send_sem=ring_send.at[lane], recv_sem=ring_recv.at[lane, number],
            device_id=(ring_to[axis, sign], col), device_id_type=MESH)

    def strip(owner):
        return pltpu.make_async_remote_copy(
            src_ref=grads.at[pl.ds(p_rows, 16)], dst_ref=B.at[part(owner * tb + p_rows, 16, 16)],
            send_sem=act_send.at[1], recv_sem=act_recv.at[11],
            device_id=(across, col), device_id_type=MESH)

    sent, landed = [], set()

    def await_messages(messages):
        for message in messages:
            if message not in landed:
                landed.add(message)
                ring(message, message[4] + 1).wait_recv()

    def brought(message):
        axis, sign, kind, off, hops = message
        if hops > 0:
            return [(axis, sign, kind, off, hops - 1)]
        if off == 0:
            return []
        other = "x" if axis == "z" else "z"
        last = HOPS[other] - 1
        if abs(off) == HOPS[other]:
            return [(other, 1, kind, 0, last), (other, -1, kind, 0, last)]
        return [(other, -1 if off > 0 else 1, kind, 0, abs(off) - 1)]

    def send(axis, kind, off, hops):
        mirrored = off if abs(off) == HOPS["x" if axis == "z" else "z"] else -off
        pair = [(axis, 1, kind, off, hops), (axis, -1, kind, mirrored, hops)]
        for message in pair:
            await_messages(brought(message))
            ring(message, hops).start()
            sent.append(message)

    def brings(message, dz):
        axis, sign, _, off, hops = message
        if axis == "x":
            return off == dz
        return dz == HOPS["z"] if hops == HOPS["z"] - 1 else dz == -sign * (hops + 1)

    def act(i, owner, first, size, to, src=None):
        there = A.at[part(owner * shard + first, hs, size)]
        return pltpu.make_async_remote_copy(
            src_ref=there if src is None else src, dst_ref=there,
            send_sem=act_send.at[0], recv_sem=act_recv.at[i],
            device_id=(row, to), device_id_type=MESH)

    low, high = acts.at[pl.ds(0, hs)], acts.at[pl.ds(hs, hs)]
    act_out = {
        0: act(0, col, 0, hs, up, low), 3: act(3, col, hs, hs, down, high),
        1: act(1, col, hs, hs, up, high), 4: act(4, col, 0, hs, down, low),
        6: act(6, col, 0, shard, twin, acts),
        2: act(2, down, 0, hs, up), 5: act(5, up, hs, hs, down),
        7: act(7, down, 0, shard, twin), 8: act(8, up, 0, shard, twin),
        9: act(9, far, 0, hs, twin), 10: act(10, far, hs, hs, twin),
    }
    swap = 1 - 2 * core
    act_in = {
        0: act(0, down, 0, hs, up), 1: act(1, down, hs, hs, up), 2: act(2, far, 0, hs, up),
        3: act(3, up, hs, hs, down), 4: act(4, up, 0, hs, down), 5: act(5, far, hs, hs, down),
        6: act(6, twin, 0, shard, twin), 7: act(7, down + swap, 0, shard, twin),
        8: act(8, up + swap, 0, shard, twin), 9: act(9, far + swap, 0, hs, twin),
        10: act(10, far + swap, hs, hs, twin),
    }
    act_steps = {
        "own low": ((), (0, 3, 6)), "own high": ((), (1, 4)), "near": ((0, 3), (2, 5)),
        "cross": ((1, 4), (7, 8)), "far": ((2, 5), (9, 10)), "all": ((6, 7, 8, 9, 10), ()),
        "strip": ((), ()), "strip out": ((), ()),
    }

    def fours(i):
        dz, odd = div(i + 1, 2) * (2 * rem(i, 2) - 1), div(i, 5)
        return (dz, 0), (dz, 1), (dz, 3), (dz - 6 * odd, 2 - 2 * odd)

    def twos(i):
        return (5 - 2 * rem(i, 2) + div(i, 3), 1 + div(i + 1, 2)), (5 - div(i + 2, 3), i - 1)

    def await_blocks(offsets):
        for dz, dx in offsets:
            dz, dx = (dz + Z // 2 - 1) % Z - Z // 2 + 1, (dx + 1) % X - 1
            await_messages([m for m in sent if brings(m, dz) and (
                m[3] == dx if m[0] == "z" else dx == -m[1] * (m[4] + 1) or (dx == 2 and m[4] == 1))])

    def add_products(blocks, order):
        def ahead(n):
            for message in order[n]:
                send(*message)
            await_blocks(static_blocks(blocks, n))

        def add(i, carry):
            for n in range(len(order)):
                pl.when(i == n)(functools.partial(ahead, n))
            tokens = [part(at_offset(dz, dx) * tb, tb, tb) for dz, dx in blocks(i)]
            G[...] += lax.dot_general(
                jnp.concatenate([A[t, :] for t in tokens], 0), jnp.concatenate([B[t, :] for t in tokens], 0),
                (((0,), (0,)), ((), ())), preferred_element_type=F32)
            return carry

        lax.fori_loop(0, len(order), add, 0)

    def static_blocks(blocks, n):
        if blocks is fours:
            dz, odd = (n + 1) // 2 * (2 * (n % 2) - 1), n // 5
            return (dz, 0), (dz, 1), (dz, 3), (dz - 6 * odd, 2 - 2 * odd)
        return (5 - 2 * (n % 2) + n // 3, 1 + (n + 1) // 2), (5 - (n + 2) // 3, n - 1)

    for entry in ORDER:
        if isinstance(entry, str):
            arrive, leave = act_steps[entry]
            for i in arrive:
                act_in[i].wait_recv()
            for i in leave:
                act_out[i].start()
            if entry == "strip out":
                await_messages([("x", s, "P", 0, 1) for s in (1, -1)])
                strip(row).start()
            if entry == "strip":
                strip(across).wait_recv()
            if entry == "own high":
                loads[0].wait()
                loads[1].wait()
                G[...] = jnp.zeros_like(G)
        else:
            send(*entry)
    to_z(lambda to: pl.semaphore_signal(known.at[0], inc=1, device_id=to, device_id_type=MESH))
    for load in loads[2:]:
        load.wait()
    col_part[...] = jnp.zeros_like(col_part)
    row_part[...] = jnp.zeros_like(row_part)
    lane_ids = lax.broadcasted_iota(jnp.int32, (1, LANES), 1)
    states_sums = [whole(states[k]) for k in (0, 2)]
    add_products(fours, FOURS_ORDER)
    pl.semaphore_wait(known.at[0], Z - 1)
    to_x(lambda to: pl.semaphore_signal(known.at[1], inc=1, device_id=to, device_id_type=MESH))
    add_products(twos, TWOS_ORDER)
    pl.semaphore_wait(known.at[1], X - 1)
    def exchange(phase, src, got, slot, to_each, sems):
        send_sem, recv_sem = sems

        def copy(source, target, to):
            return pltpu.make_async_remote_copy(
                src_ref=source, dst_ref=target,
                send_sem=send_sem.at[phase], recv_sem=recv_sem.at[phase],
                device_id=to, device_id_type=MESH)

        others = got.at[phase, pl.ds(0, got.shape[1] - 1)]

        def start():
            to_each(lambda to: copy(src, got.at[phase, slot], to).start())
            got[phase, slot] = src[...]

        def result():
            copy(others, others, (row, twin)).wait_recv()
            return jnp.sum(got[phase], axis=0)

        def drain():
            copy(others, others, (row, twin)).wait_send()

        return start, result, drain

    def sums(block):
        def rows_of(i, col_sum):
            at = part(i * LANES, LANES, LANES)
            row_sum = jnp.zeros((LANES, LANES), F32)
            col_sums = []
            for j in range(nc):
                square = block(at, j)
                row_sum += square
                col_sums.append(jnp.sum(square.reshape(LANES // 8, 8, LANES), axis=0))
            row_sums[at, :] = row_sum
            return col_sum + jnp.concatenate(col_sums, 1)

        return lax.fori_loop(0, nr, rows_of, jnp.zeros((8, cols), F32))

    def reduced(phase, col_sum, beside, meanwhile):
        col_sum = jnp.sum(col_sum, axis=0, keepdims=True)
        col_sums = [col_sum[:, j * LANES:(j + 1) * LANES] for j in range(nc)]
        values = whole(functools.reduce(jnp.add, col_sums))
        for lane, value in enumerate(beside):
            values = jnp.where(lane_ids == lane + 1, value, values)
        tot_part[phase] = jnp.broadcast_to(values, (1, LANES))
        by_twin = exchange(phase, tot_part.at[phase], tot_got, core, to_twin, (tot_send, tot_recv))
        by_twin[0]()
        for j in range(nc):
            col_part[phase, j:j + 1, :] = col_sums[j]
        by_x = exchange(phase, col_part.at[phase], x_got, x, to_x, (x_send, x_recv))
        by_x[0]()
        for i in range(nr):
            turned = row_sums[i * LANES:(i + 1) * LANES, :].T
            row_part[phase, i:i + 1, :] = jnp.sum(turned, axis=0, keepdims=True)
        by_row = exchange(phase, row_part.at[phase], row_got, col, to_col, (row_send, row_recv))
        by_row[0]()
        all_part[phase] = by_twin[1]()
        by_all = exchange(phase, all_part.at[phase], all_got, row * Y + y, to_chips, (all_send, all_recv))
        by_all[0]()
        z_part[phase] = by_x[1]()
        by_z = exchange(phase, z_part.at[phase], col_got, z, to_z, (col_send, col_recv))
        by_z[0]()
        meanwhile()
        row_all = by_row[1]()
        col_all = by_z[1]()
        for one in (by_twin, by_x, by_row, by_z):
            one[2]()
        totals = by_all[1]()
        return row_all, col_all, totals, by_all[2]

    def down_rows(factors):
        for i in range(nr):
            row_scale[i * LANES:(i + 1) * LANES, :] = jnp.broadcast_to(factors[i:i + 1, :], (LANES, LANES)).T

    def squared(at, j):
        g = G[at, j * LANES:(j + 1) * LANES]
        return g * g

    def gather_drain():
        for lane, (axis, sign) in enumerate(ring_to):
            gone = sum(extent(m)[1] for m in sent if m[:2] == (axis, sign))
            gone = B.at[pl.ds(0, gone)]
            pltpu.make_async_remote_copy(
                src_ref=gone, dst_ref=gone, send_sem=ring_send.at[lane], recv_sem=ring_recv.at[lane, 0],
                device_id=(ring_to[axis, sign], col), device_id_type=MESH).wait_send()
        gone = A.at[pl.ds(0, 7 * shard)]
        pltpu.make_async_remote_copy(
            src_ref=gone, dst_ref=gone, send_sem=act_send.at[0], recv_sem=act_recv.at[0],
            device_id=(row, twin), device_id_type=MESH).wait_send()
        strip(row).wait_send()

    col_sum = sums(squared)
    row_all, col_all, totals, drain0 = reduced(0, col_sum, states_sums, gather_drain)
    total, row_state_sum, row_conf_sum = totals[:, 0:1], totals[:, 1:2] * (1.0 / C), totals[:, 2:3] * (1.0 / C)
    spread = jnp.minimum(1.0, (full_rows * full_cols) / (total + 1e-06))
    keep, fresh = second_decay, 1.0 - second_decay
    row_new = keep * states[0] + fresh * (spread * row_all * (1.0 / full_cols) + tiny_moment)
    col_new = keep * states[1] + fresh * (spread * col_all * (1.0 / full_rows) + tiny_moment)
    row_mean = keep * (row_state_sum * (1.0 / full_rows)) + fresh * (
        spread * total * (1.0 / (full_rows * full_cols)) + tiny_moment)
    down_rows(lax.rsqrt(row_new))
    packed[0] = row_new
    packed[1] = col_new
    col_scale = lax.rsqrt(col_new) * jnp.sqrt(spread * row_mean)

    def strays(at, j):
        here = (at, slice(j * LANES, (j + 1) * LANES))
        direction = G[here] * row_scale[at, :] * col_scale[j:j + 1, :]
        stray = direction - M[here]
        M[here] = M[here] + (1.0 - first_decay) * stray
        return stray * stray

    col_sum = sums(strays)
    row_all, col_all, totals, drain1 = reduced(1, col_sum, [], drain0)
    total = totals[:, 0:1]
    share = first_decay * first_decay
    row_conf_new = keep * states[2] + fresh * (row_all * (share / full_cols) + tiny_confidence)
    col_conf_new = keep * states[3] + fresh * (col_all * (share / full_rows) + tiny_confidence)
    conf_mean = keep * (row_conf_sum * (1.0 / full_rows)) + fresh * (
        total * (share / (full_rows * full_cols)) + tiny_confidence)
    packed[2] = row_conf_new
    packed[3] = col_conf_new
    packed[4] = lax.rsqrt(row_conf_new)
    packed[5] = lax.rsqrt(col_conf_new) * jnp.sqrt(conf_mean)
    drain1()


def finish(M, packed, moment_out, update_out, row_out, col_out, row_conf_out, col_conf_out, U, sem, block_sem):
    rows, cols = U.shape
    nr, nc = rows // LANES, cols // LANES
    stores = [pltpu.make_async_copy(M, moment_out, sem.at[0])]
    for k, (out, n) in enumerate(((row_out, nr), (col_out, nc), (row_conf_out, nr), (col_conf_out, nc))):
        stores.append(pltpu.make_async_copy(packed.at[k, pl.ds(0, n)], out, sem.at[1 + k]))
    for store in stores:
        store.start()

    def block_store(i):
        at = pl.ds(pl.multiple_of(i * LANES, LANES), LANES)
        return pltpu.make_async_copy(U.at[at], update_out.at[at], block_sem.at[i])

    def scale_block(i, carry):
        at = pl.ds(pl.multiple_of(i * LANES, LANES), LANES)
        scale = jnp.broadcast_to(packed[4, pl.ds(i, 1), :], (LANES, LANES)).T
        for j in range(nc):
            here = (at, slice(j * LANES, (j + 1) * LANES))
            U[here] = M[here] * scale * packed[5, j:j + 1, :]
        block_store(i).start()
        return carry

    def wait_block(i, carry):
        block_store(i).wait()
        return carry

    lax.fori_loop(0, nr, scale_block, 0)
    lax.fori_loop(0, nr, wait_block, 0)
    for store in stores:
        store.wait()


def on_device(acts, out_grads, moment, row_state, col_state, row_conf, col_conf):
    R, C = lax.axis_size("row"), lax.axis_size("col")
    rows, cols = moment.shape
    nr, nc = rows // LANES, cols // LANES
    dma = pltpu.SemaphoreType.DMA
    big = jax.ShapeDtypeStruct((rows, cols), F32)
    by_row, by_col = (jax.ShapeDtypeStruct((n, LANES), F32) for n in (nr, nc))
    in_hbm = pl.BlockSpec(memory_space=pltpu.HBM)
    in_vmem = pl.BlockSpec(memory_space=pltpu.VMEM)
    tokens = R * out_grads.shape[0]
    moment_new, packed = pl.pallas_call(
        functools.partial(kernel, R, C),
        out_shape=(pltpu.VMEM((rows, cols), F32), pltpu.VMEM((6, 8, LANES), F32)),
        in_specs=[in_hbm] * 7,
        out_specs=(in_vmem,) * 2,
        scratch_shapes=[
            pltpu.VMEM((tokens, rows), acts.dtype),
            pltpu.VMEM((tokens, cols), out_grads.dtype),
            pltpu.VMEM((rows, cols), F32),
            pltpu.VMEM((4, 8, LANES), F32),
            pltpu.VMEM((rows, LANES), F32),
            pltpu.VMEM((rows, LANES), F32),
            pltpu.VMEM((2, 8, LANES), F32),
            pltpu.VMEM((2, C, 8, LANES), F32),
            pltpu.VMEM((2, 8, LANES), F32),
            pltpu.VMEM((2, X, 8, LANES), F32),
            pltpu.VMEM((2, 8, LANES), F32),
            pltpu.VMEM((2, R // X, 8, LANES), F32),
            pltpu.VMEM((2, 1, LANES), F32),
            pltpu.VMEM((2, 2, 1, LANES), F32),
            pltpu.VMEM((2, 1, LANES), F32),
            pltpu.VMEM((2, R * C // 2, 1, LANES), F32),
            dma((4,)), dma((4, 20)), dma((2,)), dma((12,)), dma((7,)),
            *[dma((2,))] * 10, pltpu.SemaphoreType.REGULAR((2,)),
        ],
        compiler_params=pltpu.CompilerParams(
            collective_id=0, has_side_effects=True, vmem_limit_bytes=40 * 2**20),
        cost_estimate=pl.CostEstimate(
            flops=2 * tokens * rows * cols, transcendentals=0, bytes_accessed=30 * 2**20),
        name="came_step",
    )(*(pltpu.with_memory_space_constraint(v, pltpu.HBM) for v in (
        acts, out_grads, moment, row_state.reshape(nr, LANES), col_state.reshape(nc, LANES),
        row_conf.reshape(nr, LANES), col_conf.reshape(nc, LANES))))
    outs = pl.pallas_call(
        finish,
        out_shape=(big, big, by_row, by_col, by_row, by_col),
        in_specs=[in_vmem] * 2,
        out_specs=(in_hbm,) * 6,
        scratch_shapes=[pltpu.VMEM((rows, cols), F32), dma((5,)), dma((nr,))],
        compiler_params=pltpu.CompilerParams(vmem_limit_bytes=16 * 2**20),
        cost_estimate=pl.CostEstimate(
            flops=2 * rows * cols, transcendentals=0, bytes_accessed=12 * rows * cols),
        name="finish",
    )(moment_new, packed)
    return outs[0], outs[1], *(out.reshape(-1) for out in outs[2:])


def solution(mesh):
    placed = (
        P("col", "row"),
        P("row", "col"),
        P("row", "col"),
        P("row"),
        P("col"),
        P("row"),
        P("col"),
    )
    return jax.shard_map(
        on_device,
        mesh=mesh,
        in_specs=placed,
        out_specs=(P("row", "col"), P("row", "col"), P("row"), P("col"), P("row"), P("col")),
        check_vma=False,
    )
```

```python
import functools

import jax
import jax.numpy as jnp
from jax import lax
from jax.experimental import pallas as pl
from jax.experimental.pallas import tpu as pltpu
from jax.sharding import PartitionSpec as P

MESH = pl.DeviceIdType.MESH
F32 = jnp.float32
STEP = 10
X = 4
LANES = 128

first_decay = 0.9
tiny_moment = 1e-30
tiny_confidence = 1e-16
second_decay = 1.0 - STEP ** (-0.8)


ORDER = (
    ("z", "Q", 0, 0), ("x", "P", 0, 0), ("x", "Q", 0, 0), ("z", "P", 0, 0), "own low",
    ("z", "P", 1, 0), ("x", "P", 0, 1), ("x", "Q", 1, 0), ("z", "Q", 0, 1), "own high",
    ("x", "Q", -1, 0), ("z", "P", -1, 0), ("x", "Q", 0, 1), "strip out", ("z", "P", 0, 1),
    ("z", "Q", 0, 2), ("x", "Q", 2, 0), ("x", "Q", 1, 1), "strip", ("z", "P", 2, 0), "near",
    ("z", "P", 1, 1), ("x", "Q", -2, 0), ("x", "Q", -1, 1), ("z", "Q", 0, 3), ("z", "P", -1, 1),
    ("x", "Q", 3, 0), ("z", "P", 2, 1), "cross",
    ("x", "Q", 2, 1), ("x", "Q", -3, 0), ("z", "P", 0, 2), ("z", "P", 1, 2), ("x", "Q", -2, 1),
    ("z", "P", -1, 2), ("x", "Q", 4, 0), "far", ("z", "P", 2, 2), ("x", "Q", 3, 1), "all",
)
FOURS_ORDER = (
    (), (("z", "P", 0, 3),), (), (("x", "Q", -3, 1), ("z", "P", 1, 3)), (), (("z", "P", -1, 3),))
TWOS_ORDER = ((("x", "Q", 4, 1), ("z", "P", 2, 3)), (), (), ())
HOPS = {"z": 4, "x": 2}


def kernel(R, C, acts, grads, moment, row_state, col_state, row_conf, col_conf, M, packed,
           A, B, G, states, row_sums, row_scale, row_part, row_got, col_part, x_got, z_part, col_got,
           tot_part, tot_got, all_part, all_got,
           ring_send, ring_recv, act_send, act_recv, load_sem,
           row_send, row_recv, x_send, x_recv, col_send, col_recv, tot_send, tot_recv, all_send, all_recv, known):
    Z, Y = R // X, C // 2
    row, col = lax.axis_index("row"), lax.axis_index("col")
    div, rem = lax.div, lax.rem
    z, x, y, core = div(row, X), rem(row, X), div(col, 2), rem(col, 2)
    tb, shard = grads.shape[0], acts.shape[0]
    hs = shard // 2
    rows, cols = G.shape
    nr, nc = rows // LANES, cols // LANES
    full_rows, full_cols = rows * R, cols * C
    p_rows = 3 * tb // 8

    def at_offset(dz, dx):
        return rem(z + dz + Z, Z) * X + rem(x + dx + X, X)

    across = at_offset(0, 2)


    def part(first, unit, size):
        return pl.ds(pl.multiple_of(first, unit), size)

    ring_to = {("z", s): at_offset(s, 0) for s in (1, -1)} | {("x", s): at_offset(0, s) for s in (1, -1)}
    up, down = rem(y + 1, Y) * 2 + core, rem(y + Y - 1, Y) * 2 + core
    far, twin = rem(y + 2, Y) * 2 + core, y * 2 + 1 - core

    def whole(tile):
        return jnp.sum(tile, axis=(0, 1), keepdims=True)

    def from_far(length):
        return sorted(range(length), key=lambda d: -min(d, length - d))

    def to_twin(go):
        go((row, twin))

    def to_x(go):
        for dx in from_far(X)[:-1]:
            go((at_offset(0, dx), col))

    def to_z(go):
        for dz in from_far(Z)[:-1]:
            go((at_offset(dz, 0), col))

    def to_col(go):
        for dy in from_far(Y):
            for dc in (1, 0):
                if dy or dc:
                    go((row, rem(y + dy, Y) * 2 + rem(core + dc, 2)))

    def to_chips(go):
        def plane(a, carry):
            dz = Z // 2 + div(a + 1, 2) * (2 * rem(a, 2) - 1)
            for dx in from_far(X):
                for dy in from_far(Y):
                    to = at_offset(dz, dx), rem(y + dy, Y) * 2 + core
                    if dx or dy:
                        go(to)
                    else:
                        pl.when(a < Z - 1)(functools.partial(go, to))
            return carry
        lax.fori_loop(0, Z, plane, 0)

    barrier = pltpu.get_barrier_semaphore()
    for r in ring_to.values():
        pl.semaphore_signal(barrier, inc=1, device_id=(r, col), device_id_type=MESH)
    for c in (up, down, twin):
        pl.semaphore_signal(barrier, inc=1, device_id=(row, c), device_id_type=MESH)

    loads = [
        pltpu.make_async_copy(grads, B.at[part(row * tb, tb, tb)], load_sem.at[0]),
        pltpu.make_async_copy(acts, A.at[part(col * shard, shard, shard)], load_sem.at[1]),
        pltpu.make_async_copy(moment, M, load_sem.at[2]),
        pltpu.make_async_copy(row_state, states.at[0, pl.ds(0, nr)], load_sem.at[3]),
        pltpu.make_async_copy(col_state, states.at[1, pl.ds(0, nc)], load_sem.at[4]),
        pltpu.make_async_copy(row_conf, states.at[2, pl.ds(0, nr)], load_sem.at[5]),
        pltpu.make_async_copy(col_conf, states.at[3, pl.ds(0, nc)], load_sem.at[6]),
    ]
    states[...] = jnp.zeros_like(states)
    for load in loads:
        load.start()
    pl.semaphore_wait(barrier, 7)

    def extent(message):
        axis, sign, kind, off, hops = message
        first, size = (0, p_rows) if kind == "P" else (p_rows, tb - p_rows)
        if axis == "z" and kind == "P" and off == HOPS["x"]:
            size += 16
        if axis == "x" and kind == "Q" and hops == HOPS["x"] - 1:
            first, size = first + 16, size - 16
        if hops == HOPS[axis] - 1:
            low = (size // 2 + 15) // 16 * 16
            low = size - low if off % 2 else low
            return (first, low) if sign > 0 else (first + low, size - low)
        return first, size

    def placed(message, hops):
        axis, sign, _, off, _ = message
        dz, dx = (-sign * hops, off) if axis == "z" else (off, -sign * hops)
        first, size = extent(message)
        return B.at[part(at_offset(dz, dx) * tb + first, 16, size)]

    numbers = {}

    def ring(message, hops):
        axis, sign, _, off, made = message
        lane = 2 * (axis == "x") + (sign < 0)
        number = numbers.setdefault(message, sum(m[:2] == message[:2] for m in numbers))
        first, size = extent(message)
        there = placed(message, hops)
        return pltpu.make_async_remote_copy(
            src_ref=grads.at[pl.ds(first, size)] if made == 0 and off == 0 else there, dst_ref=there,
            send_sem=ring_send.at[lane], recv_sem=ring_recv.at[lane, number],
            device_id=(ring_to[axis, sign], col), device_id_type=MESH)

    def strip(owner):
        return pltpu.make_async_remote_copy(
            src_ref=grads.at[pl.ds(p_rows, 16)], dst_ref=B.at[part(owner * tb + p_rows, 16, 16)],
            send_sem=act_send.at[1], recv_sem=act_recv.at[11],
            device_id=(across, col), device_id_type=MESH)

    sent, landed = [], set()

    def await_messages(messages):
        for message in messages:
            if message not in landed:
                landed.add(message)
                ring(message, message[4] + 1).wait_recv()

    def brought(message):
        axis, sign, kind, off, hops = message
        if hops > 0:
            return [(axis, sign, kind, off, hops - 1)]
        if off == 0:
            return []
        other = "x" if axis == "z" else "z"
        last = HOPS[other] - 1
        if abs(off) == HOPS[other]:
            return [(other, 1, kind, 0, last), (other, -1, kind, 0, last)]
        return [(other, -1 if off > 0 else 1, kind, 0, abs(off) - 1)]

    def send(axis, kind, off, hops):
        mirrored = off if abs(off) == HOPS["x" if axis == "z" else "z"] else -off
        pair = [(axis, 1, kind, off, hops), (axis, -1, kind, mirrored, hops)]
        for message in pair:
            await_messages(brought(message))
            ring(message, hops).start()
            sent.append(message)

    def brings(message, dz):
        axis, sign, _, off, hops = message
        if axis == "x":
            return off == dz
        return dz == HOPS["z"] if hops == HOPS["z"] - 1 else dz == -sign * (hops + 1)

    def act(i, owner, first, size, to, src=None):
        there = A.at[part(owner * shard + first, hs, size)]
        return pltpu.make_async_remote_copy(
            src_ref=there if src is None else src, dst_ref=there,
            send_sem=act_send.at[0], recv_sem=act_recv.at[i],
            device_id=(row, to), device_id_type=MESH)

    low, high = acts.at[pl.ds(0, hs)], acts.at[pl.ds(hs, hs)]
    act_out = {
        0: act(0, col, 0, hs, up, low), 3: act(3, col, hs, hs, down, high),
        1: act(1, col, hs, hs, up, high), 4: act(4, col, 0, hs, down, low),
        6: act(6, col, 0, shard, twin, acts),
        2: act(2, down, 0, hs, up), 5: act(5, up, hs, hs, down),
        7: act(7, down, 0, shard, twin), 8: act(8, up, 0, shard, twin),
        9: act(9, far, 0, hs, twin), 10: act(10, far, hs, hs, twin),
    }
    swap = 1 - 2 * core
    act_in = {
        0: act(0, down, 0, hs, up), 1: act(1, down, hs, hs, up), 2: act(2, far, 0, hs, up),
        3: act(3, up, hs, hs, down), 4: act(4, up, 0, hs, down), 5: act(5, far, hs, hs, down),
        6: act(6, twin, 0, shard, twin), 7: act(7, down + swap, 0, shard, twin),
        8: act(8, up + swap, 0, shard, twin), 9: act(9, far + swap, 0, hs, twin),
        10: act(10, far + swap, hs, hs, twin),
    }
    act_steps = {
        "own low": ((), (0, 3, 6)), "own high": ((), (1, 4)), "near": ((0, 3), (2, 5)),
        "cross": ((1, 4), (7, 8)), "far": ((2, 5), (9, 10)), "all": ((6, 7, 8, 9, 10), ()),
        "strip": ((), ()), "strip out": ((), ()),
    }

    def fours(i):
        dz, odd = div(i + 1, 2) * (2 * rem(i, 2) - 1), div(i, 5)
        return (dz, 0), (dz, 1), (dz, 3), (dz - 6 * odd, 2 - 2 * odd)

    def twos(i):
        return (5 - 2 * rem(i, 2) + div(i, 3), 1 + div(i + 1, 2)), (5 - div(i + 2, 3), i - 1)

    def await_blocks(offsets):
        for dz, dx in offsets:
            dz, dx = (dz + Z // 2 - 1) % Z - Z // 2 + 1, (dx + 1) % X - 1
            await_messages([m for m in sent if brings(m, dz) and (
                m[3] == dx if m[0] == "z" else dx == -m[1] * (m[4] + 1) or (dx == 2 and m[4] == 1))])

    def add_products(blocks, order):
        def ahead(n):
            for message in order[n]:
                send(*message)
            await_blocks(static_blocks(blocks, n))

        def add(i, carry):
            for n in range(len(order)):
                pl.when(i == n)(functools.partial(ahead, n))
            tokens = [part(at_offset(dz, dx) * tb, tb, tb) for dz, dx in blocks(i)]
            G[...] += lax.dot_general(
                jnp.concatenate([A[t, :] for t in tokens], 0), jnp.concatenate([B[t, :] for t in tokens], 0),
                (((0,), (0,)), ((), ())), preferred_element_type=F32)
            return carry

        lax.fori_loop(0, len(order), add, 0)

    def static_blocks(blocks, n):
        if blocks is fours:
            dz, odd = (n + 1) // 2 * (2 * (n % 2) - 1), n // 5
            return (dz, 0), (dz, 1), (dz, 3), (dz - 6 * odd, 2 - 2 * odd)
        return (5 - 2 * (n % 2) + n // 3, 1 + (n + 1) // 2), (5 - (n + 2) // 3, n - 1)

    for entry in ORDER:
        if isinstance(entry, str):
            arrive, leave = act_steps[entry]
            for i in arrive:
                act_in[i].wait_recv()
            for i in leave:
                act_out[i].start()
            if entry == "strip out":
                await_messages([("x", s, "P", 0, 1) for s in (1, -1)])
                strip(row).start()
            if entry == "strip":
                strip(across).wait_recv()
            if entry == "own high":
                loads[0].wait()
                loads[1].wait()
                G[...] = jnp.zeros_like(G)
        else:
            send(*entry)
    to_z(lambda to: pl.semaphore_signal(known.at[0], inc=1, device_id=to, device_id_type=MESH))
    for load in loads[2:]:
        load.wait()
    col_part[...] = jnp.zeros_like(col_part)
    row_part[...] = jnp.zeros_like(row_part)
    lane_ids = lax.broadcasted_iota(jnp.int32, (1, LANES), 1)
    states_sums = [whole(states[k]) for k in (0, 2)]
    add_products(fours, FOURS_ORDER)
    pl.semaphore_wait(known.at[0], Z - 1)
    to_x(lambda to: pl.semaphore_signal(known.at[1], inc=1, device_id=to, device_id_type=MESH))
    add_products(twos, TWOS_ORDER)
    pl.semaphore_wait(known.at[1], X - 1)
    def exchange(phase, src, got, slot, to_each, sems):
        send_sem, recv_sem = sems

        def copy(source, target, to):
            return pltpu.make_async_remote_copy(
                src_ref=source, dst_ref=target,
                send_sem=send_sem.at[phase], recv_sem=recv_sem.at[phase],
                device_id=to, device_id_type=MESH)

        others = got.at[phase, pl.ds(0, got.shape[1] - 1)]

        def start():
            to_each(lambda to: copy(src, got.at[phase, slot], to).start())
            got[phase, slot] = src[...]

        def result():
            copy(others, others, (row, twin)).wait_recv()
            return jnp.sum(got[phase], axis=0)

        def drain():
            copy(others, others, (row, twin)).wait_send()

        return start, result, drain

    def sums(block):
        def rows_of(i, col_sum):
            at = part(i * LANES, LANES, LANES)
            row_sum = jnp.zeros((LANES, LANES), F32)
            col_sums = []
            for j in range(nc):
                square = block(at, j)
                row_sum += square
                col_sums.append(jnp.sum(square.reshape(LANES // 8, 8, LANES), axis=0))
            row_sums[at, :] = row_sum
            return col_sum + jnp.concatenate(col_sums, 1)

        return lax.fori_loop(0, nr, rows_of, jnp.zeros((8, cols), F32))

    def reduced(phase, col_sum, beside, meanwhile):
        col_sums = [col_sum[:, j * LANES:(j + 1) * LANES] for j in range(nc)]
        values = whole(functools.reduce(jnp.add, col_sums))
        for lane, value in enumerate(beside):
            values = jnp.where(lane_ids == lane + 1, value, values)
        tot_part[phase] = jnp.broadcast_to(values, (1, LANES))
        by_twin = exchange(phase, tot_part.at[phase], tot_got, core, to_twin, (tot_send, tot_recv))
        by_twin[0]()
        for j in range(nc):
            col_part[phase, j:j + 1, :] = jnp.sum(col_sums[j], axis=0, keepdims=True)
        by_x = exchange(phase, col_part.at[phase], x_got, x, to_x, (x_send, x_recv))
        by_x[0]()
        for i in range(nr):
            turned = row_sums[i * LANES:(i + 1) * LANES, :].T
            row_part[phase, i:i + 1, :] = jnp.sum(turned, axis=0, keepdims=True)
        by_row = exchange(phase, row_part.at[phase], row_got, col, to_col, (row_send, row_recv))
        by_row[0]()
        all_part[phase] = by_twin[1]()
        by_all = exchange(phase, all_part.at[phase], all_got, row * Y + y, to_chips, (all_send, all_recv))
        by_all[0]()
        z_part[phase] = by_x[1]()
        by_z = exchange(phase, z_part.at[phase], col_got, z, to_z, (col_send, col_recv))
        by_z[0]()
        meanwhile()
        row_all = by_row[1]()
        col_all = by_z[1]()
        for one in (by_twin, by_x, by_row, by_z):
            one[2]()
        totals = by_all[1]()
        return row_all, col_all, totals, by_all[2]

    def down_rows(factors):
        for i in range(nr):
            row_scale[i * LANES:(i + 1) * LANES, :] = jnp.broadcast_to(factors[i:i + 1, :], (LANES, LANES)).T

    def squared(at, j):
        g = G[at, j * LANES:(j + 1) * LANES]
        return g * g

    def gather_drain():
        for lane, (axis, sign) in enumerate(ring_to):
            gone = sum(extent(m)[1] for m in sent if m[:2] == (axis, sign))
            gone = B.at[pl.ds(0, gone)]
            pltpu.make_async_remote_copy(
                src_ref=gone, dst_ref=gone, send_sem=ring_send.at[lane], recv_sem=ring_recv.at[lane, 0],
                device_id=(ring_to[axis, sign], col), device_id_type=MESH).wait_send()
        gone = A.at[pl.ds(0, 7 * shard)]
        pltpu.make_async_remote_copy(
            src_ref=gone, dst_ref=gone, send_sem=act_send.at[0], recv_sem=act_recv.at[0],
            device_id=(row, twin), device_id_type=MESH).wait_send()
        strip(row).wait_send()

    col_sum = sums(squared)
    row_all, col_all, totals, drain0 = reduced(0, col_sum, states_sums, gather_drain)
    total, row_state_sum, row_conf_sum = totals[:, 0:1], totals[:, 1:2] * (1.0 / C), totals[:, 2:3] * (1.0 / C)
    spread = jnp.minimum(1.0, (full_rows * full_cols) / (total + 1e-06))
    keep, fresh = second_decay, 1.0 - second_decay
    row_new = keep * states[0] + fresh * (spread * row_all * (1.0 / full_cols) + tiny_moment)
    col_new = keep * states[1] + fresh * (spread * col_all * (1.0 / full_rows) + tiny_moment)
    row_mean = keep * (row_state_sum * (1.0 / full_rows)) + fresh * (
        spread * total * (1.0 / (full_rows * full_cols)) + tiny_moment)
    down_rows(lax.rsqrt(row_new))
    packed[0] = row_new
    packed[1] = col_new
    col_scale = lax.rsqrt(col_new) * jnp.sqrt(spread * row_mean)

    def strays(at, j):
        here = (at, slice(j * LANES, (j + 1) * LANES))
        direction = G[here] * row_scale[at, :] * col_scale[j:j + 1, :]
        stray = direction - M[here]
        M[here] = M[here] + (1.0 - first_decay) * stray
        return stray * stray

    col_sum = sums(strays)
    row_all, col_all, totals, drain1 = reduced(1, col_sum, [], drain0)
    total = totals[:, 0:1]
    share = first_decay * first_decay
    row_conf_new = keep * states[2] + fresh * (row_all * (share / full_cols) + tiny_confidence)
    col_conf_new = keep * states[3] + fresh * (col_all * (share / full_rows) + tiny_confidence)
    conf_mean = keep * (row_conf_sum * (1.0 / full_rows)) + fresh * (
        total * (share / (full_rows * full_cols)) + tiny_confidence)
    packed[2] = row_conf_new
    packed[3] = col_conf_new
    packed[4] = lax.rsqrt(row_conf_new)
    packed[5] = lax.rsqrt(col_conf_new) * jnp.sqrt(conf_mean)
    drain1()


def finish(M, packed, moment_out, update_out, row_out, col_out, row_conf_out, col_conf_out, U, sem, block_sem):
    rows, cols = U.shape
    nr, nc = rows // LANES, cols // LANES
    stores = [pltpu.make_async_copy(M, moment_out, sem.at[0])]
    for k, (out, n) in enumerate(((row_out, nr), (col_out, nc), (row_conf_out, nr), (col_conf_out, nc))):
        stores.append(pltpu.make_async_copy(packed.at[k, pl.ds(0, n)], out, sem.at[1 + k]))
    for store in stores:
        store.start()

    def block_store(i):
        at = pl.ds(pl.multiple_of(i * LANES, LANES), LANES)
        return pltpu.make_async_copy(U.at[at], update_out.at[at], block_sem.at[i])

    def scale_block(i, carry):
        at = pl.ds(pl.multiple_of(i * LANES, LANES), LANES)
        scale = jnp.broadcast_to(packed[4, pl.ds(i, 1), :], (LANES, LANES)).T
        for j in range(nc):
            here = (at, slice(j * LANES, (j + 1) * LANES))
            U[here] = M[here] * scale * packed[5, j:j + 1, :]
        block_store(i).start()
        return carry

    def wait_block(i, carry):
        block_store(i).wait()
        return carry

    lax.fori_loop(0, nr, scale_block, 0)
    lax.fori_loop(0, nr, wait_block, 0)
    for store in stores:
        store.wait()


def on_device(acts, out_grads, moment, row_state, col_state, row_conf, col_conf):
    R, C = lax.axis_size("row"), lax.axis_size("col")
    rows, cols = moment.shape
    nr, nc = rows // LANES, cols // LANES
    dma = pltpu.SemaphoreType.DMA
    big = jax.ShapeDtypeStruct((rows, cols), F32)
    by_row, by_col = (jax.ShapeDtypeStruct((n, LANES), F32) for n in (nr, nc))
    in_hbm = pl.BlockSpec(memory_space=pltpu.HBM)
    in_vmem = pl.BlockSpec(memory_space=pltpu.VMEM)
    tokens = R * out_grads.shape[0]
    moment_new, packed = pl.pallas_call(
        functools.partial(kernel, R, C),
        out_shape=(pltpu.VMEM((rows, cols), F32), pltpu.VMEM((6, 8, LANES), F32)),
        in_specs=[in_hbm] * 7,
        out_specs=(in_vmem,) * 2,
        scratch_shapes=[
            pltpu.VMEM((tokens, rows), acts.dtype),
            pltpu.VMEM((tokens, cols), out_grads.dtype),
            pltpu.VMEM((rows, cols), F32),
            pltpu.VMEM((4, 8, LANES), F32),
            pltpu.VMEM((rows, LANES), F32),
            pltpu.VMEM((rows, LANES), F32),
            pltpu.VMEM((2, 8, LANES), F32),
            pltpu.VMEM((2, C, 8, LANES), F32),
            pltpu.VMEM((2, 8, LANES), F32),
            pltpu.VMEM((2, X, 8, LANES), F32),
            pltpu.VMEM((2, 8, LANES), F32),
            pltpu.VMEM((2, R // X, 8, LANES), F32),
            pltpu.VMEM((2, 1, LANES), F32),
            pltpu.VMEM((2, 2, 1, LANES), F32),
            pltpu.VMEM((2, 1, LANES), F32),
            pltpu.VMEM((2, R * C // 2, 1, LANES), F32),
            dma((4,)), dma((4, 20)), dma((2,)), dma((12,)), dma((7,)),
            *[dma((2,))] * 10, pltpu.SemaphoreType.REGULAR((2,)),
        ],
        compiler_params=pltpu.CompilerParams(
            collective_id=0, has_side_effects=True, vmem_limit_bytes=40 * 2**20),
        cost_estimate=pl.CostEstimate(
            flops=2 * tokens * rows * cols, transcendentals=0, bytes_accessed=30 * 2**20),
        name="came_step",
    )(*(pltpu.with_memory_space_constraint(v, pltpu.HBM) for v in (
        acts, out_grads, moment, row_state.reshape(nr, LANES), col_state.reshape(nc, LANES),
        row_conf.reshape(nr, LANES), col_conf.reshape(nc, LANES))))
    outs = pl.pallas_call(
        finish,
        out_shape=(big, big, by_row, by_col, by_row, by_col),
        in_specs=[in_vmem] * 2,
        out_specs=(in_hbm,) * 6,
        scratch_shapes=[pltpu.VMEM((rows, cols), F32), dma((5,)), dma((nr,))],
        compiler_params=pltpu.CompilerParams(vmem_limit_bytes=16 * 2**20),
        cost_estimate=pl.CostEstimate(
            flops=2 * rows * cols, transcendentals=0, bytes_accessed=12 * rows * cols),
        name="finish",
    )(moment_new, packed)
    return outs[0], outs[1], *(out.reshape(-1) for out in outs[2:])


def solution(mesh):
    placed = (
        P("col", "row"),
        P("row", "col"),
        P("row", "col"),
        P("row"),
        P("col"),
        P("row"),
        P("col"),
    )
    return jax.shard_map(
        on_device,
        mesh=mesh,
        in_specs=placed,
        out_specs=(P("row", "col"), P("row", "col"), P("row"), P("col"), P("row"), P("col")),
        check_vma=False,
    )
```

```python
import functools

import jax
import jax.numpy as jnp
from jax import lax
from jax.experimental import pallas as pl
from jax.experimental.pallas import tpu as pltpu
from jax.sharding import PartitionSpec as P

MESH = pl.DeviceIdType.MESH
F32 = jnp.float32
STEP = 10
X = 4
LANES = 128

first_decay = 0.9
tiny_moment = 1e-30
tiny_confidence = 1e-16
second_decay = 1.0 - STEP ** (-0.8)


ORDER = (
    ("z", "Q", 0, 0), ("x", "P", 0, 0), ("x", "Q", 0, 0), ("z", "P", 0, 0), "own low",
    ("z", "P", 1, 0), ("x", "P", 0, 1), ("x", "Q", 1, 0), ("z", "Q", 0, 1), "own high",
    ("x", "Q", -1, 0), ("z", "P", -1, 0), ("x", "Q", 0, 1), "strip out", ("z", "P", 0, 1),
    ("z", "Q", 0, 2), ("x", "Q", 2, 0), ("x", "Q", 1, 1), "strip", ("z", "P", 2, 0), "near",
    ("z", "P", 1, 1), ("x", "Q", -2, 0), ("x", "Q", -1, 1), ("z", "Q", 0, 3), ("z", "P", -1, 1),
    ("x", "Q", 3, 0), ("z", "P", 2, 1), "cross",
    ("x", "Q", 2, 1), ("x", "Q", -3, 0), ("z", "P", 0, 2), ("z", "P", 1, 2), ("x", "Q", -2, 1),
    ("z", "P", -1, 2), ("x", "Q", 4, 0), "far", ("z", "P", 2, 2), ("x", "Q", 3, 1), "all",
)
FOURS_ORDER = (
    (), (("z", "P", 0, 3),), (), (("x", "Q", -3, 1), ("z", "P", 1, 3)), (), (("z", "P", -1, 3),))
TWOS_ORDER = ((("x", "Q", 4, 1), ("z", "P", 2, 3)), (), (), ())
HOPS = {"z": 4, "x": 2}


def kernel(R, C, acts, grads, moment, row_state, col_state, row_conf, col_conf, M, packed,
           A, B, G, states, row_sums, row_scale, row_part, row_got, col_part, x_got, x_part, col_got,
           tot_part, tot_got, all_part, all_got,
           ring_send, ring_recv, act_send, act_recv, load_sem,
           row_send, row_recv, x_send, x_recv, col_send, col_recv, tot_send, tot_recv, all_send, all_recv, known):
    Z, Y = R // X, C // 2
    row, col = lax.axis_index("row"), lax.axis_index("col")
    div, rem = lax.div, lax.rem
    z, x, y, core = div(row, X), rem(row, X), div(col, 2), rem(col, 2)
    tb, shard = grads.shape[0], acts.shape[0]
    hs = shard // 2
    rows, cols = G.shape
    nr, nc = rows // LANES, cols // LANES
    full_rows, full_cols = rows * R, cols * C
    p_rows = 3 * tb // 8

    def at_offset(dz, dx):
        return rem(z + dz + Z, Z) * X + rem(x + dx + X, X)

    across = at_offset(0, 2)


    def part(first, unit, size):
        return pl.ds(pl.multiple_of(first, unit), size)

    ring_to = {("z", s): at_offset(s, 0) for s in (1, -1)} | {("x", s): at_offset(0, s) for s in (1, -1)}
    up, down = rem(y + 1, Y) * 2 + core, rem(y + Y - 1, Y) * 2 + core
    far, twin = rem(y + 2, Y) * 2 + core, y * 2 + 1 - core

    def whole(tile):
        return jnp.sum(tile, axis=(0, 1), keepdims=True)

    def from_far(length):
        return sorted(range(length), key=lambda d: -min(d, length - d))

    def to_twin(go):
        go((row, twin))

    def to_x(go):
        for dx in from_far(X)[:-1]:
            go((at_offset(0, dx), col))

    def to_z(go):
        for dz in from_far(Z)[:-1]:
            go((at_offset(dz, 0), col))

    def to_col(go):
        for dy in from_far(Y):
            for dc in (1, 0):
                if dy or dc:
                    go((row, rem(y + dy, Y) * 2 + rem(core + dc, 2)))

    def to_chips(go):
        def plane(a, carry):
            dz = Z // 2 + div(a + 1, 2) * (2 * rem(a, 2) - 1)
            for dx in from_far(X):
                for dy in from_far(Y):
                    to = at_offset(dz, dx), rem(y + dy, Y) * 2 + core
                    if dx or dy:
                        go(to)
                    else:
                        pl.when(a < Z - 1)(functools.partial(go, to))
            return carry
        lax.fori_loop(0, Z, plane, 0)

    barrier = pltpu.get_barrier_semaphore()
    for r in ring_to.values():
        pl.semaphore_signal(barrier, inc=1, device_id=(r, col), device_id_type=MESH)
    for c in (up, down, twin):
        pl.semaphore_signal(barrier, inc=1, device_id=(row, c), device_id_type=MESH)

    loads = [
        pltpu.make_async_copy(grads, B.at[part(row * tb, tb, tb)], load_sem.at[0]),
        pltpu.make_async_copy(acts, A.at[part(col * shard, shard, shard)], load_sem.at[1]),
        pltpu.make_async_copy(moment, M, load_sem.at[2]),
        pltpu.make_async_copy(row_state, states.at[0, pl.ds(0, nr)], load_sem.at[3]),
        pltpu.make_async_copy(col_state, states.at[1, pl.ds(0, nc)], load_sem.at[4]),
        pltpu.make_async_copy(row_conf, states.at[2, pl.ds(0, nr)], load_sem.at[5]),
        pltpu.make_async_copy(col_conf, states.at[3, pl.ds(0, nc)], load_sem.at[6]),
    ]
    states[...] = jnp.zeros_like(states)
    for load in loads:
        load.start()
    pl.semaphore_wait(barrier, 7)

    def extent(message):
        axis, sign, kind, off, hops = message
        first, size = (0, p_rows) if kind == "P" else (p_rows, tb - p_rows)
        if axis == "z" and kind == "P" and off == HOPS["x"]:
            size += 16
        if axis == "x" and kind == "Q" and hops == HOPS["x"] - 1:
            first, size = first + 16, size - 16
        if hops == HOPS[axis] - 1:
            low = (size // 2 + 15) // 16 * 16
            low = size - low if off % 2 else low
            return (first, low) if sign > 0 else (first + low, size - low)
        return first, size

    def placed(message, hops):
        axis, sign, _, off, _ = message
        dz, dx = (-sign * hops, off) if axis == "z" else (off, -sign * hops)
        first, size = extent(message)
        return B.at[part(at_offset(dz, dx) * tb + first, 16, size)]

    numbers = {}

    def ring(message, hops):
        axis, sign, _, off, made = message
        lane = 2 * (axis == "x") + (sign < 0)
        number = numbers.setdefault(message, sum(m[:2] == message[:2] for m in numbers))
        first, size = extent(message)
        there = placed(message, hops)
        return pltpu.make_async_remote_copy(
            src_ref=grads.at[pl.ds(first, size)] if made == 0 and off == 0 else there, dst_ref=there,
            send_sem=ring_send.at[lane], recv_sem=ring_recv.at[lane, number],
            device_id=(ring_to[axis, sign], col), device_id_type=MESH)

    def strip(owner):
        return pltpu.make_async_remote_copy(
            src_ref=grads.at[pl.ds(p_rows, 16)], dst_ref=B.at[part(owner * tb + p_rows, 16, 16)],
            send_sem=act_send.at[1], recv_sem=act_recv.at[11],
            device_id=(across, col), device_id_type=MESH)

    sent, landed = [], set()

    def await_messages(messages):
        for message in messages:
            if message not in landed:
                landed.add(message)
                ring(message, message[4] + 1).wait_recv()

    def brought(message):
        axis, sign, kind, off, hops = message
        if hops > 0:
            return [(axis, sign, kind, off, hops - 1)]
        if off == 0:
            return []
        other = "x" if axis == "z" else "z"
        last = HOPS[other] - 1
        if abs(off) == HOPS[other]:
            return [(other, 1, kind, 0, last), (other, -1, kind, 0, last)]
        return [(other, -1 if off > 0 else 1, kind, 0, abs(off) - 1)]

    def send(axis, kind, off, hops):
        mirrored = off if abs(off) == HOPS["x" if axis == "z" else "z"] else -off
        pair = [(axis, 1, kind, off, hops), (axis, -1, kind, mirrored, hops)]
        for message in pair:
            await_messages(brought(message))
            ring(message, hops).start()
            sent.append(message)

    def brings(message, dz):
        axis, sign, _, off, hops = message
        if axis == "x":
            return off == dz
        return dz == HOPS["z"] if hops == HOPS["z"] - 1 else dz == -sign * (hops + 1)

    def act(i, owner, first, size, to, src=None):
        there = A.at[part(owner * shard + first, hs, size)]
        return pltpu.make_async_remote_copy(
            src_ref=there if src is None else src, dst_ref=there,
            send_sem=act_send.at[0], recv_sem=act_recv.at[i],
            device_id=(row, to), device_id_type=MESH)

    low, high = acts.at[pl.ds(0, hs)], acts.at[pl.ds(hs, hs)]
    act_out = {
        0: act(0, col, 0, hs, up, low), 3: act(3, col, hs, hs, down, high),
        1: act(1, col, hs, hs, up, high), 4: act(4, col, 0, hs, down, low),
        6: act(6, col, 0, shard, twin, acts),
        2: act(2, down, 0, hs, up), 5: act(5, up, hs, hs, down),
        7: act(7, down, 0, shard, twin), 8: act(8, up, 0, shard, twin),
        9: act(9, far, 0, hs, twin), 10: act(10, far, hs, hs, twin),
    }
    swap = 1 - 2 * core
    act_in = {
        0: act(0, down, 0, hs, up), 1: act(1, down, hs, hs, up), 2: act(2, far, 0, hs, up),
        3: act(3, up, hs, hs, down), 4: act(4, up, 0, hs, down), 5: act(5, far, hs, hs, down),
        6: act(6, twin, 0, shard, twin), 7: act(7, down + swap, 0, shard, twin),
        8: act(8, up + swap, 0, shard, twin), 9: act(9, far + swap, 0, hs, twin),
        10: act(10, far + swap, hs, hs, twin),
    }
    act_steps = {
        "own low": ((), (0, 3, 6)), "own high": ((), (1, 4)), "near": ((0, 3), (2, 5)),
        "cross": ((1, 4), (7, 8)), "far": ((2, 5), (9, 10)), "all": ((6, 7, 8, 9, 10), ()),
        "strip": ((), ()), "strip out": ((), ()),
    }

    def fours(i):
        dz, odd = div(i + 1, 2) * (2 * rem(i, 2) - 1), div(i, 5)
        return (dz, 0), (dz, 1), (dz, 3), (dz - 6 * odd, 2 - 2 * odd)

    def twos(i):
        return (5 - 2 * rem(i, 2) + div(i, 3), 1 + div(i + 1, 2)), (5 - div(i + 2, 3), i - 1)

    def await_blocks(offsets):
        for dz, dx in offsets:
            dz, dx = (dz + Z // 2 - 1) % Z - Z // 2 + 1, (dx + 1) % X - 1
            await_messages([m for m in sent if brings(m, dz) and (
                m[3] == dx if m[0] == "z" else dx == -m[1] * (m[4] + 1) or (dx == 2 and m[4] == 1))])

    def add_products(blocks, order):
        def ahead(n):
            for message in order[n]:
                send(*message)
            await_blocks(static_blocks(blocks, n))

        def add(i, carry):
            for n in range(len(order)):
                pl.when(i == n)(functools.partial(ahead, n))
            tokens = [part(at_offset(dz, dx) * tb, tb, tb) for dz, dx in blocks(i)]
            G[...] += lax.dot_general(
                jnp.concatenate([A[t, :] for t in tokens], 0), jnp.concatenate([B[t, :] for t in tokens], 0),
                (((0,), (0,)), ((), ())), preferred_element_type=F32)
            return carry

        lax.fori_loop(0, len(order), add, 0)

    def static_blocks(blocks, n):
        if blocks is fours:
            dz, odd = (n + 1) // 2 * (2 * (n % 2) - 1), n // 5
            return (dz, 0), (dz, 1), (dz, 3), (dz - 6 * odd, 2 - 2 * odd)
        return (5 - 2 * (n % 2) + n // 3, 1 + (n + 1) // 2), (5 - (n + 2) // 3, n - 1)

    for entry in ORDER:
        if isinstance(entry, str):
            arrive, leave = act_steps[entry]
            for i in arrive:
                act_in[i].wait_recv()
            for i in leave:
                act_out[i].start()
            if entry == "strip out":
                await_messages([("x", s, "P", 0, 1) for s in (1, -1)])
                strip(row).start()
            if entry == "strip":
                strip(across).wait_recv()
            if entry == "own high":
                loads[0].wait()
                loads[1].wait()
                G[...] = jnp.zeros_like(G)
        else:
            send(*entry)
    to_z(lambda to: pl.semaphore_signal(known.at[0], inc=1, device_id=to, device_id_type=MESH))
    for load in loads[2:]:
        load.wait()
    col_part[...] = jnp.zeros_like(col_part)
    row_part[...] = jnp.zeros_like(row_part)
    lane_ids = lax.broadcasted_iota(jnp.int32, (1, LANES), 1)
    states_sums = [whole(states[k]) for k in (0, 2)]
    add_products(fours, FOURS_ORDER)
    pl.semaphore_wait(known.at[0], Z - 1)
    to_x(lambda to: pl.semaphore_signal(known.at[1], inc=1, device_id=to, device_id_type=MESH))
    add_products(twos, TWOS_ORDER)
    pl.semaphore_wait(known.at[1], X - 1)
    def exchange(phase, src, got, slot, to_each, sems):
        send_sem, recv_sem = sems

        def copy(source, target, to):
            return pltpu.make_async_remote_copy(
                src_ref=source, dst_ref=target,
                send_sem=send_sem.at[phase], recv_sem=recv_sem.at[phase],
                device_id=to, device_id_type=MESH)

        others = got.at[phase, pl.ds(0, got.shape[1] - 1)]

        def start():
            to_each(lambda to: copy(src, got.at[phase, slot], to).start())
            got[phase, slot] = src[...]

        def result():
            copy(others, others, (row, twin)).wait_recv()
            return jnp.sum(got[phase], axis=0)

        def drain():
            copy(others, others, (row, twin)).wait_send()

        return start, result, drain

    def sums(block):
        def rows_of(i, col_sum):
            at = part(i * LANES, LANES, LANES)
            row_sum = jnp.zeros((LANES, LANES), F32)
            col_sums = []
            for j in range(nc):
                square = block(at, j)
                row_sum += square
                col_sums.append(jnp.sum(square.reshape(LANES // 8, 8, LANES), axis=0))
            row_sums[at, :] = row_sum
            return col_sum + jnp.concatenate(col_sums, 1)

        return lax.fori_loop(0, nr, rows_of, jnp.zeros((8, cols), F32))

    def reduced(phase, col_sum, beside, meanwhile):
        col_sums = [col_sum[:, j * LANES:(j + 1) * LANES] for j in range(nc)]
        values = whole(functools.reduce(jnp.add, col_sums))
        for lane, value in enumerate(beside):
            values = jnp.where(lane_ids == lane + 1, value, values)
        tot_part[phase] = jnp.broadcast_to(values, (1, LANES))
        by_twin = exchange(phase, tot_part.at[phase], tot_got, core, to_twin, (tot_send, tot_recv))
        by_twin[0]()
        for j in range(nc):
            col_part[phase, j:j + 1, :] = jnp.sum(col_sums[j], axis=0, keepdims=True)
        by_z = exchange(phase, col_part.at[phase], col_got, z, to_z, (col_send, col_recv))
        by_z[0]()
        for i in range(nr):
            turned = row_sums[i * LANES:(i + 1) * LANES, :].T
            row_part[phase, i:i + 1, :] = jnp.sum(turned, axis=0, keepdims=True)
        by_row = exchange(phase, row_part.at[phase], row_got, col, to_col, (row_send, row_recv))
        by_row[0]()
        all_part[phase] = by_twin[1]()
        by_all = exchange(phase, all_part.at[phase], all_got, row * Y + y, to_chips, (all_send, all_recv))
        by_all[0]()
        x_part[phase] = by_z[1]()
        by_x = exchange(phase, x_part.at[phase], x_got, x, to_x, (x_send, x_recv))
        by_x[0]()
        meanwhile()
        row_all = by_row[1]()
        col_all = by_x[1]()
        for one in (by_twin, by_z, by_row, by_x):
            one[2]()
        totals = by_all[1]()
        return row_all, col_all, totals, by_all[2]

    def down_rows(factors):
        for i in range(nr):
            row_scale[i * LANES:(i + 1) * LANES, :] = jnp.broadcast_to(factors[i:i + 1, :], (LANES, LANES)).T

    def squared(at, j):
        g = G[at, j * LANES:(j + 1) * LANES]
        return g * g

    def gather_drain():
        for lane, (axis, sign) in enumerate(ring_to):
            gone = sum(extent(m)[1] for m in sent if m[:2] == (axis, sign))
            gone = B.at[pl.ds(0, gone)]
            pltpu.make_async_remote_copy(
                src_ref=gone, dst_ref=gone, send_sem=ring_send.at[lane], recv_sem=ring_recv.at[lane, 0],
                device_id=(ring_to[axis, sign], col), device_id_type=MESH).wait_send()
        gone = A.at[pl.ds(0, 7 * shard)]
        pltpu.make_async_remote_copy(
            src_ref=gone, dst_ref=gone, send_sem=act_send.at[0], recv_sem=act_recv.at[0],
            device_id=(row, twin), device_id_type=MESH).wait_send()
        strip(row).wait_send()

    col_sum = sums(squared)
    row_all, col_all, totals, drain0 = reduced(0, col_sum, states_sums, gather_drain)
    total, row_state_sum, row_conf_sum = totals[:, 0:1], totals[:, 1:2] * (1.0 / C), totals[:, 2:3] * (1.0 / C)
    spread = jnp.minimum(1.0, (full_rows * full_cols) / (total + 1e-06))
    keep, fresh = second_decay, 1.0 - second_decay
    row_new = keep * states[0] + fresh * (spread * row_all * (1.0 / full_cols) + tiny_moment)
    col_new = keep * states[1] + fresh * (spread * col_all * (1.0 / full_rows) + tiny_moment)
    row_mean = keep * (row_state_sum * (1.0 / full_rows)) + fresh * (
        spread * total * (1.0 / (full_rows * full_cols)) + tiny_moment)
    down_rows(lax.rsqrt(row_new))
    packed[0] = row_new
    packed[1] = col_new
    col_scale = lax.rsqrt(col_new) * jnp.sqrt(spread * row_mean)

    def strays(at, j):
        here = (at, slice(j * LANES, (j + 1) * LANES))
        direction = G[here] * row_scale[at, :] * col_scale[j:j + 1, :]
        stray = direction - M[here]
        M[here] = M[here] + (1.0 - first_decay) * stray
        return stray * stray

    col_sum = sums(strays)
    row_all, col_all, totals, drain1 = reduced(1, col_sum, [], drain0)
    total = totals[:, 0:1]
    share = first_decay * first_decay
    row_conf_new = keep * states[2] + fresh * (row_all * (share / full_cols) + tiny_confidence)
    col_conf_new = keep * states[3] + fresh * (col_all * (share / full_rows) + tiny_confidence)
    conf_mean = keep * (row_conf_sum * (1.0 / full_rows)) + fresh * (
        total * (share / (full_rows * full_cols)) + tiny_confidence)
    packed[2] = row_conf_new
    packed[3] = col_conf_new
    packed[4] = lax.rsqrt(row_conf_new)
    packed[5] = lax.rsqrt(col_conf_new) * jnp.sqrt(conf_mean)
    drain1()


def finish(M, packed, moment_out, update_out, row_out, col_out, row_conf_out, col_conf_out, U, sem, block_sem):
    rows, cols = U.shape
    nr, nc = rows // LANES, cols // LANES
    stores = [pltpu.make_async_copy(M, moment_out, sem.at[0])]
    for k, (out, n) in enumerate(((row_out, nr), (col_out, nc), (row_conf_out, nr), (col_conf_out, nc))):
        stores.append(pltpu.make_async_copy(packed.at[k, pl.ds(0, n)], out, sem.at[1 + k]))
    for store in stores:
        store.start()

    def block_store(i):
        at = pl.ds(pl.multiple_of(i * LANES, LANES), LANES)
        return pltpu.make_async_copy(U.at[at], update_out.at[at], block_sem.at[i])

    def scale_block(i, carry):
        at = pl.ds(pl.multiple_of(i * LANES, LANES), LANES)
        scale = jnp.broadcast_to(packed[4, pl.ds(i, 1), :], (LANES, LANES)).T
        for j in range(nc):
            here = (at, slice(j * LANES, (j + 1) * LANES))
            U[here] = M[here] * scale * packed[5, j:j + 1, :]
        block_store(i).start()
        return carry

    def wait_block(i, carry):
        block_store(i).wait()
        return carry

    lax.fori_loop(0, nr, scale_block, 0)
    lax.fori_loop(0, nr, wait_block, 0)
    for store in stores:
        store.wait()


def on_device(acts, out_grads, moment, row_state, col_state, row_conf, col_conf):
    R, C = lax.axis_size("row"), lax.axis_size("col")
    rows, cols = moment.shape
    nr, nc = rows // LANES, cols // LANES
    dma = pltpu.SemaphoreType.DMA
    big = jax.ShapeDtypeStruct((rows, cols), F32)
    by_row, by_col = (jax.ShapeDtypeStruct((n, LANES), F32) for n in (nr, nc))
    in_hbm = pl.BlockSpec(memory_space=pltpu.HBM)
    in_vmem = pl.BlockSpec(memory_space=pltpu.VMEM)
    tokens = R * out_grads.shape[0]
    moment_new, packed = pl.pallas_call(
        functools.partial(kernel, R, C),
        out_shape=(pltpu.VMEM((rows, cols), F32), pltpu.VMEM((6, 8, LANES), F32)),
        in_specs=[in_hbm] * 7,
        out_specs=(in_vmem,) * 2,
        scratch_shapes=[
            pltpu.VMEM((tokens, rows), acts.dtype),
            pltpu.VMEM((tokens, cols), out_grads.dtype),
            pltpu.VMEM((rows, cols), F32),
            pltpu.VMEM((4, 8, LANES), F32),
            pltpu.VMEM((rows, LANES), F32),
            pltpu.VMEM((rows, LANES), F32),
            pltpu.VMEM((2, 8, LANES), F32),
            pltpu.VMEM((2, C, 8, LANES), F32),
            pltpu.VMEM((2, 8, LANES), F32),
            pltpu.VMEM((2, X, 8, LANES), F32),
            pltpu.VMEM((2, 8, LANES), F32),
            pltpu.VMEM((2, R // X, 8, LANES), F32),
            pltpu.VMEM((2, 1, LANES), F32),
            pltpu.VMEM((2, 2, 1, LANES), F32),
            pltpu.VMEM((2, 1, LANES), F32),
            pltpu.VMEM((2, R * C // 2, 1, LANES), F32),
            dma((4,)), dma((4, 20)), dma((2,)), dma((12,)), dma((7,)),
            *[dma((2,))] * 10, pltpu.SemaphoreType.REGULAR((2,)),
        ],
        compiler_params=pltpu.CompilerParams(
            collective_id=0, has_side_effects=True, vmem_limit_bytes=40 * 2**20),
        cost_estimate=pl.CostEstimate(
            flops=2 * tokens * rows * cols, transcendentals=0, bytes_accessed=30 * 2**20),
        name="came_step",
    )(*(pltpu.with_memory_space_constraint(v, pltpu.HBM) for v in (
        acts, out_grads, moment, row_state.reshape(nr, LANES), col_state.reshape(nc, LANES),
        row_conf.reshape(nr, LANES), col_conf.reshape(nc, LANES))))
    outs = pl.pallas_call(
        finish,
        out_shape=(big, big, by_row, by_col, by_row, by_col),
        in_specs=[in_vmem] * 2,
        out_specs=(in_hbm,) * 6,
        scratch_shapes=[pltpu.VMEM((rows, cols), F32), dma((5,)), dma((nr,))],
        compiler_params=pltpu.CompilerParams(vmem_limit_bytes=16 * 2**20),
        cost_estimate=pl.CostEstimate(
            flops=2 * rows * cols, transcendentals=0, bytes_accessed=12 * rows * cols),
        name="finish",
    )(moment_new, packed)
    return outs[0], outs[1], *(out.reshape(-1) for out in outs[2:])


def solution(mesh):
    placed = (
        P("col", "row"),
        P("row", "col"),
        P("row", "col"),
        P("row"),
        P("col"),
        P("row"),
        P("col"),
    )
    return jax.shard_map(
        on_device,
        mesh=mesh,
        in_specs=placed,
        out_specs=(P("row", "col"), P("row", "col"), P("row"), P("col"), P("row"), P("col")),
        check_vma=False,
    )
```

```python
import functools

import jax
import jax.numpy as jnp
from jax import lax
from jax.experimental import pallas as pl
from jax.experimental.pallas import tpu as pltpu
from jax.sharding import PartitionSpec as P

MESH = pl.DeviceIdType.MESH
F32 = jnp.float32
STEP = 10
X = 4
LANES = 128

first_decay = 0.9
tiny_moment = 1e-30
tiny_confidence = 1e-16
second_decay = 1.0 - STEP ** (-0.8)


ORDER = (
    ("z", "Q", 0, 0), ("x", "P", 0, 0), ("x", "Q", 0, 0), ("z", "P", 0, 0), "own low",
    ("z", "P", 1, 0), ("x", "P", 0, 1), ("x", "Q", 1, 0), ("z", "Q", 0, 1), "own high",
    ("x", "Q", -1, 0), ("z", "P", -1, 0), ("x", "Q", 0, 1), "strip out", ("z", "P", 0, 1),
    ("z", "Q", 0, 2), ("x", "Q", 2, 0), ("x", "Q", 1, 1), "strip", ("z", "P", 2, 0), "near",
    ("z", "P", 1, 1), ("x", "Q", -2, 0), ("x", "Q", -1, 1), ("z", "Q", 0, 3), ("z", "P", -1, 1),
    ("x", "Q", 3, 0), ("z", "P", 2, 1), "cross",
    ("x", "Q", 2, 1), ("x", "Q", -3, 0), ("z", "P", 0, 2), ("z", "P", 1, 2), ("x", "Q", -2, 1),
    ("z", "P", -1, 2), ("x", "Q", 4, 0), "far", ("z", "P", 2, 2), ("x", "Q", 3, 1), "all",
)
FOURS_ORDER = (
    (), (("z", "P", 0, 3),), (), (("x", "Q", -3, 1), ("z", "P", 1, 3)), (), (("z", "P", -1, 3),))
TWOS_ORDER = ((("x", "Q", 4, 1), ("z", "P", 2, 3)), (), (), ())
HOPS = {"z": 4, "x": 2}


def kernel(R, C, acts, grads, moment, row_state, col_state, row_conf, col_conf, M, packed,
           A, B, G, states, row_sums, row_scale, row_part, row_got, col_part, x_got, x_part, col_got,
           tot_part, tot_got, all_part, all_got,
           ring_send, ring_recv, act_send, act_recv, load_sem,
           row_send, row_recv, x_send, x_recv, col_send, col_recv, tot_send, tot_recv, all_send, all_recv, known):
    Z, Y = R // X, C // 2
    row, col = lax.axis_index("row"), lax.axis_index("col")
    div, rem = lax.div, lax.rem
    z, x, y, core = div(row, X), rem(row, X), div(col, 2), rem(col, 2)
    tb, shard = grads.shape[0], acts.shape[0]
    hs = shard // 2
    rows, cols = G.shape
    nr, nc = rows // LANES, cols // LANES
    full_rows, full_cols = rows * R, cols * C
    p_rows = 3 * tb // 8

    def at_offset(dz, dx):
        return rem(z + dz + Z, Z) * X + rem(x + dx + X, X)

    across = at_offset(0, 2)


    def part(first, unit, size):
        return pl.ds(pl.multiple_of(first, unit), size)

    ring_to = {("z", s): at_offset(s, 0) for s in (1, -1)} | {("x", s): at_offset(0, s) for s in (1, -1)}
    up, down = rem(y + 1, Y) * 2 + core, rem(y + Y - 1, Y) * 2 + core
    far, twin = rem(y + 2, Y) * 2 + core, y * 2 + 1 - core

    def whole(tile):
        return jnp.sum(tile, axis=(0, 1), keepdims=True)

    def from_far(length):
        return sorted(range(length), key=lambda d: -min(d, length - d))

    def to_twin(go):
        go((row, twin))

    def to_x(go):
        for dx in from_far(X)[:-1]:
            go((at_offset(0, dx), col))

    def to_z(go):
        for dz in from_far(Z)[:-1]:
            go((at_offset(dz, 0), col))

    def to_col(go):
        for dy in from_far(Y):
            for dc in (1, 0):
                if dy or dc:
                    go((row, rem(y + dy, Y) * 2 + rem(core + dc, 2)))

    def to_chips(go):
        def plane(a, carry):
            dz = Z // 2 + div(a + 1, 2) * (2 * rem(a, 2) - 1)
            for dx in from_far(X):
                for dy in from_far(Y):
                    to = at_offset(dz, dx), rem(y + dy, Y) * 2 + core
                    if dx or dy:
                        go(to)
                    else:
                        pl.when(a < Z - 1)(functools.partial(go, to))
            return carry
        lax.fori_loop(0, Z, plane, 0)

    barrier = pltpu.get_barrier_semaphore()
    for r in ring_to.values():
        pl.semaphore_signal(barrier, inc=1, device_id=(r, col), device_id_type=MESH)
    for c in (up, down, twin):
        pl.semaphore_signal(barrier, inc=1, device_id=(row, c), device_id_type=MESH)

    pl.semaphore_wait(barrier, 7)

    def extent(message):
        axis, sign, kind, off, hops = message
        first, size = (0, p_rows) if kind == "P" else (p_rows, tb - p_rows)
        if axis == "z" and kind == "P" and off == HOPS["x"] and hops < HOPS["z"] - 1:
            size += 16
        if axis == "x" and kind == "Q" and hops == HOPS["x"] - 1 and off != HOPS["z"]:
            first, size = first + 16, size - 16
        if hops == HOPS[axis] - 1:
            low = (size // 2 + 15) // 16 * 16
            low = size - low if off % 2 or off == HOPS["z"] else low
            return (first, low) if sign > 0 else (first + low, size - low)
        return first, size

    def placed(message, hops):
        axis, sign, _, off, _ = message
        dz, dx = (-sign * hops, off) if axis == "z" else (off, -sign * hops)
        first, size = extent(message)
        return B.at[part(at_offset(dz, dx) * tb + first, 16, size)]

    numbers = {}

    def ring(message, hops):
        axis, sign, _, off, made = message
        lane = 2 * (axis == "x") + (sign < 0)
        number = numbers.setdefault(message, sum(m[:2] == message[:2] for m in numbers))
        first, size = extent(message)
        there = placed(message, hops)
        return pltpu.make_async_remote_copy(
            src_ref=grads.at[pl.ds(first, size)] if made == 0 and off == 0 else there, dst_ref=there,
            send_sem=ring_send.at[lane], recv_sem=ring_recv.at[lane, number],
            device_id=(ring_to[axis, sign], col), device_id_type=MESH)

    def strip(owner):
        return pltpu.make_async_remote_copy(
            src_ref=grads.at[pl.ds(p_rows, 16)], dst_ref=B.at[part(owner * tb + p_rows, 16, 16)],
            send_sem=act_send.at[1], recv_sem=act_recv.at[11],
            device_id=(across, col), device_id_type=MESH)

    sent, landed = [], set()

    def await_messages(messages):
        for message in messages:
            if message not in landed:
                landed.add(message)
                ring(message, message[4] + 1).wait_recv()

    def brought(message):
        axis, sign, kind, off, hops = message
        if hops > 0:
            return [(axis, sign, kind, off, hops - 1)]
        if off == 0:
            return []
        other = "x" if axis == "z" else "z"
        last = HOPS[other] - 1
        if abs(off) == HOPS[other]:
            return [(other, 1, kind, 0, last), (other, -1, kind, 0, last)]
        return [(other, -1 if off > 0 else 1, kind, 0, abs(off) - 1)]

    def send(axis, kind, off, hops):
        mirrored = off if abs(off) == HOPS["x" if axis == "z" else "z"] else -off
        pair = [(axis, 1, kind, off, hops), (axis, -1, kind, mirrored, hops)]
        for message in pair:
            await_messages(brought(message))
            ring(message, hops).start()
            sent.append(message)

    def brings(message, dz):
        axis, sign, _, off, hops = message
        if axis == "x":
            return off == dz
        return dz == HOPS["z"] if hops == HOPS["z"] - 1 else dz == -sign * (hops + 1)

    def act(i, owner, first, size, to, src=None):
        there = A.at[part(owner * shard + first, hs, size)]
        return pltpu.make_async_remote_copy(
            src_ref=there if src is None else src, dst_ref=there,
            send_sem=act_send.at[0], recv_sem=act_recv.at[i],
            device_id=(row, to), device_id_type=MESH)

    low, high = acts.at[pl.ds(0, hs)], acts.at[pl.ds(hs, hs)]
    act_out = {
        0: act(0, col, 0, hs, up, low), 3: act(3, col, hs, hs, down, high),
        1: act(1, col, hs, hs, up, high), 4: act(4, col, 0, hs, down, low),
        6: act(6, col, 0, shard, twin, acts),
        2: act(2, down, 0, hs, up), 5: act(5, up, hs, hs, down),
        7: act(7, down, 0, shard, twin), 8: act(8, up, 0, shard, twin),
        9: act(9, far, 0, hs, twin), 10: act(10, far, hs, hs, twin),
    }
    swap = 1 - 2 * core
    act_in = {
        0: act(0, down, 0, hs, up), 1: act(1, down, hs, hs, up), 2: act(2, far, 0, hs, up),
        3: act(3, up, hs, hs, down), 4: act(4, up, 0, hs, down), 5: act(5, far, hs, hs, down),
        6: act(6, twin, 0, shard, twin), 7: act(7, down + swap, 0, shard, twin),
        8: act(8, up + swap, 0, shard, twin), 9: act(9, far + swap, 0, hs, twin),
        10: act(10, far + swap, hs, hs, twin),
    }
    act_steps = {
        "own low": ((), (0, 3, 6)), "own high": ((), (1, 4)), "near": ((0, 3), (2, 5)),
        "cross": ((1, 4), (7, 8)), "far": ((2, 5), (9, 10)), "all": ((6, 7, 8, 9, 10), ()),
        "strip": ((), ()), "strip out": ((), ()),
    }

    def fours(i):
        dz, odd = div(i + 1, 2) * (2 * rem(i, 2) - 1), div(i, 5)
        return (dz, 0), (dz, 1), (dz, 3), (dz - 6 * odd, 2 - 2 * odd)

    def twos(i):
        return (5 - 2 * rem(i, 2) + div(i, 3), 1 + div(i + 1, 2)), (5 - div(i + 2, 3), i - 1)

    def await_blocks(offsets):
        for dz, dx in offsets:
            dz, dx = (dz + Z // 2 - 1) % Z - Z // 2 + 1, (dx + 1) % X - 1
            await_messages([m for m in sent if brings(m, dz) and (
                m[3] == dx if m[0] == "z" else dx == -m[1] * (m[4] + 1) or (dx == 2 and m[4] == 1))])

    def add_products(blocks, order):
        def ahead(n):
            for message in order[n]:
                send(*message)
            await_blocks(static_blocks(blocks, n))

        def add(i, carry):
            for n in range(len(order)):
                pl.when(i == n)(functools.partial(ahead, n))
            tokens = [part(at_offset(dz, dx) * tb, tb, tb) for dz, dx in blocks(i)]
            G[...] += lax.dot_general(
                jnp.concatenate([A[t, :] for t in tokens], 0), jnp.concatenate([B[t, :] for t in tokens], 0),
                (((0,), (0,)), ((), ())), preferred_element_type=F32)
            return carry

        lax.fori_loop(0, len(order), add, 0)

    def static_blocks(blocks, n):
        if blocks is fours:
            dz, odd = (n + 1) // 2 * (2 * (n % 2) - 1), n // 5
            return (dz, 0), (dz, 1), (dz, 3), (dz - 6 * odd, 2 - 2 * odd)
        return (5 - 2 * (n % 2) + n // 3, 1 + (n + 1) // 2), (5 - (n + 2) // 3, n - 1)

    loads = [
        pltpu.make_async_copy(grads, B.at[part(row * tb, tb, tb)], load_sem.at[0]),
        pltpu.make_async_copy(acts, A.at[part(col * shard, shard, shard)], load_sem.at[1]),
        pltpu.make_async_copy(moment, M, load_sem.at[2]),
        pltpu.make_async_copy(row_state, states.at[0, pl.ds(0, nr)], load_sem.at[3]),
        pltpu.make_async_copy(col_state, states.at[1, pl.ds(0, nc)], load_sem.at[4]),
        pltpu.make_async_copy(row_conf, states.at[2, pl.ds(0, nr)], load_sem.at[5]),
        pltpu.make_async_copy(col_conf, states.at[3, pl.ds(0, nc)], load_sem.at[6]),
    ]
    for entry in ORDER:
        if isinstance(entry, str):
            arrive, leave = act_steps[entry]
            for i in arrive:
                act_in[i].wait_recv()
            for i in leave:
                act_out[i].start()
            if entry == "strip out":
                await_messages([("x", s, "P", 0, 1) for s in (1, -1)])
                strip(row).start()
            if entry == "strip":
                strip(across).wait_recv()
            if entry == "own low":
                states[...] = jnp.zeros_like(states)
                for load in loads:
                    load.start()
            if entry == "own high":
                loads[0].wait()
                loads[1].wait()
                G[...] = jnp.zeros_like(G)
        else:
            send(*entry)
    to_z(lambda to: pl.semaphore_signal(known.at[0], inc=1, device_id=to, device_id_type=MESH))
    for load in loads[2:]:
        load.wait()
    col_part[...] = jnp.zeros_like(col_part)
    row_part[...] = jnp.zeros_like(row_part)
    lane_ids = lax.broadcasted_iota(jnp.int32, (1, LANES), 1)
    states_sums = [whole(states[k]) for k in (0, 2)]
    add_products(fours, FOURS_ORDER)
    pl.semaphore_wait(known.at[0], Z - 1)
    to_x(lambda to: pl.semaphore_signal(known.at[1], inc=1, device_id=to, device_id_type=MESH))
    add_products(twos, TWOS_ORDER)
    pl.semaphore_wait(known.at[1], X - 1)
    def exchange(phase, src, got, slot, to_each, sems):
        send_sem, recv_sem = sems

        def copy(source, target, to):
            return pltpu.make_async_remote_copy(
                src_ref=source, dst_ref=target,
                send_sem=send_sem.at[phase], recv_sem=recv_sem.at[phase],
                device_id=to, device_id_type=MESH)

        others = got.at[phase, pl.ds(0, got.shape[1] - 1)]

        def start():
            to_each(lambda to: copy(src, got.at[phase, slot], to).start())
            got[phase, slot] = src[...]

        def result():
            copy(others, others, (row, twin)).wait_recv()
            return jnp.sum(got[phase], axis=0)

        def drain():
            copy(others, others, (row, twin)).wait_send()

        return start, result, drain

    def sums(block):
        def rows_of(i, col_sum):
            at = part(i * LANES, LANES, LANES)
            row_sum = jnp.zeros((LANES, LANES), F32)
            col_sums = []
            for j in range(nc):
                square = block(at, j)
                row_sum += square
                col_sums.append(jnp.sum(square.reshape(LANES // 8, 8, LANES), axis=0))
            row_sums[at, :] = row_sum
            return col_sum + jnp.concatenate(col_sums, 1)

        return lax.fori_loop(0, nr, rows_of, jnp.zeros((8, cols), F32))

    def reduced(phase, col_sum, beside, meanwhile):
        col_sums = [col_sum[:, j * LANES:(j + 1) * LANES] for j in range(nc)]
        values = whole(functools.reduce(jnp.add, col_sums))
        for lane, value in enumerate(beside):
            values = jnp.where(lane_ids == lane + 1, value, values)
        tot_part[phase] = jnp.broadcast_to(values, (1, LANES))
        by_twin = exchange(phase, tot_part.at[phase], tot_got, core, to_twin, (tot_send, tot_recv))
        by_twin[0]()
        for j in range(nc):
            col_part[phase, j:j + 1, :] = jnp.sum(col_sums[j], axis=0, keepdims=True)
        by_z = exchange(phase, col_part.at[phase], col_got, z, to_z, (col_send, col_recv))
        by_z[0]()
        for i in range(nr):
            turned = row_sums[i * LANES:(i + 1) * LANES, :].T
            row_part[phase, i:i + 1, :] = jnp.sum(turned, axis=0, keepdims=True)
        by_row = exchange(phase, row_part.at[phase], row_got, col, to_col, (row_send, row_recv))
        by_row[0]()
        all_part[phase] = by_twin[1]()
        by_all = exchange(phase, all_part.at[phase], all_got, row * Y + y, to_chips, (all_send, all_recv))
        by_all[0]()
        x_part[phase] = by_z[1]()
        by_x = exchange(phase, x_part.at[phase], x_got, x, to_x, (x_send, x_recv))
        by_x[0]()
        meanwhile()
        row_all = by_row[1]()
        col_all = by_x[1]()
        for one in (by_twin, by_z, by_row, by_x):
            one[2]()
        totals = by_all[1]()
        return row_all, col_all, totals, by_all[2]

    def down_rows(factors):
        for i in range(nr):
            row_scale[i * LANES:(i + 1) * LANES, :] = jnp.broadcast_to(factors[i:i + 1, :], (LANES, LANES)).T

    def squared(at, j):
        g = G[at, j * LANES:(j + 1) * LANES]
        return g * g

    def gather_drain():
        for lane, (axis, sign) in enumerate(ring_to):
            gone = sum(extent(m)[1] for m in sent if m[:2] == (axis, sign))
            gone = B.at[pl.ds(0, gone)]
            pltpu.make_async_remote_copy(
                src_ref=gone, dst_ref=gone, send_sem=ring_send.at[lane], recv_sem=ring_recv.at[lane, 0],
                device_id=(ring_to[axis, sign], col), device_id_type=MESH).wait_send()
        gone = A.at[pl.ds(0, 7 * shard)]
        pltpu.make_async_remote_copy(
            src_ref=gone, dst_ref=gone, send_sem=act_send.at[0], recv_sem=act_recv.at[0],
            device_id=(row, twin), device_id_type=MESH).wait_send()
        strip(row).wait_send()

    col_sum = sums(squared)
    row_all, col_all, totals, drain0 = reduced(0, col_sum, states_sums, gather_drain)
    total, row_state_sum, row_conf_sum = totals[:, 0:1], totals[:, 1:2] * (1.0 / C), totals[:, 2:3] * (1.0 / C)
    spread = jnp.minimum(1.0, (full_rows * full_cols) / (total + 1e-06))
    keep, fresh = second_decay, 1.0 - second_decay
    row_new = keep * states[0] + fresh * (spread * row_all * (1.0 / full_cols) + tiny_moment)
    col_new = keep * states[1] + fresh * (spread * col_all * (1.0 / full_rows) + tiny_moment)
    row_mean = keep * (row_state_sum * (1.0 / full_rows)) + fresh * (
        spread * total * (1.0 / (full_rows * full_cols)) + tiny_moment)
    down_rows(lax.rsqrt(row_new))
    packed[0] = row_new
    packed[1] = col_new
    col_scale = lax.rsqrt(col_new) * jnp.sqrt(spread * row_mean)

    def strays(at, j):
        here = (at, slice(j * LANES, (j + 1) * LANES))
        direction = G[here] * row_scale[at, :] * col_scale[j:j + 1, :]
        stray = direction - M[here]
        M[here] = M[here] + (1.0 - first_decay) * stray
        return stray * stray

    col_sum = sums(strays)
    row_all, col_all, totals, drain1 = reduced(1, col_sum, [], drain0)
    total = totals[:, 0:1]
    share = first_decay * first_decay
    row_conf_new = keep * states[2] + fresh * (row_all * (share / full_cols) + tiny_confidence)
    col_conf_new = keep * states[3] + fresh * (col_all * (share / full_rows) + tiny_confidence)
    conf_mean = keep * (row_conf_sum * (1.0 / full_rows)) + fresh * (
        total * (share / (full_rows * full_cols)) + tiny_confidence)
    packed[2] = row_conf_new
    packed[3] = col_conf_new
    packed[4] = lax.rsqrt(row_conf_new)
    packed[5] = lax.rsqrt(col_conf_new) * jnp.sqrt(conf_mean)
    drain1()


def finish(M, packed, moment_out, update_out, row_out, col_out, row_conf_out, col_conf_out, U, sem, block_sem):
    rows, cols = U.shape
    nr, nc = rows // LANES, cols // LANES
    stores = [pltpu.make_async_copy(M, moment_out, sem.at[0])]
    for k, (out, n) in enumerate(((row_out, nr), (col_out, nc), (row_conf_out, nr), (col_conf_out, nc))):
        stores.append(pltpu.make_async_copy(packed.at[k, pl.ds(0, n)], out, sem.at[1 + k]))
    for store in stores:
        store.start()

    def block_store(i):
        at = pl.ds(pl.multiple_of(i * LANES, LANES), LANES)
        return pltpu.make_async_copy(U.at[at], update_out.at[at], block_sem.at[i])

    def scale_block(i, carry):
        at = pl.ds(pl.multiple_of(i * LANES, LANES), LANES)
        scale = jnp.broadcast_to(packed[4, pl.ds(i, 1), :], (LANES, LANES)).T
        for j in range(nc):
            here = (at, slice(j * LANES, (j + 1) * LANES))
            U[here] = M[here] * scale * packed[5, j:j + 1, :]
        block_store(i).start()
        return carry

    def wait_block(i, carry):
        block_store(i).wait()
        return carry

    lax.fori_loop(0, nr, scale_block, 0)
    lax.fori_loop(0, nr, wait_block, 0)
    for store in stores:
        store.wait()


def on_device(acts, out_grads, moment, row_state, col_state, row_conf, col_conf):
    R, C = lax.axis_size("row"), lax.axis_size("col")
    rows, cols = moment.shape
    nr, nc = rows // LANES, cols // LANES
    dma = pltpu.SemaphoreType.DMA
    big = jax.ShapeDtypeStruct((rows, cols), F32)
    by_row, by_col = (jax.ShapeDtypeStruct((n, LANES), F32) for n in (nr, nc))
    in_hbm = pl.BlockSpec(memory_space=pltpu.HBM)
    in_vmem = pl.BlockSpec(memory_space=pltpu.VMEM)
    tokens = R * out_grads.shape[0]
    moment_new, packed = pl.pallas_call(
        functools.partial(kernel, R, C),
        out_shape=(pltpu.VMEM((rows, cols), F32), pltpu.VMEM((6, 8, LANES), F32)),
        in_specs=[in_hbm] * 7,
        out_specs=(in_vmem,) * 2,
        scratch_shapes=[
            pltpu.VMEM((tokens, rows), acts.dtype),
            pltpu.VMEM((tokens, cols), out_grads.dtype),
            pltpu.VMEM((rows, cols), F32),
            pltpu.VMEM((4, 8, LANES), F32),
            pltpu.VMEM((rows, LANES), F32),
            pltpu.VMEM((rows, LANES), F32),
            pltpu.VMEM((2, 8, LANES), F32),
            pltpu.VMEM((2, C, 8, LANES), F32),
            pltpu.VMEM((2, 8, LANES), F32),
            pltpu.VMEM((2, X, 8, LANES), F32),
            pltpu.VMEM((2, 8, LANES), F32),
            pltpu.VMEM((2, R // X, 8, LANES), F32),
            pltpu.VMEM((2, 1, LANES), F32),
            pltpu.VMEM((2, 2, 1, LANES), F32),
            pltpu.VMEM((2, 1, LANES), F32),
            pltpu.VMEM((2, R * C // 2, 1, LANES), F32),
            dma((4,)), dma((4, 20)), dma((2,)), dma((12,)), dma((7,)),
            *[dma((2,))] * 10, pltpu.SemaphoreType.REGULAR((2,)),
        ],
        compiler_params=pltpu.CompilerParams(
            collective_id=0, has_side_effects=True, vmem_limit_bytes=40 * 2**20),
        cost_estimate=pl.CostEstimate(
            flops=2 * tokens * rows * cols, transcendentals=0, bytes_accessed=30 * 2**20),
        name="came_step",
    )(*(pltpu.with_memory_space_constraint(v, pltpu.HBM) for v in (
        acts, out_grads, moment, row_state.reshape(nr, LANES), col_state.reshape(nc, LANES),
        row_conf.reshape(nr, LANES), col_conf.reshape(nc, LANES))))
    outs = pl.pallas_call(
        finish,
        out_shape=(big, big, by_row, by_col, by_row, by_col),
        in_specs=[in_vmem] * 2,
        out_specs=(in_hbm,) * 6,
        scratch_shapes=[pltpu.VMEM((rows, cols), F32), dma((5,)), dma((nr,))],
        compiler_params=pltpu.CompilerParams(vmem_limit_bytes=16 * 2**20),
        cost_estimate=pl.CostEstimate(
            flops=2 * rows * cols, transcendentals=0, bytes_accessed=12 * rows * cols),
        name="finish",
    )(moment_new, packed)
    return outs[0], outs[1], *(out.reshape(-1) for out in outs[2:])


def solution(mesh):
    placed = (
        P("col", "row"),
        P("row", "col"),
        P("row", "col"),
        P("row"),
        P("col"),
        P("row"),
        P("col"),
    )
    return jax.shard_map(
        on_device,
        mesh=mesh,
        in_specs=placed,
        out_specs=(P("row", "col"), P("row", "col"), P("row"), P("col"), P("row"), P("col")),
        check_vma=False,
    )
```

```python
import functools

import jax
import jax.numpy as jnp
from jax import lax
from jax.experimental import pallas as pl
from jax.experimental.pallas import tpu as pltpu
from jax.sharding import PartitionSpec as P

MESH = pl.DeviceIdType.MESH
F32 = jnp.float32
STEP = 10
X = 4
LANES = 128

first_decay = 0.9
tiny_moment = 1e-30
tiny_confidence = 1e-16
second_decay = 1.0 - STEP ** (-0.8)


ORDER = (
    ("z", "Q", 0, 0), ("x", "P", 0, 0), ("x", "Q", 0, 0), ("z", "P", 0, 0), "own low",
    ("z", "P", 1, 0), ("x", "P", 0, 1), ("x", "Q", 1, 0), ("z", "Q", 0, 1), "own high",
    ("x", "Q", -1, 0), ("z", "P", -1, 0), ("x", "Q", 0, 1), "strip out", ("z", "P", 0, 1),
    ("z", "Q", 0, 2), ("x", "Q", 2, 0), ("x", "Q", 1, 1), "strip", ("z", "P", 2, 0), "near",
    ("z", "P", 1, 1), ("x", "Q", -2, 0), ("x", "Q", -1, 1), ("z", "Q", 0, 3), ("z", "P", -1, 1),
    ("x", "Q", 3, 0), ("z", "P", 2, 1), "cross",
    ("x", "Q", 2, 1), ("x", "Q", -3, 0), ("z", "P", 0, 2), ("z", "P", 1, 2), ("x", "Q", -2, 1),
    ("z", "P", -1, 2), ("x", "Q", 4, 0), "far", ("z", "P", 2, 2), ("x", "Q", 3, 1), "all",
)
FOURS_ORDER = (
    (), (("z", "P", 0, 3),), (), (("x", "Q", -3, 1), ("z", "P", 1, 3)), (), (("z", "P", -1, 3),))
TWOS_ORDER = ((("x", "Q", 4, 1), ("z", "P", 2, 3)), (), (), ())
HOPS = {"z": 4, "x": 2}


def kernel(R, C, acts, grads, moment, row_state, col_state, row_conf, col_conf, M, packed,
           A, B, G, states, col_acc, row_sums, row_scale, row_part, row_got, col_part, x_got, x_part, col_got,
           tot_part, tot_got, all_part, all_got,
           ring_send, ring_recv, act_send, act_recv, load_sem,
           row_send, row_recv, x_send, x_recv, col_send, col_recv, tot_send, tot_recv, all_send, all_recv, known):
    Z, Y = R // X, C // 2
    row, col = lax.axis_index("row"), lax.axis_index("col")
    div, rem = lax.div, lax.rem
    z, x, y, core = div(row, X), rem(row, X), div(col, 2), rem(col, 2)
    tb, shard = grads.shape[0], acts.shape[0]
    hs = shard // 2
    rows, cols = G.shape
    nr, nc = rows // LANES, cols // LANES
    full_rows, full_cols = rows * R, cols * C
    p_rows = 3 * tb // 8

    def at_offset(dz, dx):
        return rem(z + dz + Z, Z) * X + rem(x + dx + X, X)

    across = at_offset(0, 2)


    def part(first, unit, size):
        return pl.ds(pl.multiple_of(first, unit), size)

    ring_to = {("z", s): at_offset(s, 0) for s in (1, -1)} | {("x", s): at_offset(0, s) for s in (1, -1)}
    up, down = rem(y + 1, Y) * 2 + core, rem(y + Y - 1, Y) * 2 + core
    far, twin = rem(y + 2, Y) * 2 + core, y * 2 + 1 - core

    def whole(tile):
        return jnp.sum(tile, axis=(0, 1), keepdims=True)

    def from_far(length):
        return sorted(range(length), key=lambda d: -min(d, length - d))

    def to_twin(go):
        go((row, twin))

    def to_x(go):
        for dx in from_far(X)[:-1]:
            go((at_offset(0, dx), col))

    def to_z(go):
        for dz in from_far(Z)[:-1]:
            go((at_offset(dz, 0), col))

    def to_col(go):
        for dy in from_far(Y):
            for dc in (1, 0):
                if dy or dc:
                    go((row, rem(y + dy, Y) * 2 + rem(core + dc, 2)))

    def to_chips(go):
        def plane(a, carry):
            dz = Z // 2 + div(a + 1, 2) * (2 * rem(a, 2) - 1)
            for dx in from_far(X):
                for dy in from_far(Y):
                    to = at_offset(dz, dx), rem(y + dy, Y) * 2 + core
                    if dx or dy:
                        go(to)
                    else:
                        pl.when(a < Z - 1)(functools.partial(go, to))
            return carry
        lax.fori_loop(0, Z, plane, 0)

    barrier = pltpu.get_barrier_semaphore()
    for r in ring_to.values():
        pl.semaphore_signal(barrier, inc=1, device_id=(r, col), device_id_type=MESH)
    for c in (up, down, twin):
        pl.semaphore_signal(barrier, inc=1, device_id=(row, c), device_id_type=MESH)

    loads = [
        pltpu.make_async_copy(grads, B.at[part(row * tb, tb, tb)], load_sem.at[0]),
        pltpu.make_async_copy(acts, A.at[part(col * shard, shard, shard)], load_sem.at[1]),
        pltpu.make_async_copy(moment, M, load_sem.at[2]),
        pltpu.make_async_copy(row_state, states.at[0, pl.ds(0, nr)], load_sem.at[3]),
        pltpu.make_async_copy(col_state, states.at[1, pl.ds(0, nc)], load_sem.at[4]),
        pltpu.make_async_copy(row_conf, states.at[2, pl.ds(0, nr)], load_sem.at[5]),
        pltpu.make_async_copy(col_conf, states.at[3, pl.ds(0, nc)], load_sem.at[6]),
    ]
    states[...] = jnp.zeros_like(states)
    for load in loads:
        load.start()
    pl.semaphore_wait(barrier, 7)

    def extent(message):
        axis, sign, kind, off, hops = message
        first, size = (0, p_rows) if kind == "P" else (p_rows, tb - p_rows)
        if axis == "z" and kind == "P" and off == HOPS["x"]:
            size += 16
        if axis == "x" and kind == "Q" and hops == HOPS["x"] - 1:
            first, size = first + 16, size - 16
        if hops == HOPS[axis] - 1:
            low = (size // 2 + 15) // 16 * 16
            low = size - low if off % 2 else low
            return (first, low) if sign > 0 else (first + low, size - low)
        return first, size

    def placed(message, hops):
        axis, sign, _, off, _ = message
        dz, dx = (-sign * hops, off) if axis == "z" else (off, -sign * hops)
        first, size = extent(message)
        return B.at[part(at_offset(dz, dx) * tb + first, 16, size)]

    numbers = {}

    def ring(message, hops):
        axis, sign, _, off, made = message
        lane = 2 * (axis == "x") + (sign < 0)
        number = numbers.setdefault(message, sum(m[:2] == message[:2] for m in numbers))
        first, size = extent(message)
        there = placed(message, hops)
        return pltpu.make_async_remote_copy(
            src_ref=grads.at[pl.ds(first, size)] if made == 0 and off == 0 else there, dst_ref=there,
            send_sem=ring_send.at[lane], recv_sem=ring_recv.at[lane, number],
            device_id=(ring_to[axis, sign], col), device_id_type=MESH)

    def strip(owner):
        return pltpu.make_async_remote_copy(
            src_ref=grads.at[pl.ds(p_rows, 16)], dst_ref=B.at[part(owner * tb + p_rows, 16, 16)],
            send_sem=act_send.at[1], recv_sem=act_recv.at[11],
            device_id=(across, col), device_id_type=MESH)

    sent, landed = [], set()

    def await_messages(messages):
        for message in messages:
            if message not in landed:
                landed.add(message)
                ring(message, message[4] + 1).wait_recv()

    def brought(message):
        axis, sign, kind, off, hops = message
        if hops > 0:
            return [(axis, sign, kind, off, hops - 1)]
        if off == 0:
            return []
        other = "x" if axis == "z" else "z"
        last = HOPS[other] - 1
        if abs(off) == HOPS[other]:
            return [(other, 1, kind, 0, last), (other, -1, kind, 0, last)]
        return [(other, -1 if off > 0 else 1, kind, 0, abs(off) - 1)]

    def send(axis, kind, off, hops):
        mirrored = off if abs(off) == HOPS["x" if axis == "z" else "z"] else -off
        pair = [(axis, 1, kind, off, hops), (axis, -1, kind, mirrored, hops)]
        for message in pair:
            await_messages(brought(message))
            ring(message, hops).start()
            sent.append(message)

    def brings(message, dz):
        axis, sign, _, off, hops = message
        if axis == "x":
            return off == dz
        return dz == HOPS["z"] if hops == HOPS["z"] - 1 else dz == -sign * (hops + 1)

    def act(i, owner, first, size, to, src=None):
        there = A.at[part(owner * shard + first, hs, size)]
        return pltpu.make_async_remote_copy(
            src_ref=there if src is None else src, dst_ref=there,
            send_sem=act_send.at[0], recv_sem=act_recv.at[i],
            device_id=(row, to), device_id_type=MESH)

    low, high = acts.at[pl.ds(0, hs)], acts.at[pl.ds(hs, hs)]
    act_out = {
        0: act(0, col, 0, hs, up, low), 3: act(3, col, hs, hs, down, high),
        1: act(1, col, hs, hs, up, high), 4: act(4, col, 0, hs, down, low),
        6: act(6, col, 0, shard, twin, acts),
        2: act(2, down, 0, hs, up), 5: act(5, up, hs, hs, down),
        7: act(7, down, 0, shard, twin), 8: act(8, up, 0, shard, twin),
        9: act(9, far, 0, hs, twin), 10: act(10, far, hs, hs, twin),
    }
    swap = 1 - 2 * core
    act_in = {
        0: act(0, down, 0, hs, up), 1: act(1, down, hs, hs, up), 2: act(2, far, 0, hs, up),
        3: act(3, up, hs, hs, down), 4: act(4, up, 0, hs, down), 5: act(5, far, hs, hs, down),
        6: act(6, twin, 0, shard, twin), 7: act(7, down + swap, 0, shard, twin),
        8: act(8, up + swap, 0, shard, twin), 9: act(9, far + swap, 0, hs, twin),
        10: act(10, far + swap, hs, hs, twin),
    }
    act_steps = {
        "own low": ((), (0, 3, 6)), "own high": ((), (1, 4)), "near": ((0, 3), (2, 5)),
        "cross": ((1, 4), (7, 8)), "far": ((2, 5), (9, 10)), "all": ((6, 7, 8, 9, 10), ()),
        "strip": ((), ()), "strip out": ((), ()),
    }

    def fours(i):
        dz, odd = div(i + 1, 2) * (2 * rem(i, 2) - 1), div(i, 5)
        return (dz, 0), (dz, 1), (dz, 3), (dz - 6 * odd, 2 - 2 * odd)

    def twos(i):
        return (5 - 2 * rem(i, 2) + div(i, 3), 1 + div(i + 1, 2)), (5 - div(i + 2, 3), i - 1)

    def await_blocks(offsets):
        for dz, dx in offsets:
            dz, dx = (dz + Z // 2 - 1) % Z - Z // 2 + 1, (dx + 1) % X - 1
            await_messages([m for m in sent if brings(m, dz) and (
                m[3] == dx if m[0] == "z" else dx == -m[1] * (m[4] + 1) or (dx == 2 and m[4] == 1))])

    def add_products(blocks, order):
        def ahead(n):
            for message in order[n]:
                send(*message)
            await_blocks(static_blocks(blocks, n))

        def add(i, carry):
            for n in range(len(order)):
                pl.when(i == n)(functools.partial(ahead, n))
            tokens = [part(at_offset(dz, dx) * tb, tb, tb) for dz, dx in blocks(i)]
            G[...] += lax.dot_general(
                jnp.concatenate([A[t, :] for t in tokens], 0), jnp.concatenate([B[t, :] for t in tokens], 0),
                (((0,), (0,)), ((), ())), preferred_element_type=F32)
            return carry

        lax.fori_loop(0, len(order), add, 0)

    def static_blocks(blocks, n):
        if blocks is fours:
            dz, odd = (n + 1) // 2 * (2 * (n % 2) - 1), n // 5
            return (dz, 0), (dz, 1), (dz, 3), (dz - 6 * odd, 2 - 2 * odd)
        return (5 - 2 * (n % 2) + n // 3, 1 + (n + 1) // 2), (5 - (n + 2) // 3, n - 1)

    for entry in ORDER:
        if isinstance(entry, str):
            arrive, leave = act_steps[entry]
            for i in arrive:
                act_in[i].wait_recv()
            for i in leave:
                act_out[i].start()
            if entry == "strip out":
                await_messages([("x", s, "P", 0, 1) for s in (1, -1)])
                strip(row).start()
            if entry == "strip":
                strip(across).wait_recv()
            if entry == "own high":
                loads[0].wait()
                loads[1].wait()
                G[...] = jnp.zeros_like(G)
        else:
            send(*entry)
    to_z(lambda to: pl.semaphore_signal(known.at[0], inc=1, device_id=to, device_id_type=MESH))
    for load in loads[2:]:
        load.wait()
    col_part[...] = jnp.zeros_like(col_part)
    row_part[...] = jnp.zeros_like(row_part)
    lane_ids = lax.broadcasted_iota(jnp.int32, (1, LANES), 1)
    states_sums = [whole(states[k]) for k in (0, 2)]
    add_products(fours, FOURS_ORDER)
    pl.semaphore_wait(known.at[0], Z - 1)
    to_x(lambda to: pl.semaphore_signal(known.at[1], inc=1, device_id=to, device_id_type=MESH))
    add_products(twos, TWOS_ORDER)
    pl.semaphore_wait(known.at[1], X - 1)
    def exchange(phase, src, got, slot, to_each, sems):
        send_sem, recv_sem = sems

        def copy(source, target, to):
            return pltpu.make_async_remote_copy(
                src_ref=source, dst_ref=target,
                send_sem=send_sem.at[phase], recv_sem=recv_sem.at[phase],
                device_id=to, device_id_type=MESH)

        others = got.at[phase, pl.ds(0, got.shape[1] - 1)]

        def start():
            to_each(lambda to: copy(src, got.at[phase, slot], to).start())
            got[phase, slot] = src[...]

        def result():
            copy(others, others, (row, twin)).wait_recv()
            return jnp.sum(got[phase], axis=0)

        def drain():
            copy(others, others, (row, twin)).wait_send()

        return start, result, drain

    def sums(block):
        def rows_of(i, col_sum):
            at = part(i * LANES, LANES, LANES)
            row_sum = jnp.zeros((LANES, LANES), F32)
            col_sums = []
            for j in range(nc):
                square = block(at, j)
                row_sum += square
                col_sums.append(jnp.sum(square.reshape(LANES // 8, 8, LANES), axis=0))
            row_sums[at, :] = row_sum
            return col_sum + jnp.concatenate(col_sums, 1)

        return lax.fori_loop(0, nr, rows_of, jnp.zeros((8, cols), F32))

    def squared(at, j):
        g = G[at, j * LANES:(j + 1) * LANES]
        return g * g

    def strays(at, j):
        here = (at, slice(j * LANES, (j + 1) * LANES))
        direction = G[here] * row_scale[at, :] * packed[5, j:j + 1, :]
        stray = direction - M[here]
        M[here] = M[here] + (1.0 - first_decay) * stray
        return stray * stray

    def gather_drain():
        for lane, (axis, sign) in enumerate(ring_to):
            gone = sum(extent(m)[1] for m in sent if m[:2] == (axis, sign))
            gone = B.at[pl.ds(0, gone)]
            pltpu.make_async_remote_copy(
                src_ref=gone, dst_ref=gone, send_sem=ring_send.at[lane], recv_sem=ring_recv.at[lane, 0],
                device_id=(ring_to[axis, sign], col), device_id_type=MESH).wait_send()
        gone = A.at[pl.ds(0, 7 * shard)]
        pltpu.make_async_remote_copy(
            src_ref=gone, dst_ref=gone, send_sem=act_send.at[0], recv_sem=act_recv.at[0],
            device_id=(row, twin), device_id_type=MESH).wait_send()
        strip(row).wait_send()

    def factors(phase, carry):
        first = phase == 0

        def first_sums():
            col_acc[...] = sums(squared)

        def second_sums():
            col_acc[...] = sums(strays)

        pl.when(first)(first_sums)
        pl.when(phase == 1)(second_sums)
        col_sums = [col_acc[:, j * LANES:(j + 1) * LANES] for j in range(nc)]
        values = whole(functools.reduce(jnp.add, col_sums))
        for lane, value in enumerate(states_sums):
            values = jnp.where(lane_ids == lane + 1, value, values)
        tot_part[phase] = values
        by_twin = exchange(phase, tot_part.at[phase], tot_got, core, to_twin, (tot_send, tot_recv))
        by_twin[0]()
        for j in range(nc):
            col_part[phase, j:j + 1, :] = jnp.sum(col_sums[j], axis=0, keepdims=True)
        by_z = exchange(phase, col_part.at[phase], col_got, z, to_z, (col_send, col_recv))
        by_z[0]()
        for i in range(nr):
            turned = row_sums[i * LANES:(i + 1) * LANES, :].T
            row_part[phase, i:i + 1, :] = jnp.sum(turned, axis=0, keepdims=True)
        by_row = exchange(phase, row_part.at[phase], row_got, col, to_col, (row_send, row_recv))
        by_row[0]()
        all_part[phase] = by_twin[1]()
        by_all = exchange(phase, all_part.at[phase], all_got, row * Y + y, to_chips, (all_send, all_recv))
        by_all[0]()
        x_part[phase] = by_z[1]()
        by_x = exchange(phase, x_part.at[phase], x_got, x, to_x, (x_send, x_recv))
        by_x[0]()
        pl.when(first)(gather_drain)
        row_all = by_row[1]()
        col_all = by_x[1]()
        for one in (by_twin, by_z, by_row, by_x):
            one[2]()
        totals = by_all[1]()
        total = totals[:, 0:1]
        state_sum = jnp.where(first, totals[:, 1:2], totals[:, 2:3]) * (1.0 / C)
        clipped = jnp.minimum(1.0, (full_rows * full_cols) / (total + 1e-06))
        share = jnp.where(first, clipped, first_decay * first_decay)
        tiny = jnp.where(first, tiny_moment, tiny_confidence)
        keep, fresh = second_decay, 1.0 - second_decay
        row_new = keep * states[2 * phase] + fresh * (share * row_all * (1.0 / full_cols) + tiny)
        col_new = keep * states[2 * phase + 1] + fresh * (share * col_all * (1.0 / full_rows) + tiny)
        mean = keep * (state_sum * (1.0 / full_rows)) + fresh * (
            share * total * (1.0 / (full_rows * full_cols)) + tiny)
        row_root = lax.rsqrt(row_new)

        def turn():
            for i in range(nr):
                row_scale[i * LANES:(i + 1) * LANES, :] = jnp.broadcast_to(
                    row_root[i:i + 1, :], (LANES, LANES)).T

        pl.when(first)(turn)
        packed[2 * phase] = row_new
        packed[2 * phase + 1] = col_new
        packed[4] = row_root
        packed[5] = lax.rsqrt(col_new) * jnp.sqrt(jnp.where(first, clipped, 1.0) * mean)
        by_all[2]()
        return carry

    lax.fori_loop(0, 2, factors, 0)


def finish(M, packed, moment_out, update_out, row_out, col_out, row_conf_out, col_conf_out, U, sem, block_sem):
    rows, cols = U.shape
    nr, nc = rows // LANES, cols // LANES
    stores = [pltpu.make_async_copy(M, moment_out, sem.at[0])]
    for k, (out, n) in enumerate(((row_out, nr), (col_out, nc), (row_conf_out, nr), (col_conf_out, nc))):
        stores.append(pltpu.make_async_copy(packed.at[k, pl.ds(0, n)], out, sem.at[1 + k]))
    for store in stores:
        store.start()

    def block_store(i):
        at = pl.ds(pl.multiple_of(i * LANES, LANES), LANES)
        return pltpu.make_async_copy(U.at[at], update_out.at[at], block_sem.at[i])

    def scale_block(i, carry):
        at = pl.ds(pl.multiple_of(i * LANES, LANES), LANES)
        scale = jnp.broadcast_to(packed[4, pl.ds(i, 1), :], (LANES, LANES)).T
        for j in range(nc):
            here = (at, slice(j * LANES, (j + 1) * LANES))
            U[here] = M[here] * scale * packed[5, j:j + 1, :]
        block_store(i).start()
        return carry

    def wait_block(i, carry):
        block_store(i).wait()
        return carry

    lax.fori_loop(0, nr, scale_block, 0)
    lax.fori_loop(0, nr, wait_block, 0)
    for store in stores:
        store.wait()


def on_device(acts, out_grads, moment, row_state, col_state, row_conf, col_conf):
    R, C = lax.axis_size("row"), lax.axis_size("col")
    rows, cols = moment.shape
    nr, nc = rows // LANES, cols // LANES
    dma = pltpu.SemaphoreType.DMA
    big = jax.ShapeDtypeStruct((rows, cols), F32)
    by_row, by_col = (jax.ShapeDtypeStruct((n, LANES), F32) for n in (nr, nc))
    in_hbm = pl.BlockSpec(memory_space=pltpu.HBM)
    in_vmem = pl.BlockSpec(memory_space=pltpu.VMEM)
    tokens = R * out_grads.shape[0]
    moment_new, packed = pl.pallas_call(
        functools.partial(kernel, R, C),
        out_shape=(pltpu.VMEM((rows, cols), F32), pltpu.VMEM((6, 8, LANES), F32)),
        in_specs=[in_hbm] * 7,
        out_specs=(in_vmem,) * 2,
        scratch_shapes=[
            pltpu.VMEM((tokens, rows), acts.dtype),
            pltpu.VMEM((tokens, cols), out_grads.dtype),
            pltpu.VMEM((rows, cols), F32),
            pltpu.VMEM((4, 8, LANES), F32),
            pltpu.VMEM((8, cols), F32),
            pltpu.VMEM((rows, LANES), F32),
            pltpu.VMEM((rows, LANES), F32),
            pltpu.VMEM((2, 8, LANES), F32),
            pltpu.VMEM((2, C, 8, LANES), F32),
            pltpu.VMEM((2, 8, LANES), F32),
            pltpu.VMEM((2, X, 8, LANES), F32),
            pltpu.VMEM((2, 8, LANES), F32),
            pltpu.VMEM((2, R // X, 8, LANES), F32),
            pltpu.VMEM((2, 1, LANES), F32),
            pltpu.VMEM((2, 2, 1, LANES), F32),
            pltpu.VMEM((2, 1, LANES), F32),
            pltpu.VMEM((2, R * C // 2, 1, LANES), F32),
            dma((4,)), dma((4, 20)), dma((2,)), dma((12,)), dma((7,)),
            *[dma((2,))] * 10, pltpu.SemaphoreType.REGULAR((2,)),
        ],
        compiler_params=pltpu.CompilerParams(
            collective_id=0, has_side_effects=True, vmem_limit_bytes=40 * 2**20),
        cost_estimate=pl.CostEstimate(
            flops=2 * tokens * rows * cols, transcendentals=0, bytes_accessed=30 * 2**20),
        name="came_step",
    )(*(pltpu.with_memory_space_constraint(v, pltpu.HBM) for v in (
        acts, out_grads, moment, row_state.reshape(nr, LANES), col_state.reshape(nc, LANES),
        row_conf.reshape(nr, LANES), col_conf.reshape(nc, LANES))))
    outs = pl.pallas_call(
        finish,
        out_shape=(big, big, by_row, by_col, by_row, by_col),
        in_specs=[in_vmem] * 2,
        out_specs=(in_hbm,) * 6,
        scratch_shapes=[pltpu.VMEM((rows, cols), F32), dma((5,)), dma((nr,))],
        compiler_params=pltpu.CompilerParams(vmem_limit_bytes=16 * 2**20),
        cost_estimate=pl.CostEstimate(
            flops=2 * rows * cols, transcendentals=0, bytes_accessed=12 * rows * cols),
        name="finish",
    )(moment_new, packed)
    return outs[0], outs[1], *(out.reshape(-1) for out in outs[2:])


def solution(mesh):
    placed = (
        P("col", "row"),
        P("row", "col"),
        P("row", "col"),
        P("row"),
        P("col"),
        P("row"),
        P("col"),
    )
    return jax.shard_map(
        on_device,
        mesh=mesh,
        in_specs=placed,
        out_specs=(P("row", "col"), P("row", "col"), P("row"), P("col"), P("row"), P("col")),
        check_vma=False,
    )
```

```python
import functools

import jax
import jax.numpy as jnp
from jax import lax
from jax.experimental import pallas as pl
from jax.experimental.pallas import tpu as pltpu
from jax.sharding import PartitionSpec as P

MESH = pl.DeviceIdType.MESH
F32 = jnp.float32
STEP = 10
X = 4
LANES = 128

first_decay = 0.9
tiny_moment = 1e-30
tiny_confidence = 1e-16
second_decay = 1.0 - STEP ** (-0.8)


ORDER = (
    ("z", "Q", 0, 0), ("x", "P", 0, 0), ("x", "Q", 0, 0), ("z", "P", 0, 0), "own low",
    ("z", "P", 1, 0), ("x", "P", 0, 1), ("x", "Q", 1, 0), ("z", "Q", 0, 1), "own high",
    ("x", "Q", -1, 0), ("z", "P", -1, 0), ("x", "Q", 0, 1), "strip out", ("z", "P", 0, 1),
    ("z", "Q", 0, 2), ("x", "Q", 2, 0), ("x", "Q", 1, 1), "strip", ("z", "P", 2, 0), "near",
    ("z", "P", 1, 1), ("x", "Q", -2, 0), ("x", "Q", -1, 1), ("z", "Q", 0, 3), ("z", "P", -1, 1),
    ("x", "Q", 3, 0), ("z", "P", 2, 1), "cross",
    ("x", "Q", 2, 1), ("x", "Q", -3, 0), ("z", "P", 0, 2), ("z", "P", 1, 2), ("x", "Q", -2, 1),
    ("z", "P", -1, 2), ("x", "Q", 4, 0), "far", ("z", "P", 2, 2), ("x", "Q", 3, 1), "all",
)
FOURS_ORDER = (
    (), (("z", "P", 0, 3),), (), (("x", "Q", -3, 1), ("z", "P", 1, 3)), (), (("z", "P", -1, 3),))
TWOS_ORDER = ((("x", "Q", 4, 1), ("z", "P", 2, 3)), (), (), ())
HOPS = {"z": 4, "x": 2}


def kernel(R, C, acts, grads, moment, row_state, col_state, row_conf, col_conf, M, packed,
           A, B, G, states, row_sums, row_scale, row_part, row_got, col_part, x_got, x_part, col_got,
           tot_part, tot_got, all_part, all_got,
           ring_send, ring_recv, act_send, act_recv, load_sem,
           row_send, row_recv, x_send, x_recv, col_send, col_recv, tot_send, tot_recv, all_send, all_recv, known):
    Z, Y = R // X, C // 2
    row, col = lax.axis_index("row"), lax.axis_index("col")
    div, rem = lax.div, lax.rem
    z, x, y, core = div(row, X), rem(row, X), div(col, 2), rem(col, 2)
    tb, shard = grads.shape[0], acts.shape[0]
    hs = shard // 2
    rows, cols = G.shape
    nr, nc = rows // LANES, cols // LANES
    full_rows, full_cols = rows * R, cols * C
    p_rows = 3 * tb // 8

    def at_offset(dz, dx):
        return rem(z + dz + Z, Z) * X + rem(x + dx + X, X)

    across = at_offset(0, 2)


    def part(first, unit, size):
        return pl.ds(pl.multiple_of(first, unit), size)

    ring_to = {("z", s): at_offset(s, 0) for s in (1, -1)} | {("x", s): at_offset(0, s) for s in (1, -1)}
    up, down = rem(y + 1, Y) * 2 + core, rem(y + Y - 1, Y) * 2 + core
    far, twin = rem(y + 2, Y) * 2 + core, y * 2 + 1 - core

    def whole(tile):
        return jnp.sum(tile, axis=(0, 1), keepdims=True)

    def from_far(length):
        return sorted(range(length), key=lambda d: -min(d, length - d))

    def to_twin(go):
        go((row, twin))

    def to_x(go):
        for dx in from_far(X)[:-1]:
            go((at_offset(0, dx), col))

    def to_z(go):
        for dz in from_far(Z)[:-1]:
            go((at_offset(dz, 0), col))

    def to_col(go):
        for dy in from_far(Y):
            for dc in (1, 0):
                if dy or dc:
                    go((row, rem(y + dy, Y) * 2 + rem(core + dc, 2)))

    def to_chips(go):
        def plane(a, carry):
            dz = Z // 2 + div(a + 1, 2) * (2 * rem(a, 2) - 1)
            for dx in from_far(X):
                for dy in from_far(Y):
                    to = at_offset(dz, dx), rem(y + dy, Y) * 2 + core
                    if dx or dy:
                        go(to)
                    else:
                        pl.when(a < Z - 1)(functools.partial(go, to))
            return carry
        lax.fori_loop(0, Z, plane, 0)

    barrier = pltpu.get_barrier_semaphore()
    for r in ring_to.values():
        pl.semaphore_signal(barrier, inc=1, device_id=(r, col), device_id_type=MESH)
    for c in (up, down, twin):
        pl.semaphore_signal(barrier, inc=1, device_id=(row, c), device_id_type=MESH)

    loads = [
        pltpu.make_async_copy(grads, B.at[part(row * tb, tb, tb)], load_sem.at[0]),
        pltpu.make_async_copy(acts, A.at[part(col * shard, shard, shard)], load_sem.at[1]),
        pltpu.make_async_copy(moment, M, load_sem.at[2]),
        pltpu.make_async_copy(row_state, states.at[0, pl.ds(0, nr)], load_sem.at[3]),
        pltpu.make_async_copy(col_state, states.at[1, pl.ds(0, nc)], load_sem.at[4]),
        pltpu.make_async_copy(row_conf, states.at[2, pl.ds(0, nr)], load_sem.at[5]),
        pltpu.make_async_copy(col_conf, states.at[3, pl.ds(0, nc)], load_sem.at[6]),
    ]
    states[...] = jnp.zeros_like(states)
    for load in loads:
        load.start()
    pl.semaphore_wait(barrier, 7)

    def extent(message):
        axis, sign, kind, off, hops = message
        first, size = (0, p_rows) if kind == "P" else (p_rows, tb - p_rows)
        if axis == "z" and kind == "P" and off == HOPS["x"]:
            size += 16
        if axis == "x" and kind == "Q" and hops == HOPS["x"] - 1:
            first, size = first + 16, size - 16
        if hops == HOPS[axis] - 1:
            low = (size // 2 + 15) // 16 * 16
            low = size - low if off % 2 else low
            return (first, low) if sign > 0 else (first + low, size - low)
        return first, size

    def placed(message, hops):
        axis, sign, _, off, _ = message
        dz, dx = (-sign * hops, off) if axis == "z" else (off, -sign * hops)
        first, size = extent(message)
        return B.at[part(at_offset(dz, dx) * tb + first, 16, size)]

    numbers = {}

    def ring(message, hops):
        axis, sign, _, off, made = message
        lane = 2 * (axis == "x") + (sign < 0)
        number = numbers.setdefault(message, sum(m[:2] == message[:2] for m in numbers))
        first, size = extent(message)
        there = placed(message, hops)
        return pltpu.make_async_remote_copy(
            src_ref=grads.at[pl.ds(first, size)] if made == 0 and off == 0 else there, dst_ref=there,
            send_sem=ring_send.at[lane], recv_sem=ring_recv.at[lane, number],
            device_id=(ring_to[axis, sign], col), device_id_type=MESH)

    def strip(owner):
        return pltpu.make_async_remote_copy(
            src_ref=grads.at[pl.ds(p_rows, 16)], dst_ref=B.at[part(owner * tb + p_rows, 16, 16)],
            send_sem=act_send.at[1], recv_sem=act_recv.at[11],
            device_id=(across, col), device_id_type=MESH)

    sent, landed = [], set()

    def await_messages(messages):
        for message in messages:
            if message not in landed:
                landed.add(message)
                ring(message, message[4] + 1).wait_recv()

    def brought(message):
        axis, sign, kind, off, hops = message
        if hops > 0:
            return [(axis, sign, kind, off, hops - 1)]
        if off == 0:
            return []
        other = "x" if axis == "z" else "z"
        last = HOPS[other] - 1
        if abs(off) == HOPS[other]:
            return [(other, 1, kind, 0, last), (other, -1, kind, 0, last)]
        return [(other, -1 if off > 0 else 1, kind, 0, abs(off) - 1)]

    def send(axis, kind, off, hops):
        mirrored = off if abs(off) == HOPS["x" if axis == "z" else "z"] else -off
        pair = [(axis, 1, kind, off, hops), (axis, -1, kind, mirrored, hops)]
        for message in pair:
            await_messages(brought(message))
            ring(message, hops).start()
            sent.append(message)

    def brings(message, dz):
        axis, sign, _, off, hops = message
        if axis == "x":
            return off == dz
        return dz == HOPS["z"] if hops == HOPS["z"] - 1 else dz == -sign * (hops + 1)

    def act(i, owner, first, size, to, src=None):
        there = A.at[part(owner * shard + first, hs, size)]
        return pltpu.make_async_remote_copy(
            src_ref=there if src is None else src, dst_ref=there,
            send_sem=act_send.at[0], recv_sem=act_recv.at[i],
            device_id=(row, to), device_id_type=MESH)

    low, high = acts.at[pl.ds(0, hs)], acts.at[pl.ds(hs, hs)]
    act_out = {
        0: act(0, col, 0, hs, up, low), 3: act(3, col, hs, hs, down, high),
        1: act(1, col, hs, hs, up, high), 4: act(4, col, 0, hs, down, low),
        6: act(6, col, 0, shard, twin, acts),
        2: act(2, down, 0, hs, up), 5: act(5, up, hs, hs, down),
        7: act(7, down, 0, shard, twin), 8: act(8, up, 0, shard, twin),
        9: act(9, far, 0, hs, twin), 10: act(10, far, hs, hs, twin),
    }
    swap = 1 - 2 * core
    act_in = {
        0: act(0, down, 0, hs, up), 1: act(1, down, hs, hs, up), 2: act(2, far, 0, hs, up),
        3: act(3, up, hs, hs, down), 4: act(4, up, 0, hs, down), 5: act(5, far, hs, hs, down),
        6: act(6, twin, 0, shard, twin), 7: act(7, down + swap, 0, shard, twin),
        8: act(8, up + swap, 0, shard, twin), 9: act(9, far + swap, 0, hs, twin),
        10: act(10, far + swap, hs, hs, twin),
    }
    act_steps = {
        "own low": ((), (0, 3, 6)), "own high": ((), (1, 4)), "near": ((0, 3), (2, 5)),
        "cross": ((1, 4), (7, 8)), "far": ((2, 5), (9, 10)), "all": ((6, 7, 8, 9, 10), ()),
        "strip": ((), ()), "strip out": ((), ()),
    }

    def fours(i):
        dz, odd = div(i + 1, 2) * (2 * rem(i, 2) - 1), div(i, 5)
        return (dz, 0), (dz, 1), (dz, 3), (dz - 6 * odd, 2 - 2 * odd)

    def twos(i):
        return (5 - 2 * rem(i, 2) + div(i, 3), 1 + div(i + 1, 2)), (5 - div(i + 2, 3), i - 1)

    def await_blocks(offsets):
        for dz, dx in offsets:
            dz, dx = (dz + Z // 2 - 1) % Z - Z // 2 + 1, (dx + 1) % X - 1
            await_messages([m for m in sent if brings(m, dz) and (
                m[3] == dx if m[0] == "z" else dx == -m[1] * (m[4] + 1) or (dx == 2 and m[4] == 1))])

    def add_products(blocks, order):
        def ahead(n):
            for message in order[n]:
                send(*message)
            await_blocks(static_blocks(blocks, n))

        def add(i, carry):
            for n in range(len(order)):
                pl.when(i == n)(functools.partial(ahead, n))
            tokens = [part(at_offset(dz, dx) * tb, tb, tb) for dz, dx in blocks(i)]
            G[...] += lax.dot_general(
                jnp.concatenate([A[t, :] for t in tokens], 0), jnp.concatenate([B[t, :] for t in tokens], 0),
                (((0,), (0,)), ((), ())), preferred_element_type=F32)
            return carry

        lax.fori_loop(0, len(order), add, 0)

    def static_blocks(blocks, n):
        if blocks is fours:
            dz, odd = (n + 1) // 2 * (2 * (n % 2) - 1), n // 5
            return (dz, 0), (dz, 1), (dz, 3), (dz - 6 * odd, 2 - 2 * odd)
        return (5 - 2 * (n % 2) + n // 3, 1 + (n + 1) // 2), (5 - (n + 2) // 3, n - 1)

    for entry in ORDER:
        if isinstance(entry, str):
            arrive, leave = act_steps[entry]
            for i in arrive:
                act_in[i].wait_recv()
            for i in leave:
                act_out[i].start()
            if entry == "strip out":
                await_messages([("x", s, "P", 0, 1) for s in (1, -1)])
                strip(row).start()
            if entry == "strip":
                strip(across).wait_recv()
            if entry == "own high":
                loads[0].wait()
                loads[1].wait()
                G[...] = jnp.zeros_like(G)
        else:
            send(*entry)
    to_z(lambda to: pl.semaphore_signal(known.at[0], inc=1, device_id=to, device_id_type=MESH))
    for load in loads[2:]:
        load.wait()
    col_part[...] = jnp.zeros_like(col_part)
    row_part[...] = jnp.zeros_like(row_part)
    row_sums[...] = jnp.zeros_like(row_sums)
    lane_ids = lax.broadcasted_iota(jnp.int32, (1, LANES), 1)
    states_sums = [whole(states[k]) for k in (0, 2)]
    add_products(fours, FOURS_ORDER)
    pl.semaphore_wait(known.at[0], Z - 1)
    to_x(lambda to: pl.semaphore_signal(known.at[1], inc=1, device_id=to, device_id_type=MESH))
    add_products(twos, TWOS_ORDER)
    pl.semaphore_wait(known.at[1], X - 1)
    def exchange(phase, src, got, slot, to_each, sems):
        send_sem, recv_sem = sems

        def copy(source, target, to):
            return pltpu.make_async_remote_copy(
                src_ref=source, dst_ref=target,
                send_sem=send_sem.at[phase], recv_sem=recv_sem.at[phase],
                device_id=to, device_id_type=MESH)

        others = got.at[phase, pl.ds(0, got.shape[1] - 1)]

        def start():
            to_each(lambda to: copy(src, got.at[phase, slot], to).start())
            got[phase, slot] = src[...]

        def result():
            copy(others, others, (row, twin)).wait_recv()
            return jnp.sum(got[phase], axis=0)

        def drain():
            copy(others, others, (row, twin)).wait_send()

        return start, result, drain

    def turn_sums(phase, i):
        turned = row_sums[part(i * LANES, LANES, LANES), :].T
        row_part[phase, pl.ds(i, 1), :] = jnp.sum(turned, axis=0, keepdims=True)

    def sums(phase, block):
        def rows_of(i, col_sum):
            at = part(i * LANES, LANES, LANES)
            turn_sums(phase, jnp.maximum(i - 1, 0))
            row_sum = jnp.zeros((LANES, LANES), F32)
            col_sums = []
            for j in range(nc):
                square = block(at, j)
                row_sum += square
                col_sums.append(jnp.sum(square.reshape(LANES // 8, 8, LANES), axis=0))
            row_sums[at, :] = row_sum
            return col_sum + jnp.concatenate(col_sums, 1)

        return lax.fori_loop(0, nr, rows_of, jnp.zeros((8, cols), F32))

    def reduced(phase, col_sum, beside, meanwhile):
        col_sums = [col_sum[:, j * LANES:(j + 1) * LANES] for j in range(nc)]
        values = whole(functools.reduce(jnp.add, col_sums))
        for lane, value in enumerate(beside):
            values = jnp.where(lane_ids == lane + 1, value, values)
        tot_part[phase] = jnp.broadcast_to(values, (1, LANES))
        by_twin = exchange(phase, tot_part.at[phase], tot_got, core, to_twin, (tot_send, tot_recv))
        by_twin[0]()
        for j in range(nc):
            col_part[phase, j:j + 1, :] = jnp.sum(col_sums[j], axis=0, keepdims=True)
        by_z = exchange(phase, col_part.at[phase], col_got, z, to_z, (col_send, col_recv))
        by_z[0]()
        turn_sums(phase, nr - 1)
        by_row = exchange(phase, row_part.at[phase], row_got, col, to_col, (row_send, row_recv))
        by_row[0]()
        all_part[phase] = by_twin[1]()
        by_all = exchange(phase, all_part.at[phase], all_got, row * Y + y, to_chips, (all_send, all_recv))
        by_all[0]()
        x_part[phase] = by_z[1]()
        by_x = exchange(phase, x_part.at[phase], x_got, x, to_x, (x_send, x_recv))
        by_x[0]()
        meanwhile()
        row_all = by_row[1]()
        col_all = by_x[1]()
        for one in (by_twin, by_z, by_row, by_x):
            one[2]()
        totals = by_all[1]()
        return row_all, col_all, totals, by_all[2]

    def down_rows(factors):
        for i in range(nr):
            row_scale[i * LANES:(i + 1) * LANES, :] = jnp.broadcast_to(factors[i:i + 1, :], (LANES, LANES)).T

    def squared(at, j):
        g = G[at, j * LANES:(j + 1) * LANES]
        return g * g

    def gather_drain():
        for lane, (axis, sign) in enumerate(ring_to):
            gone = sum(extent(m)[1] for m in sent if m[:2] == (axis, sign))
            gone = B.at[pl.ds(0, gone)]
            pltpu.make_async_remote_copy(
                src_ref=gone, dst_ref=gone, send_sem=ring_send.at[lane], recv_sem=ring_recv.at[lane, 0],
                device_id=(ring_to[axis, sign], col), device_id_type=MESH).wait_send()
        gone = A.at[pl.ds(0, 7 * shard)]
        pltpu.make_async_remote_copy(
            src_ref=gone, dst_ref=gone, send_sem=act_send.at[0], recv_sem=act_recv.at[0],
            device_id=(row, twin), device_id_type=MESH).wait_send()
        strip(row).wait_send()

    col_sum = sums(0, squared)
    row_all, col_all, totals, drain0 = reduced(0, col_sum, states_sums, gather_drain)
    total, row_state_sum, row_conf_sum = totals[:, 0:1], totals[:, 1:2] * (1.0 / C), totals[:, 2:3] * (1.0 / C)
    spread = jnp.minimum(1.0, (full_rows * full_cols) / (total + 1e-06))
    keep, fresh = second_decay, 1.0 - second_decay
    row_new = keep * states[0] + fresh * (spread * row_all * (1.0 / full_cols) + tiny_moment)
    col_new = keep * states[1] + fresh * (spread * col_all * (1.0 / full_rows) + tiny_moment)
    row_mean = keep * (row_state_sum * (1.0 / full_rows)) + fresh * (
        spread * total * (1.0 / (full_rows * full_cols)) + tiny_moment)
    down_rows(lax.rsqrt(row_new))
    packed[0] = row_new
    packed[1] = col_new
    col_scale = lax.rsqrt(col_new) * jnp.sqrt(spread * row_mean)

    def strays(at, j):
        here = (at, slice(j * LANES, (j + 1) * LANES))
        direction = G[here] * row_scale[at, :] * col_scale[j:j + 1, :]
        stray = direction - M[here]
        M[here] = M[here] + (1.0 - first_decay) * stray
        return stray * stray

    col_sum = sums(1, strays)
    row_all, col_all, totals, drain1 = reduced(1, col_sum, [], drain0)
    total = totals[:, 0:1]
    share = first_decay * first_decay
    row_conf_new = keep * states[2] + fresh * (row_all * (share / full_cols) + tiny_confidence)
    col_conf_new = keep * states[3] + fresh * (col_all * (share / full_rows) + tiny_confidence)
    conf_mean = keep * (row_conf_sum * (1.0 / full_rows)) + fresh * (
        total * (share / (full_rows * full_cols)) + tiny_confidence)
    packed[2] = row_conf_new
    packed[3] = col_conf_new
    packed[4] = lax.rsqrt(row_conf_new)
    packed[5] = lax.rsqrt(col_conf_new) * jnp.sqrt(conf_mean)
    drain1()


def finish(M, packed, moment_out, update_out, row_out, col_out, row_conf_out, col_conf_out, U, sem, block_sem):
    rows, cols = U.shape
    nr, nc = rows // LANES, cols // LANES
    stores = [pltpu.make_async_copy(M, moment_out, sem.at[0])]
    for k, (out, n) in enumerate(((row_out, nr), (col_out, nc), (row_conf_out, nr), (col_conf_out, nc))):
        stores.append(pltpu.make_async_copy(packed.at[k, pl.ds(0, n)], out, sem.at[1 + k]))
    for store in stores:
        store.start()

    def block_store(i):
        at = pl.ds(pl.multiple_of(i * LANES, LANES), LANES)
        return pltpu.make_async_copy(U.at[at], update_out.at[at], block_sem.at[i])

    def scale_block(i, carry):
        at = pl.ds(pl.multiple_of(i * LANES, LANES), LANES)
        scale = jnp.broadcast_to(packed[4, pl.ds(i, 1), :], (LANES, LANES)).T
        for j in range(nc):
            here = (at, slice(j * LANES, (j + 1) * LANES))
            U[here] = M[here] * scale * packed[5, j:j + 1, :]
        block_store(i).start()
        return carry

    def wait_block(i, carry):
        block_store(i).wait()
        return carry

    lax.fori_loop(0, nr, scale_block, 0)
    lax.fori_loop(0, nr, wait_block, 0)
    for store in stores:
        store.wait()


def on_device(acts, out_grads, moment, row_state, col_state, row_conf, col_conf):
    R, C = lax.axis_size("row"), lax.axis_size("col")
    rows, cols = moment.shape
    nr, nc = rows // LANES, cols // LANES
    dma = pltpu.SemaphoreType.DMA
    big = jax.ShapeDtypeStruct((rows, cols), F32)
    by_row, by_col = (jax.ShapeDtypeStruct((n, LANES), F32) for n in (nr, nc))
    in_hbm = pl.BlockSpec(memory_space=pltpu.HBM)
    in_vmem = pl.BlockSpec(memory_space=pltpu.VMEM)
    tokens = R * out_grads.shape[0]
    moment_new, packed = pl.pallas_call(
        functools.partial(kernel, R, C),
        out_shape=(pltpu.VMEM((rows, cols), F32), pltpu.VMEM((6, 8, LANES), F32)),
        in_specs=[in_hbm] * 7,
        out_specs=(in_vmem,) * 2,
        scratch_shapes=[
            pltpu.VMEM((tokens, rows), acts.dtype),
            pltpu.VMEM((tokens, cols), out_grads.dtype),
            pltpu.VMEM((rows, cols), F32),
            pltpu.VMEM((4, 8, LANES), F32),
            pltpu.VMEM((rows, LANES), F32),
            pltpu.VMEM((rows, LANES), F32),
            pltpu.VMEM((2, 8, LANES), F32),
            pltpu.VMEM((2, C, 8, LANES), F32),
            pltpu.VMEM((2, 8, LANES), F32),
            pltpu.VMEM((2, X, 8, LANES), F32),
            pltpu.VMEM((2, 8, LANES), F32),
            pltpu.VMEM((2, R // X, 8, LANES), F32),
            pltpu.VMEM((2, 1, LANES), F32),
            pltpu.VMEM((2, 2, 1, LANES), F32),
            pltpu.VMEM((2, 1, LANES), F32),
            pltpu.VMEM((2, R * C // 2, 1, LANES), F32),
            dma((4,)), dma((4, 20)), dma((2,)), dma((12,)), dma((7,)),
            *[dma((2,))] * 10, pltpu.SemaphoreType.REGULAR((2,)),
        ],
        compiler_params=pltpu.CompilerParams(
            collective_id=0, has_side_effects=True, vmem_limit_bytes=40 * 2**20),
        cost_estimate=pl.CostEstimate(
            flops=2 * tokens * rows * cols, transcendentals=0, bytes_accessed=30 * 2**20),
        name="came_step",
    )(*(pltpu.with_memory_space_constraint(v, pltpu.HBM) for v in (
        acts, out_grads, moment, row_state.reshape(nr, LANES), col_state.reshape(nc, LANES),
        row_conf.reshape(nr, LANES), col_conf.reshape(nc, LANES))))
    outs = pl.pallas_call(
        finish,
        out_shape=(big, big, by_row, by_col, by_row, by_col),
        in_specs=[in_vmem] * 2,
        out_specs=(in_hbm,) * 6,
        scratch_shapes=[pltpu.VMEM((rows, cols), F32), dma((5,)), dma((nr,))],
        compiler_params=pltpu.CompilerParams(vmem_limit_bytes=16 * 2**20),
        cost_estimate=pl.CostEstimate(
            flops=2 * rows * cols, transcendentals=0, bytes_accessed=12 * rows * cols),
        name="finish",
    )(moment_new, packed)
    return outs[0], outs[1], *(out.reshape(-1) for out in outs[2:])


def solution(mesh):
    placed = (
        P("col", "row"),
        P("row", "col"),
        P("row", "col"),
        P("row"),
        P("col"),
        P("row"),
        P("col"),
    )
    return jax.shard_map(
        on_device,
        mesh=mesh,
        in_specs=placed,
        out_specs=(P("row", "col"), P("row", "col"), P("row"), P("col"), P("row"), P("col")),
        check_vma=False,
    )
```
